128 devices in a mesh: shard: 16 (over y, z_lo, core), ctx: 2 (over z_hi), tp: 4 (over x).
Axes of the slice: x: 4, y: 4, z: 4 (z_hi: 2, z_lo: 2; z = z_hi * 2 + z_lo), core: 2. Of those that a mesh axis runs over, the one named last changes fastest.
Arguments:
- tokens: bfloat16 [32, 28, 42, 1280], P('shard', 'ctx', None, 'tp'), may hold values from -6 to 6
- valid_mask: int32 [32, 28, 42], P('shard', 'ctx'), may hold values from 0 to 1, as said below
- ln1_gain: float32 [1280], replicated, may hold values from 0.25 to 1.75
- ln1_bias: float32 [1280], replicated, may hold values from -3 to 3
- qkv_weight: bfloat16 [3, 1280, 1280], P(None, 'shard', 'tp'), may hold values from -0.15625 to 0.15625
- qkv_bias: float32 [2, 1280], P(None, 'tp'), may hold values from -3 to 3
- rel_rows: bfloat16 [27, 80], replicated, may hold values from -0.69921875 to 0.69921875
- rel_cols: bfloat16 [27, 80], replicated, may hold values from -0.69921875 to 0.69921875
- proj_weight: bfloat16 [1280, 1280], P('tp', 'shard'), may hold values from -0.625 to 0.625
- proj_bias: float32 [1280], replicated, may hold values from -3 to 3
- ln2_gain: float32 [1280], replicated, may hold values from 0.25 to 1.75
- ln2_bias: float32 [1280], replicated, may hold values from -3 to 3
- fc1_weight: bfloat16 [1280, 5120], P('shard', 'tp'), may hold values from -0.15625 to 0.15625
- fc1_bias: float32 [5120], P('tp'), may hold values from -3 to 3
- fc2_weight: bfloat16 [5120, 1280], P('tp', 'shard'), may hold values from -0.078125 to 0.078125
- fc2_bias: float32 [1280], replicated, may hold values from -3 to 3
- cotangent: bfloat16 [32, 28, 42, 1280], P('shard', 'ctx', None, 'tp'), may hold values from -6 to 6
Outputs:
- result: bfloat16 [32, 28, 42, 1280], P('shard', 'ctx', None, 'tp')
- grad_tokens: float32 [32, 28, 42, 1280], P('shard', 'ctx', None, 'tp')
- grad_ln1_gain: float32 [1280], replicated
- grad_ln1_bias: float32 [1280], replicated
- grad_qkv_weight: float32 [3, 1280, 1280], P(None, 'shard', 'tp')
- grad_qkv_bias: float32 [2, 1280], P(None, 'tp')
- grad_rel_rows: float32 [27, 80], replicated
- grad_rel_cols: float32 [27, 80], replicated
- grad_proj_weight: float32 [1280, 1280], P('tp', 'shard')
- grad_proj_bias: float32 [1280], replicated
- grad_ln2_gain: float32 [1280], replicated
- grad_ln2_bias: float32 [1280], replicated
- grad_fc1_weight: float32 [1280, 5120], P('shard', 'tp')
- grad_fc1_bias: float32 [5120], P('tp')
- grad_fc2_weight: float32 [5120, 1280], P('tp', 'shard')
- grad_fc2_bias: float32 [1280], replicated
The draws below stay inside these ranges and needn't reach their ends.
Inputs may be any that keep to these rules, and one draw needn't show every extreme that they name: `valid_mask`: the ones of each image form a top-left rectangle of more than 14 rows and more than 28 columns.
All inputs are finite; a program needn't handle non-finite values.
Results may differ from the reference program's by a relative error of at most 0.025.
Values may be sent and summed in bfloat16 or wider, within the bound.
No kernel may reach another device: no remote copies, remote signals or barrier semaphores. Data moves between devices by JAX's collectives and lax.ppermute only.
A program may use at most 320 MiB of HBM per device.

```python
import jax
import jax.numpy as jnp
from jax import lax

D = 1280
HEADS = 16
HDIM = 80
FF = 5120
WIN = 14
IMAGES = 32
HP = 28
WP = 42
RELS = 27


def draw_valid_mask(key, part):
    key = jax.random.fold_in(key, 11)
    row_key, col_key = jax.random.split(key)
    rows_valid = jax.random.randint(row_key, (IMAGES,), HP - WIN + 1, HP + 1)
    cols_valid = jax.random.randint(col_key, (IMAGES,), WP - WIN + 1, WP + 1)
    row_ids = jnp.arange(HP)[None, :, None]
    col_ids = jnp.arange(WP)[None, None, :]
    inside = (row_ids < rows_valid[:, None, None]) & (col_ids < cols_valid[:, None, None])
    return inside.astype(jnp.int32)


def block_levels(key, dims, cuts, smallest, top_value):
    gain, own = 1.0, jax.random.fold_in(key, 6)
    for axis_at, parts in cuts:
        draws = jnp.exp(jax.random.uniform(jax.random.fold_in(own, axis_at), (parts,), jnp.float32, smallest / len(cuts), top_value / len(cuts)))
        gain = gain * jnp.repeat(draws, dims[axis_at] // parts).reshape([-1 if axis == axis_at else 1 for axis in range(len(dims))])
    return gain


def gaussian(key, shape, spread, bound, pieces=(), kind=jnp.bfloat16):
    drawn = jax.random.normal(key, shape, jnp.float32) * spread
    if len(pieces) > 0:
        drawn = block_levels(key, shape, pieces, -0.22, 0.18) * drawn
    return jnp.clip(drawn, min=-bound, max=bound).astype(kind)


def setup_inputs(seed: int = 0) -> dict:
    arg_keys = jax.random.split(jax.random.key(seed), 18)
    tokens = gaussian(arg_keys[0], (IMAGES, HP, WP, D), 1.0, 6.0, ((0, 16), (1, 2), (3, 4)))
    valid_mask = draw_valid_mask(jax.random.fold_in(arg_keys[17], 71), 0)
    ln1_gain = jnp.clip(1.0 + 0.15 * jax.random.normal(arg_keys[2], (D,), jnp.float32), 0.25, 1.75)
    ln1_bias = gaussian(arg_keys[3], (D,), 0.3, 3.0, (), jnp.float32)
    qkv_weight = gaussian(arg_keys[4], (3, D, D), D ** -0.5, 0.15625, ((1, 16), (2, 4)))
    qkv_bias = gaussian(arg_keys[5], (2, D), 0.3, 3.0, ((1, 4),), jnp.float32)
    rel_rows = gaussian(arg_keys[6], (RELS, HDIM), 0.12, 0.69921875)
    rel_cols = gaussian(arg_keys[7], (RELS, HDIM), 0.12, 0.69921875)
    proj_weight = gaussian(arg_keys[8], (D, D), (D // 16) ** -0.5, 0.625, ((0, 4), (1, 16)))
    proj_bias = gaussian(arg_keys[9], (D,), 0.3, 3.0, (), jnp.float32)
    ln2_gain = jnp.clip(1.0 + 0.15 * jax.random.normal(arg_keys[10], (D,), jnp.float32), 0.25, 1.75)
    ln2_bias = gaussian(arg_keys[11], (D,), 0.3, 3.0, (), jnp.float32)
    fc1_weight = gaussian(arg_keys[12], (D, FF), D ** -0.5, 0.15625, ((0, 16), (1, 4)))
    fc1_bias = gaussian(arg_keys[13], (FF,), 0.3, 3.0, ((0, 4),), jnp.float32)
    fc2_weight = gaussian(arg_keys[14], (FF, D), FF ** -0.5, 0.078125, ((0, 4), (1, 16)))
    fc2_bias = gaussian(arg_keys[15], (D,), 0.3, 3.0, (), jnp.float32)
    cotangent = gaussian(arg_keys[16], (IMAGES, HP, WP, D), 1.0, 6.0, ((0, 16), (1, 2), (3, 4)))
    return {"tokens": tokens, "valid_mask": valid_mask, "ln1_gain": ln1_gain, "ln1_bias": ln1_bias, "qkv_weight": qkv_weight, "qkv_bias": qkv_bias, "rel_rows": rel_rows, "rel_cols": rel_cols, "proj_weight": proj_weight, "proj_bias": proj_bias, "ln2_gain": ln2_gain, "ln2_bias": ln2_bias, "fc1_weight": fc1_weight, "fc1_bias": fc1_bias, "fc2_weight": fc2_weight, "fc2_bias": fc2_bias, "cotangent": cotangent}


@jax.custom_vjp
def low(v):
    return lax.optimization_barrier(v.astype(jnp.bfloat16)).astype(jnp.float32)

@jax.custom_vjp
def low_back(v):
    return v

def low_keep(v):
    return (low(v), None)

def low_pass(kept, grad):
    return (grad,)

def back_keep(v):
    return (v, None)

def back_low(kept, grad):
    return (low(grad),)
low.defvjp(low_keep, low_pass)
low_back.defvjp(back_keep, back_low)
epsilon = 1e-06
highest = lax.Precision.HIGHEST

def layer_norm(values, gain_term, bias_term):
    average = lax.optimization_barrier(jnp.mean(values, axis=-1, keepdims=True))
    centered = values - average
    inverse = lax.rsqrt(lax.optimization_barrier(jnp.mean(centered * centered, axis=-1, keepdims=True)) + epsilon)
    return centered * inverse * gain_term + bias_term

def offset_table(width_cells):
    first_pos = jnp.arange(width_cells)[:, None, None]
    second_pos = jnp.arange(width_cells)[None, :, None]
    entry_pos = jnp.arange(2 * width_cells - 1)[None, None, :]
    return (first_pos - second_pos + width_cells - 1 == entry_pos).astype(jnp.float32)

def image_block(token_grid, keep_mask, params):
    ln1_gain, ln1_bias, qkv_weight, qkv_bias, rel_rows, rel_cols, proj_weight, proj_bias, ln2_gain, ln2_bias, fc1_weight, fc1_bias, fc2_weight, fc2_bias = params
    rows_w = token_grid.shape[0] // WIN
    cols_w = token_grid.shape[1] // WIN
    offsets = offset_table(WIN)
    row_table = jnp.einsum('axd,dc->axc', offsets, rel_rows, precision=highest)
    col_table = jnp.einsum('axd,dc->axc', offsets, rel_cols, precision=highest)
    keep_cells = keep_mask[..., None]
    entering = low(layer_norm(token_grid, ln1_gain, ln1_bias) * keep_cells)
    queries = low(low_back(jnp.einsum('ijd,de->ije', entering, qkv_weight[0], precision=highest) + qkv_bias[0]))
    keys_in = low(low_back(jnp.einsum('ijd,de->ije', entering, qkv_weight[1], precision=highest)))
    values_in = low(low_back(jnp.einsum('ijd,de->ije', entering, qkv_weight[2], precision=highest) + qkv_bias[1]))
    window_form = (rows_w, WIN, cols_w, WIN, HEADS, HDIM)
    query_win = queries.reshape(window_form)
    key_win = keys_in.reshape(window_form)
    value_win = values_in.reshape(window_form)
    direct = jnp.einsum('pawbhc,pxwyhc->pwhabxy', query_win, key_win, precision=highest) * HDIM ** (-0.5)
    along_rows = jnp.einsum('pawbhc,axc->pwhabx', query_win, row_table, precision=highest)
    along_cols = jnp.einsum('pawbhc,byc->pwhaby', query_win, col_table, precision=highest)
    scores = low_back(direct + along_rows[..., None] + along_cols[..., None, :])
    flattened = scores.reshape(rows_w, cols_w, HEADS, WIN * WIN, WIN * WIN)
    attention = low(jax.nn.softmax(flattened, axis=-1)).reshape(scores.shape)
    mixed = jnp.einsum('pwhabxy,pxwyhc->pawbhc', attention, value_win, precision=highest)
    attended = low(low_back(mixed)).reshape(token_grid.shape[0], token_grid.shape[1], HEADS * HDIM)
    projected = low_back(jnp.einsum('ije,ed->ijd', attended, proj_weight, precision=highest))
    hidden = token_grid + keep_cells * (projected + proj_bias)
    entering2 = low(layer_norm(hidden, ln2_gain, ln2_bias))
    preact = low_back(jnp.einsum('ijd,df->ijf', entering2, fc1_weight, precision=highest) + fc1_bias)
    activated = low(jax.nn.gelu(preact, approximate=False))
    branch = jnp.einsum('ijf,fd->ijd', activated, fc2_weight, precision=highest) + fc2_bias
    return hidden + keep_cells * branch

def reference(tokens, valid_mask, ln1_gain, ln1_bias, qkv_weight, qkv_bias, rel_rows, rel_cols, proj_weight, proj_bias, ln2_gain, ln2_bias, fc1_weight, fc1_bias, fc2_weight, fc2_bias, cotangent):
    weights_all = tuple((element.astype(jnp.float32) for element in (ln1_gain, ln1_bias, qkv_weight, qkv_bias, rel_rows, rel_cols, proj_weight, proj_bias, ln2_gain, ln2_bias, fc1_weight, fc1_bias, fc2_weight, fc2_bias)))
    keep_all = valid_mask.astype(jnp.float32)

    def forward(token_all, weight_set):

        def per_image(pair_in):
            return image_block(pair_in[0], pair_in[1], weight_set)
        return lax.map(jax.checkpoint(per_image), (token_all, keep_all))
    result, pullback = jax.vjp(forward, tokens.astype(jnp.float32), weights_all)
    grad_tokens, grad_weights = pullback(cotangent.astype(jnp.float32))
    return (result.astype(jnp.bfloat16), grad_tokens, grad_weights[0], grad_weights[1], grad_weights[2], grad_weights[3], grad_weights[4], grad_weights[5], grad_weights[6], grad_weights[7], grad_weights[8], grad_weights[9], grad_weights[10], grad_weights[11], grad_weights[12], grad_weights[13])
```

```python
import jax
import jax.numpy as jnp
import numpy as np
from jax import lax
from jax.experimental import pallas as pl
from jax.experimental.pallas import tpu as pltpu
from jax.sharding import PartitionSpec as P

HEADS = 16
HDIM = 80
WIN = 14
D = 1280
NT = 4
HL = HEADS // NT
CELLS = WIN * WIN
WR = 208
NW = 6
TS = 320
HALF = TS // 2
HP = 128
RELS = 2 * WIN - 1
EPS = 1e-06
SCALE = HDIM ** (-0.5)
bf = jnp.bfloat16
f32 = jnp.float32
VM = 60 * 1024 * 1024


def rel_constants():
    sel = np.zeros((512, 64), np.float32)
    mask = np.zeros((WR, 512), np.float32)
    spread = np.zeros((512, WR), np.float32)
    for a in range(WIN):
        for x in range(WIN):
            sel[a * WIN + x, a - x + WIN - 1] = 1
            sel[256 + a * WIN + x, 32 + a - x + WIN - 1] = 1
    for a in range(WIN):
        for b in range(WIN):
            row = a * WIN + b
            mask[row, a * WIN : a * WIN + WIN] = 1
            mask[row, 256 + b * WIN : 256 + b * WIN + WIN] = 1
    for a in range(WIN):
        for x in range(WIN):
            for y in range(WIN):
                spread[a * WIN + x, x * WIN + y] = 1
                spread[256 + a * WIN + y, x * WIN + y] = 1
    keys = np.where(np.arange(WR) < CELLS, 0.0, -1e30).astype(np.float32)[None]
    return sel, mask, spread, keys


def dot(a, b):
    return lax.dot_general(a, b, (((1,), (0,)), ((), ())), preferred_element_type=f32)


def dot_nt(a, b):
    return lax.dot_general(a, b, (((1,), (1,)), ((), ())), preferred_element_type=f32)


def dot_tn(a, b):
    return lax.dot_general(a, b, (((0,), (0,)), ((), ())), preferred_element_type=f32)


def params():
    return pltpu.CompilerParams(vmem_limit_bytes=VM)


def cost(flops, nbytes, trans=0):
    return pl.CostEstimate(flops=int(flops), bytes_accessed=int(nbytes), transcendentals=int(trans))


def sds(shape, dtype):
    return jax.ShapeDtypeStruct(shape, dtype)


def full(shape):
    return pl.BlockSpec(shape, lambda *g: (0,) * len(shape))


ANY = pl.BlockSpec(memory_space=pl.ANY)


def stats(x):
    mean = jnp.sum(x, axis=1, keepdims=True) * (1.0 / D)
    xc = x - mean
    var = jnp.sum(xc * xc, axis=1, keepdims=True) * (1.0 / D)
    inv = lax.rsqrt(var + EPS)
    return xc * inv, inv


def colsum(x):
    return jnp.sum(x, axis=0, keepdims=True)


def acc_out(ref, value):
    @pl.when(pl.program_id(0) == 0)
    def _():
        ref[...] = jnp.zeros_like(ref)

    ref[...] += value


RB = 80


def ln1_body(tok_ref, cot_ref, keep_ref, g_ref, b_ref, x_ref, c_ref, e_ref, gb_ref, fb_ref):
    keep = keep_ref[...]
    x = jnp.concatenate([tok_ref[k].astype(f32) for k in range(NT)], axis=1)
    c = jnp.concatenate([cot_ref[k].astype(f32) for k in range(NT)], axis=1)
    n, _ = stats(x)
    e_ref[...] = (keep * (n * g_ref[...] + b_ref[...])).astype(bf)
    x_ref[...] = x.astype(bf)
    c_ref[...] = c.astype(bf)
    gb = keep * c
    gb_ref[...] = gb.astype(bf)
    acc_out(fb_ref, colsum(gb))


def ln1_call(tok4, cot4, keep, g, b):
    blk = pl.BlockSpec((NT, RB, TS), lambda i: (0, i, 0))
    row = pl.BlockSpec((RB, D), lambda i: (i, 0))
    kp = pl.BlockSpec((RB, 1), lambda i: (i, 0))
    return pl.pallas_call(
        ln1_body,
        grid=(TS // RB,),
        in_specs=[blk, blk, kp, full((1, D)), full((1, D))],
        out_specs=[row, row, row, row, full((1, D))],
        out_shape=[sds((TS, D), bf)] * 4 + [sds((1, D), f32)],
        compiler_params=params(),
        cost_estimate=cost(30 * TS * D, 14 * TS * D),
        name="ln1",
    )(tok4, cot4, keep, g, b)


def ln2_body(r0, c1, c3, x, keep, pb, g, b, h_ref, e_ref):
    s = r0[...] + c1[...].astype(f32) + c3[...].astype(f32)
    h = x[...].astype(f32) + keep[...] * (s + pb[...])
    h_ref[...] = h
    n, _ = stats(h)
    e_ref[...] = (n * g[...] + b[...]).astype(bf)


def ln2_call(r0, c1, c3, x, keep, pb, g, b):
    row = pl.BlockSpec((RB, D), lambda i: (i, 0))
    kp = pl.BlockSpec((RB, 1), lambda i: (i, 0))
    return pl.pallas_call(
        ln2_body,
        grid=(TS // RB,),
        in_specs=[row, row, row, row, kp] + [full((1, D))] * 3,
        out_specs=[row, row],
        out_shape=[sds((TS, D), f32), sds((TS, D), bf)],
        compiler_params=params(),
        cost_estimate=cost(20 * TS * D, 16 * TS * D),
        name="ln2",
    )(r0, c1, c3, x, keep, pb, g, b)


def result_body(r0, c1, c3, h, keep, fb, o_ref):
    s = r0[...] + c1[...].astype(f32) + c3[...].astype(f32)
    o = (h[...] + keep[...] * (s + fb[...])).astype(bf)
    for k in range(NT):
        o_ref[k] = o[:, k * TS : (k + 1) * TS]


def result_call(r0, c1, c3, h, keep, fb):
    row = pl.BlockSpec((RB, D), lambda i: (i, 0))
    kp = pl.BlockSpec((RB, 1), lambda i: (i, 0))
    return pl.pallas_call(
        result_body,
        grid=(TS // RB,),
        in_specs=[row, row, row, row, kp, full((1, D))],
        out_specs=pl.BlockSpec((NT, RB, TS), lambda i: (0, i, 0)),
        out_shape=sds((NT, TS, TS), bf),
        compiler_params=params(),
        cost_estimate=cost(8 * TS * D, 14 * TS * D),
        name="result",
    )(r0, c1, c3, h, keep, fb)


def norm_back(w, n, inv):
    m1 = jnp.sum(w, axis=1, keepdims=True) * (1.0 / D)
    m2 = jnp.sum(w * n, axis=1, keepdims=True) * (1.0 / D)
    return inv * (w - m1 - n * m2)


def ln2b_body(r0, c1, c3, h, c, keep, g, gh_ref, gp_ref, gg_ref, gb_ref, pb_ref):
    gn = r0[...] + c1[...].astype(f32) + c3[...].astype(f32)
    n, inv = stats(h[...])
    gh = c[...].astype(f32) + norm_back(gn * g[...], n, inv)
    gh_ref[...] = gh
    kg = keep[...] * gh
    gp_ref[...] = kg.astype(bf)
    acc_out(gg_ref, colsum(gn * n))
    acc_out(gb_ref, colsum(gn))
    acc_out(pb_ref, colsum(kg))


def ln2b_call(r0, c1, c3, h, c, keep, g):
    row = pl.BlockSpec((RB, D), lambda i: (i, 0))
    kp = pl.BlockSpec((RB, 1), lambda i: (i, 0))
    return pl.pallas_call(
        ln2b_body,
        grid=(TS // RB,),
        in_specs=[row, row, row, row, row, kp, full((1, D))],
        out_specs=[row, row] + [full((1, D))] * 3,
        out_shape=[sds((TS, D), f32), sds((TS, D), bf)] + [sds((1, D), f32)] * 3,
        compiler_params=params(),
        cost_estimate=cost(30 * TS * D, 20 * TS * D),
        name="ln2b",
    )(r0, c1, c3, h, c, keep, g)


def ln1b_body(r0, c1, c3, x, gh, keep, g, o_ref, gg_ref, gb_ref):
    gn = keep[...] * (r0[...] + c1[...].astype(f32) + c3[...].astype(f32))
    n, inv = stats(x[...].astype(f32))
    gt = (gh[...] + norm_back(gn * g[...], n, inv)).astype(bf)
    for k in range(NT):
        o_ref[k] = gt[:, k * TS : (k + 1) * TS]
    acc_out(gg_ref, colsum(gn * n))
    acc_out(gb_ref, colsum(gn))


def ln1b_call(r0, c1, c3, x, gh, keep, g):
    row = pl.BlockSpec((RB, D), lambda i: (i, 0))
    kp = pl.BlockSpec((RB, 1), lambda i: (i, 0))
    return pl.pallas_call(
        ln1b_body,
        grid=(TS // RB,),
        in_specs=[row, row, row, row, row, kp, full((1, D))],
        out_specs=[pl.BlockSpec((NT, RB, TS), lambda i: (0, i, 0))] + [full((1, D))] * 2,
        out_shape=[sds((NT, TS, TS), bf)] + [sds((1, D), f32)] * 2,
        compiler_params=params(),
        cost_estimate=cost(30 * TS * D, 18 * TS * D),
        name="ln1b",
    )(r0, c1, c3, x, gh, keep, g)


def pad_body(w_ref, q_ref, p_ref):
    rows = w_ref.shape[0]
    w = w_ref[...]
    zero = jnp.zeros((rows, HP - HDIM), bf)
    for h in range(3 * HL):
        q_ref[:, h * HP : (h + 1) * HP] = jnp.concatenate([w[:, h * HDIM : (h + 1) * HDIM], zero], axis=1)
    for h in range(HL):
        s = 3 * HL + h
        p_ref[:, h * HP : (h + 1) * HP] = jnp.concatenate([w[:, s * HDIM : (s + 1) * HDIM], zero], axis=1)


def pad_call(g1):
    rb = 160
    return pl.pallas_call(
        pad_body,
        grid=(D // rb,),
        in_specs=[pl.BlockSpec((rb, D), lambda i: (i, 0))],
        out_specs=[
            pl.BlockSpec((rb, 3 * HL * HP), lambda i: (i, 0)),
            pl.BlockSpec((rb, HL * HP), lambda i: (i, 0)),
        ],
        out_shape=[sds((D, 3 * HL * HP), bf), sds((D, HL * HP), bf)],
        compiler_params=params(),
        cost_estimate=cost(D * 2048, 2 * D * (1280 + 2048)),
        name="padw",
    )(g1)


def block_of(me, j):
    return lax.rem(me + j, NT)


def qkv_body(me_ref, x_ref, w_ref, b_ref, keep_ref, o_ref):
    o_ref[0] = (dot(x_ref[...], w_ref[...]) + b_ref[...]).astype(bf)


def qkv_call(me, j, x, w, bias, into):
    n = w.shape[1]
    tn = 256
    return pl.pallas_call(
        qkv_body,
        grid_spec=pltpu.PrefetchScalarGridSpec(
            num_scalar_prefetch=1,
            grid=(n // tn,),
            in_specs=[
                pl.BlockSpec((TS, D), lambda i, m: (0, 0)),
                pl.BlockSpec((D, tn), lambda i, m: (0, i)),
                pl.BlockSpec((1, tn), lambda i, m: (0, i)),
                ANY,
            ],
            out_specs=pl.BlockSpec((1, TS, tn), lambda i, m: (block_of(m[0], j), 0, i)),
        ),
        out_shape=sds((NT, TS, n), bf),
        input_output_aliases={4: 0},
        compiler_params=params(),
        cost_estimate=cost(2 * TS * D * n, 2 * (TS * D + D * n + TS * n)),
        name="qkv",
    )(me, x, w, bias, into)


def attn_body(qkv_ref, tab_ref, sel_ref, mask_ref, sp_ref, km_ref, z_ref, o_ref, p_ref, t_ref):
    @pl.when(pl.program_id(0) == 0)
    def _():
        t_ref[...] = dot(sel_ref[...], tab_ref[...]).astype(bf)

    table = t_ref[...]
    for h in range(HL):
        q = qkv_ref[:, h * HP : (h + 1) * HP]
        k = qkv_ref[:, (HL + h) * HP : (HL + h + 1) * HP]
        v = qkv_ref[:, (2 * HL + h) * HP : (2 * HL + h + 1) * HP]
        along = (dot_nt(q, table) * mask_ref[...].astype(f32)).astype(bf)
        s = dot_nt(q, k) * SCALE + dot(along, sp_ref[...]) + km_ref[...]
        top = jnp.max(s, axis=1, keepdims=True)
        e = jnp.exp(s - top)
        p = (e * (1.0 / jnp.sum(e, axis=1, keepdims=True))).astype(bf)
        p_ref[0, h] = p
        o_ref[:, h * HP : (h + 1) * HP] = dot(p, v).astype(bf)


def attn_call(qkv, tab, sel, mask, spread, keys, into):
    n = 3 * HL * HP
    return pl.pallas_call(
        attn_body,
        grid=(NW,),
        in_specs=[
            pl.BlockSpec((WR, n), lambda i: (i, 0)),
            full((64, HP)),
            full((512, 64)),
            full((WR, 512)),
            full((512, WR)),
            full((1, WR)),
            ANY,
        ],
        out_specs=[
            pl.BlockSpec((WR, HL * HP), lambda i: (i, 0)),
            pl.BlockSpec((1, HL, WR, WR), lambda i: (i, 0, 0, 0)),
        ],
        out_shape=[sds((NT * TS, HL * HP), bf), sds((NW, HL, WR, WR), bf)],
        scratch_shapes=[pltpu.VMEM((512, HP), bf)],
        input_output_aliases={6: 0},
        compiler_params=params(),
        cost_estimate=cost(24 * 6 * 2 * WR * WR * 256, 8e6, 24 * WR * 256),
        name="attn",
    )(qkv, tab, sel, mask, spread, keys, into)


def attnb_body(qkv_ref, p_ref, ga_ref, tab_ref, sel_ref, mask_ref, sp_ref, z_ref, o_ref, rel_ref, bias_ref, t_ref):
    @pl.when(pl.program_id(0) == 0)
    def _():
        t_ref[...] = dot(sel_ref[...], tab_ref[...]).astype(bf)
        rel_ref[...] = jnp.zeros_like(rel_ref)
        bias_ref[...] = jnp.zeros_like(bias_ref)

    table = t_ref[...]
    rel = jnp.zeros((512, HP), f32)
    for h in range(HL):
        cq = slice(h * HP, (h + 1) * HP)
        ck = slice((HL + h) * HP, (HL + h + 1) * HP)
        cv = slice((2 * HL + h) * HP, (2 * HL + h + 1) * HP)
        q = qkv_ref[:, cq]
        k = qkv_ref[:, ck]
        v = qkv_ref[:, cv]
        ga = ga_ref[:, cq]
        p = p_ref[0, h]
        pf = p.astype(f32)
        gs = dot_nt(ga, v)
        delta = jnp.sum(pf * gs, axis=1, keepdims=True)
        ds = (pf * (gs - delta)).astype(bf)
        gv = dot_tn(p, ga).astype(bf)
        gk = (dot_tn(ds, q) * SCALE).astype(bf)
        sums = (dot_nt(ds, sp_ref[...]) * mask_ref[...].astype(f32)).astype(bf)
        gq = (dot(ds, k) * SCALE + dot(sums, table)).astype(bf)
        rel = rel + dot_tn(sums, q)
        o_ref[:, cq] = gq
        o_ref[:, ck] = gk
        o_ref[:, cv] = gv
        bias_ref[:, cq] += colsum(gq.astype(f32))
        bias_ref[:, cv] += colsum(gv.astype(f32))
    rel_ref[...] += rel


def attnb_call(qkv, p, ga, tab, sel, mask, spread, into):
    n = 3 * HL * HP
    return pl.pallas_call(
        attnb_body,
        grid=(NW,),
        in_specs=[
            pl.BlockSpec((WR, n), lambda i: (i, 0)),
            pl.BlockSpec((1, HL, WR, WR), lambda i: (i, 0, 0, 0)),
            pl.BlockSpec((WR, HL * HP), lambda i: (i, 0)),
            full((64, HP)),
            full((512, 64)),
            full((WR, 512)),
            full((512, WR)),
            ANY,
        ],
        out_specs=[pl.BlockSpec((WR, n), lambda i: (i, 0)), full((512, HP)), full((1, n))],
        out_shape=[sds((NT * TS, n), bf), sds((512, HP), f32), sds((1, n), f32)],
        scratch_shapes=[pltpu.VMEM((512, HP), bf)],
        input_output_aliases={7: 0},
        compiler_params=params(),
        cost_estimate=cost(24 * 10 * 2 * WR * WR * 256, 14e6),
        name="attnb",
    )(qkv, p, ga, tab, sel, mask, spread, into)


def partial_body(me_ref, a_ref, w_ref, r0, r1, r2, r3):
    w = w_ref[...]
    for j, ref in ((2, r2), (1, r1), (3, r3), (0, r0)):
        ref[...] = dot_nt(a_ref[block_of(me_ref[0], j)], w).astype(ref.dtype)


def partial_call(me, a, w, name):
    k = a.shape[2]
    tn = 256
    return pl.pallas_call(
        partial_body,
        grid_spec=pltpu.PrefetchScalarGridSpec(
            num_scalar_prefetch=1,
            grid=(D // tn,),
            in_specs=[
                pl.BlockSpec((NT, TS, k), lambda i, m: (0, 0, 0)),
                pl.BlockSpec((tn, k), lambda i, m: (i, 0)),
            ],
            out_specs=[pl.BlockSpec((TS, tn), lambda i, m: (0, i))] * 4,
        ),
        out_shape=[sds((TS, D), f32)] + [sds((TS, D), bf)] * 3,
        compiler_params=params(),
        cost_estimate=cost(2 * NT * TS * D * k, 2 * (NT * TS * k + D * k + 5 * TS * D)),
        name=name,
    )(me, a, w)


def mlp_body(z_ref, gb_ref, w1_ref, w2_ref, b1_ref, act_ref, gp_ref, br_ref, gn_ref, fb_ref, br_s, gn_s):
    step = pl.program_id(0)
    w1 = w1_ref[...]
    w2 = w2_ref[...]
    pre = dot(z_ref[...], w1) + b1_ref[...]
    ga = dot(gb_ref[...], w2)
    cdf = 0.5 + 0.5 * lax.erf(pre * 0.7071067811865476)
    act = (pre * cdf).astype(bf)
    slope = cdf + pre * (0.3989422804014327 * jnp.exp(-0.5 * pre * pre))
    gp = (ga * slope).astype(bf)
    act_ref[...] = act
    gp_ref[...] = gp
    fb_ref[...] = colsum(gp.astype(f32))
    br = dot_nt(act, w2)
    gn = dot_nt(gp, w1)

    @pl.when(step == 0)
    def _():
        br_s[...] = br
        gn_s[...] = gn

    @pl.when(step > 0)
    def _():
        br_s[...] += br
        gn_s[...] += gn

    @pl.when(step == pl.num_programs(0) - 1)
    def _():
        br_ref[...] = br_s[...].astype(br_ref.dtype)
        gn_ref[...] = gn_s[...].astype(gn_ref.dtype)


def mlp_call(z, gb, w, b1, kind):
    tf = 256
    nf = D // tf
    col = pl.BlockSpec((TS, tf), lambda i: (0, i))
    return pl.pallas_call(
        mlp_body,
        grid=(nf,),
        in_specs=[
            full((TS, D)),
            full((TS, D)),
            pl.BlockSpec((D, tf), lambda i: (0, i)),
            pl.BlockSpec((D, tf), lambda i: (0, i + nf)),
            pl.BlockSpec((1, tf), lambda i: (0, i)),
        ],
        out_specs=[col, col, full((TS, D)), full((TS, D)), pl.BlockSpec((1, tf), lambda i: (0, i))],
        out_shape=[sds((TS, D), bf), sds((TS, D), bf), sds((TS, D), kind), sds((TS, D), kind), sds((1, D), f32)],
        scratch_shapes=[pltpu.VMEM((TS, D), f32), pltpu.VMEM((TS, D), f32)],
        compiler_params=params(),
        cost_estimate=cost(8 * TS * D * D, 4 * D * D + 12 * TS * D, 2 * TS * D),
        name="mlp",
    )(z, gb, w, w, b1)


def fcgrad_body(*refs):
    o_ref = refs[-1]
    z, gp, gb, act = refs[0:4], refs[4:8], refs[8:12], refs[12:16]
    total = dot_tn(z[0][...], gp[0][...])
    for j in range(1, NT):
        total += dot_tn(z[j][...], gp[j][...])
    o_ref[:, :D] = total.astype(bf)
    total = dot_tn(gb[0][...], act[0][...])
    for j in range(1, NT):
        total += dot_tn(gb[j][...], act[j][...])
    o_ref[:, D:] = total.astype(bf)


def fcgrad_call(z, gp, gb, act):
    td = 256
    col = pl.BlockSpec((TS, td), lambda i: (0, i))
    const = full((TS, D))
    return pl.pallas_call(
        fcgrad_body,
        grid=(D // td,),
        in_specs=[col] * 4 + [const] * 4 + [col] * 4 + [const] * 4,
        out_specs=pl.BlockSpec((td, 2 * D), lambda i: (i, 0)),
        out_shape=sds((D, 2 * D), bf),
        compiler_params=params(),
        cost_estimate=cost(16 * TS * D * D, 2 * (16 * TS * D + 2 * D * D)),
        name="fcgrad",
    )(*z, *gp, *gb, *act)


def narrow(x, heads):
    return jnp.concatenate([x[:, h * HP : h * HP + HDIM] for h in range(heads)], axis=1)


def qpgrad_body(me_ref, e0, e1, e2, e3, p0, p1, p2, p3, dq_ref, at_ref, o_ref):
    me = me_ref[0]
    total = None
    for j, e in enumerate((e0, e1, e2, e3)):
        part = dot_tn(e[...], dq_ref[block_of(me, j)])
        total = part if total is None else total + part
    o_ref[:, : 3 * HL * HDIM] = narrow(total, 3 * HL).astype(bf)
    total = None
    for j, p in enumerate((p0, p1, p2, p3)):
        part = dot_tn(p[...], at_ref[block_of(me, j)])
        total = part if total is None else total + part
    o_ref[:, 3 * HL * HDIM :] = narrow(total, HL).astype(bf)


def qpgrad_call(me, e, p, dqkv, att):
    td = 256
    col = pl.BlockSpec((TS, td), lambda i, m: (0, i))
    n = 3 * HL * HP
    return pl.pallas_call(
        qpgrad_body,
        grid_spec=pltpu.PrefetchScalarGridSpec(
            num_scalar_prefetch=1,
            grid=(D // td,),
            in_specs=[col] * 8
            + [
                pl.BlockSpec((NT, TS, n), lambda i, m: (0, 0, 0)),
                pl.BlockSpec((NT, TS, HL * HP), lambda i, m: (0, 0, 0)),
            ],
            out_specs=pl.BlockSpec((td, D), lambda i, m: (i, 0)),
        ),
        out_shape=sds((D, D), bf),
        compiler_params=params(),
        cost_estimate=cost(8 * TS * D * 2048, 2 * (8 * TS * D + 4 * TS * 2048 + D * D)),
        name="qpgrad",
    )(me, *e, *p, dqkv, att)


UP = [(i, (i + 1) % NT) for i in range(NT)]
DOWN = [(i, (i - 1) % NT) for i in range(NT)]


def up(v):
    return lax.ppermute(v, "tp", UP)


def down(v):
    return lax.ppermute(v, "tp", DOWN)


def ring_gather(own):
    b3 = up(own)
    b1 = down(own)
    b2 = jnp.concatenate([up(b3[:HALF]), down(b1[HALF:])], axis=0)
    return own, b1, b2, b3


def ring_scatter(r1, r2, r3):
    a = up(r2[:HALF])
    b = down(r2[HALF:])
    s1 = jnp.concatenate([(r1[:HALF].astype(f32) + a.astype(f32)).astype(bf), r1[HALF:]], axis=0)
    s3 = jnp.concatenate([r3[:HALF], (r3[HALF:].astype(f32) + b.astype(f32)).astype(bf)], axis=0)
    return down(s3), up(s1)


def from_everyone(array, axis):
    size = lax.axis_size(axis)
    return lax.all_to_all(jnp.broadcast_to(array[None], (size, *array.shape)), axis, 0, 0, tiled=True)


def windows(grid):
    n = grid.shape[-1]
    w = grid.reshape(2, WIN, 3, WIN, n).transpose(0, 2, 1, 3, 4).reshape(NW, CELLS, n)
    w = jnp.pad(w, ((0, 0), (0, WR - CELLS), (0, 0))).reshape(NW * WR, n)
    return jnp.pad(w, ((0, NT * TS - NW * WR), (0, 0))).reshape(NT, TS, n)


def unwindows(blocks):
    n = blocks.shape[-1]
    w = blocks.reshape(NT * TS, n)[: NW * WR].reshape(NW, WR, n)[:, :CELLS]
    return w.reshape(2, 3, WIN, WIN, n).transpose(0, 2, 1, 3, 4).reshape(2, WIN, 3 * WIN, n)


def local(
    tokens,
    valid_mask,
    ln1_gain,
    ln1_bias,
    qkv_weight,
    qkv_bias,
    rel_rows,
    rel_cols,
    proj_weight,
    proj_bias,
    ln2_gain,
    ln2_bias,
    fc1_weight,
    fc1_bias,
    fc2_weight,
    fc2_bias,
    cotangent,
):
    tp_index = lax.axis_index("tp")
    me = tp_index.astype(jnp.int32).reshape(1)
    sel, mask, spread, keys = rel_constants()
    sel = jnp.asarray(sel, bf)
    mask = jnp.asarray(mask, bf)
    spread = jnp.asarray(spread, bf)
    keys = jnp.asarray(keys, f32)
    row = lambda v: v.reshape(1, -1)

    own1 = jnp.concatenate([jnp.moveaxis(qkv_weight, 1, 0).reshape(80, 960), proj_weight.T], axis=1)
    own2 = jnp.concatenate([fc1_weight, fc2_weight.T], axis=1)
    all1 = lax.all_gather(own1, "shard", axis=0, tiled=True)
    all2 = lax.all_gather(own2, "shard", axis=0, tiled=True)
    qkvp, projp = pad_call(all1)
    bias_q = jnp.pad(qkv_bias.reshape(2, HL, HDIM), ((0, 0), (0, 0), (0, HP - HDIM))).reshape(2, HL * HP)
    bias_p = row(jnp.concatenate([bias_q[0], jnp.zeros((HL * HP,), f32), bias_q[1]]))
    tab = jnp.zeros((64, HP), bf).at[:RELS, :HDIM].set(rel_rows).at[32 : 32 + RELS, :HDIM].set(rel_cols)

    keep = windows(valid_mask.astype(f32)[..., None])
    keep = lax.dynamic_index_in_dim(keep, tp_index, 0, keepdims=False)
    tok4 = lax.all_to_all(windows(tokens), "tp", 0, 0, tiled=True)
    cot4 = lax.all_to_all(windows(cotangent), "tp", 0, 0, tiled=True)
    x, c, e, gb, sum_fc2_bias = ln1_call(tok4, cot4, keep, row(ln1_gain), row(ln1_bias))

    ents = ring_gather(e)
    qkv = jnp.zeros((NT, TS, 3 * HL * HP), bf)
    for j in (0, 1, 3, 2):
        qkv = qkv_call(me, j, ents[j], qkvp, bias_p, qkv)
    flat = qkv.reshape(NT * TS, 3 * HL * HP)
    att, probs = attn_call(flat, tab, sel, mask, spread, keys, jnp.zeros((NT * TS, HL * HP), bf))
    att4 = att.reshape(NT, TS, HL * HP)
    r0, r1, r2, r3 = partial_call(me, att4, projp, "proj")
    c1, c3 = ring_scatter(r1, r2, r3)
    h, z = ln2_call(r0, c1, c3, x, keep, row(proj_bias), row(ln2_gain), row(ln2_bias))

    gbs = ring_gather(gb)
    zs = ring_gather(z)
    mlp = {}
    for j in (0, 1, 3, 2):
        mlp[j] = mlp_call(zs[j], gbs[j], all2, row(fc1_bias), f32 if j == 0 else bf)
    acts = [mlp[j][0] for j in range(NT)]
    gpres = [mlp[j][1] for j in range(NT)]
    sum_fc1_bias = sum(mlp[j][4] for j in range(NT))
    c1, c3 = ring_scatter(mlp[1][3], mlp[2][3], mlp[3][3])
    grad2 = fcgrad_call(zs, gpres, gbs, acts)
    gh, gproj, sum_ln2_gain, sum_ln2_bias, sum_proj_bias = ln2b_call(
        mlp[0][3], c1, c3, h, c, keep, row(ln2_gain)
    )
    gps = ring_gather(gproj)
    own_fc = lax.psum_scatter(grad2, "shard", scatter_dimension=0, tiled=True)
    ga = jnp.zeros((NT, TS, HL * HP), bf)
    none = jnp.zeros((1, HL * HP), f32)
    for j in (0, 1, 3, 2):
        ga = qkv_call(me, j, gps[j], projp, none, ga)
    dqkv, rel, sum_qkv_bias = attnb_call(
        flat,
        probs,
        ga.reshape(NT * TS, HL * HP),
        tab,
        sel,
        mask,
        spread,
        jnp.zeros((NT * TS, 3 * HL * HP), bf),
    )
    dqkv4 = dqkv.reshape(NT, TS, 3 * HL * HP)
    r0, r1, r2, r3 = partial_call(me, dqkv4, qkvp, "gnorm1")
    c1, c3 = ring_scatter(r1, r2, r3)
    grad1 = qpgrad_call(me, ents, gps, dqkv4, att4)
    own_qp = lax.psum_scatter(grad1, "shard", scatter_dimension=0, tiled=True)
    gt4, sum_ln1_gain, sum_ln1_bias = ln1b_call(r0, c1, c3, x, gh, keep, row(ln1_gain))
    token_grads = unwindows(lax.all_to_all(gt4, "tp", 0, 0, tiled=True)).astype(f32)

    c1, c3 = ring_scatter(mlp[1][2], mlp[2][2], mlp[3][2])
    res4 = result_call(mlp[0][2], c1, c3, h, keep, row(fc2_bias))
    result = unwindows(lax.all_to_all(res4, "tp", 0, 0, tiled=True))

    rels = jnp.dot(sel.astype(f32).T, rel, precision=lax.Precision.HIGHEST)
    world = [
        sum_ln1_gain,
        sum_ln1_bias,
        sum_ln2_gain,
        sum_ln2_bias,
        sum_proj_bias,
        sum_fc2_bias,
        rels[:RELS, :HDIM],
        rels[32 : 32 + RELS, :HDIM],
    ]
    world = jnp.concatenate([v.ravel() for v in world])
    world = jnp.sum(from_everyone(world, "tp"), axis=0)
    qb = sum_qkv_bias.reshape(3, HL, HP)[:, :, :HDIM].reshape(3, HL * HDIM)
    every = jnp.concatenate([world, qb[0], qb[2], sum_fc1_bias.ravel()]).astype(bf)
    every = jnp.sum(from_everyone(every, ("shard", "ctx")).astype(f32), axis=0)
    cuts = [D] * 6 + [RELS * HDIM] * 2 + [2 * HL * HDIM, D]
    ends = np.cumsum([0] + cuts)
    small = [every[a:b] for a, b in zip(ends, ends[1:])]

    swap = [(0, 1), (1, 0)]
    fc = own_fc.astype(f32) + lax.ppermute(own_fc, "ctx", swap).astype(f32)
    qp = own_qp.astype(f32) + lax.ppermute(own_qp, "ctx", swap).astype(f32)
    return (
        result,
        token_grads,
        small[0],
        small[1],
        jnp.moveaxis(qp[:, :960].reshape(80, 3, 320), 0, 1),
        small[8].reshape(2, HL * HDIM),
        small[6].reshape(RELS, HDIM),
        small[7].reshape(RELS, HDIM),
        qp[:, 960:].T,
        small[4],
        small[2],
        small[3],
        fc[:, :D],
        small[9],
        fc[:, D:].T,
        small[5],
    )


def solution(mesh):
    cells = P("shard", "ctx", None, "tp")
    in_specs = (
        cells,
        P("shard", "ctx", None),
        P(),
        P(),
        P(None, "shard", "tp"),
        P(None, "tp"),
        P(),
        P(),
        P("tp", "shard"),
        P(),
        P(),
        P(),
        P("shard", "tp"),
        P("tp"),
        P("tp", "shard"),
        P(),
        cells,
    )
    out_specs = (
        cells,
        cells,
        P(),
        P(),
        P(None, "shard", "tp"),
        P(None, "tp"),
        P(),
        P(),
        P("tp", "shard"),
        P(),
        P(),
        P(),
        P("shard", "tp"),
        P("tp"),
        P("tp", "shard"),
        P(),
    )
    return jax.shard_map(local, mesh=mesh, in_specs=in_specs, out_specs=out_specs, check_vma=False)
```

```python
from functools import partial

import jax
import jax.numpy as jnp
import numpy as np
from jax import lax
from jax.experimental import pallas as pl
from jax.experimental.pallas import tpu as pltpu
from jax.sharding import PartitionSpec as P

HEADS = 16
HDIM = 80
WIN = 14
D = 1280
NT = 4
HL = HEADS // NT
CELLS = WIN * WIN
WR = 208
NW = 6
TS = 320
HALF = TS // 2
HP = 128
RELS = 2 * WIN - 1
EPS = 1e-06
SCALE = HDIM ** (-0.5)
bf = jnp.bfloat16
f32 = jnp.float32
MB = 1024 * 1024


def rel_constants():
    sel = np.zeros((512, 64), np.float32)
    mask = np.zeros((WR, 512), np.float32)
    spread = np.zeros((512, WR), np.float32)
    for a in range(WIN):
        for x in range(WIN):
            sel[a * WIN + x, a - x + WIN - 1] = 1
            sel[256 + a * WIN + x, 32 + a - x + WIN - 1] = 1
    for a in range(WIN):
        for b in range(WIN):
            row = a * WIN + b
            mask[row, a * WIN : a * WIN + WIN] = 1
            mask[row, 256 + b * WIN : 256 + b * WIN + WIN] = 1
    for a in range(WIN):
        for x in range(WIN):
            for y in range(WIN):
                spread[a * WIN + x, x * WIN + y] = 1
                spread[256 + a * WIN + y, x * WIN + y] = 1
    keys = np.where(np.arange(WR) < CELLS, 0.0, -1e30).astype(np.float32)[None]
    return sel, mask, spread, keys


def dot(a, b):
    return lax.dot_general(a, b, (((1,), (0,)), ((), ())), preferred_element_type=f32)


def dot_nt(a, b):
    return lax.dot_general(a, b, (((1,), (1,)), ((), ())), preferred_element_type=f32)


def dot_tn(a, b):
    return lax.dot_general(a, b, (((0,), (0,)), ((), ())), preferred_element_type=f32)


def params(mb=16):
    return pltpu.CompilerParams(vmem_limit_bytes=mb * MB)


def cost(flops, nbytes, trans=0):
    return pl.CostEstimate(flops=int(flops), bytes_accessed=int(nbytes), transcendentals=int(trans))


def sds(shape, dtype):
    return jax.ShapeDtypeStruct(shape, dtype)


def full(shape):
    return pl.BlockSpec(shape, lambda *g: (0,) * len(shape))


ANY = pl.BlockSpec(memory_space=pl.ANY)


def stats(x):
    mean = jnp.sum(x, axis=1, keepdims=True) * (1.0 / D)
    xc = x - mean
    var = jnp.sum(xc * xc, axis=1, keepdims=True) * (1.0 / D)
    inv = lax.rsqrt(var + EPS)
    return xc * inv, inv


def colsum(x):
    return jnp.sum(x, axis=0, keepdims=True)


def acc_out(ref, value):
    @pl.when(pl.program_id(0) == 0)
    def _():
        ref[...] = jnp.zeros_like(ref)

    ref[...] += value


RB = 80


def in_feature_order(me, t, refs, use):
    r0, r1, ra, rb, r3 = refs
    r2 = jnp.where(t < NT // 2, ra[0].astype(f32), rb[0].astype(f32))
    parts = (r0[0].astype(f32), r1[0].astype(f32), r2, r3[0].astype(f32))
    for k in range(NT):

        @pl.when(me == k)
        def _(k=k):
            use(jnp.concatenate([parts[(b - k) % NT] for b in range(NT)], axis=1))


def ln1_body(me_ref, r0, r1, ra, rb, r3, keep_ref, g_ref, b_ref, x_ref, e_ref):
    me = me_ref[0]
    j = pl.program_id(0)

    def use(x):
        n, _ = stats(x)
        e_ref[0] = (keep_ref[0] * (n * g_ref[...] + b_ref[...])).astype(bf)

        @pl.when(j == 0)
        def _():
            x_ref[...] = x.astype(bf)

    in_feature_order(me, block_of(me, j), (r0, r1, ra, rb, r3), use)


def cot_body(me_ref, r0, r1, ra, rb, r3, keep_ref, c_ref, gb_ref, fb_ref):
    me = me_ref[0]
    j = pl.program_id(0)

    @pl.when((j == 0) & (pl.program_id(1) == 0))
    def _():
        fb_ref[...] = jnp.zeros_like(fb_ref)

    def use(c):
        gb = keep_ref[0] * c
        gb_ref[0] = gb.astype(bf)

        @pl.when(j == 0)
        def _():
            c_ref[...] = c.astype(bf)
            fb_ref[...] += colsum(gb)

    in_feature_order(me, block_of(me, j), (r0, r1, ra, rb, r3), use)


def raw_specs():
    steps = TS // RB
    blk = pl.BlockSpec((1, RB, TS), lambda j, i, m: (block_of(m[0], j), i, 0))
    lo = pl.BlockSpec((1, RB, TS), lambda j, i, m: (jnp.minimum(block_of(m[0], j), 1), i, 0))
    hi = pl.BlockSpec((1, RB, TS), lambda j, i, m: (jnp.maximum(block_of(m[0], j) - 2, 0), i, 0))
    keep = pl.BlockSpec((1, RB, 1), lambda j, i, m: (block_of(m[0], j), i, 0))
    mine = pl.BlockSpec((RB, D), lambda j, i, m: (jnp.minimum(j * steps + i, steps - 1), 0))
    vec = pl.BlockSpec((1, D), lambda j, i, m: (0, 0))
    return (NT, steps), [blk, blk, lo, hi, blk, keep], mine, vec


def ln1_call(me, parts, keep4, g, b):
    grid, ins, mine, vec = raw_specs()
    return pl.pallas_call(
        ln1_body,
        grid_spec=pltpu.PrefetchScalarGridSpec(
            num_scalar_prefetch=1,
            grid=grid,
            in_specs=ins + [vec, vec],
            out_specs=[mine, pl.BlockSpec((1, RB, D), lambda j, i, m: (block_of(m[0], j), i, 0))],
        ),
        out_shape=[sds((TS, D), bf), sds((NT, TS, D), bf)],
        compiler_params=params(),
        cost_estimate=cost(80 * TS * D, 20 * TS * D),
        name="ln1",
    )(me, *parts, keep4, g, b)


def cot_call(me, parts, keep4):
    grid, ins, mine, vec = raw_specs()
    return pl.pallas_call(
        cot_body,
        grid_spec=pltpu.PrefetchScalarGridSpec(
            num_scalar_prefetch=1,
            grid=grid,
            in_specs=ins,
            out_specs=[mine, pl.BlockSpec((1, RB, D), lambda j, i, m: (j, i, 0)), vec],
        ),
        out_shape=[sds((TS, D), bf), sds((NT, TS, D), bf), sds((1, D), f32)],
        compiler_params=params(),
        cost_estimate=cost(80 * TS * D, 20 * TS * D),
        name="cot",
    )(me, *parts, keep4)


def ln2_body(r0, c1, c3, x, keep, pb, g, b, h_ref, e_ref):
    s = r0[...] + c1[...].astype(f32) + c3[...].astype(f32)
    h = x[...].astype(f32) + keep[...] * (s + pb[...])
    h_ref[...] = h
    n, _ = stats(h)
    e_ref[...] = (n * g[...] + b[...]).astype(bf)


def ln2_call(r0, c1, c3, x, keep, pb, g, b):
    row = pl.BlockSpec((RB, D), lambda i: (i, 0))
    kp = pl.BlockSpec((RB, 1), lambda i: (i, 0))
    return pl.pallas_call(
        ln2_body,
        grid=(TS // RB,),
        in_specs=[row, row, row, row, kp] + [full((1, D))] * 3,
        out_specs=[row, row],
        out_shape=[sds((TS, D), f32), sds((TS, D), bf)],
        compiler_params=params(),
        cost_estimate=cost(20 * TS * D, 16 * TS * D),
        name="ln2",
    )(r0, c1, c3, x, keep, pb, g, b)


def result_body(r0, c1, c3, h, keep, fb, o_ref):
    s = r0[...] + c1[...].astype(f32) + c3[...].astype(f32)
    o = (h[...] + keep[...] * (s + fb[...])).astype(bf)
    for k in range(NT):
        o_ref[k] = o[:, k * TS : (k + 1) * TS]


def result_call(r0, c1, c3, h, keep, fb):
    row = pl.BlockSpec((RB, D), lambda i: (i, 0))
    kp = pl.BlockSpec((RB, 1), lambda i: (i, 0))
    return pl.pallas_call(
        result_body,
        grid=(TS // RB,),
        in_specs=[row, row, row, row, kp, full((1, D))],
        out_specs=pl.BlockSpec((NT, RB, TS), lambda i: (0, i, 0)),
        out_shape=sds((NT, TS, TS), bf),
        compiler_params=params(),
        cost_estimate=cost(8 * TS * D, 14 * TS * D),
        name="result",
    )(r0, c1, c3, h, keep, fb)


def norm_back(w, n, inv):
    m1 = jnp.sum(w, axis=1, keepdims=True) * (1.0 / D)
    m2 = jnp.sum(w * n, axis=1, keepdims=True) * (1.0 / D)
    return inv * (w - m1 - n * m2)


def ln2b_body(r0, c1, c3, h, c, keep, g, gh_ref, gp_ref, gg_ref, gb_ref, pb_ref):
    gn = r0[...] + c1[...].astype(f32) + c3[...].astype(f32)
    n, inv = stats(h[...])
    gh = c[...].astype(f32) + norm_back(gn * g[...], n, inv)
    gh_ref[...] = gh
    kg = keep[...] * gh
    gp_ref[...] = kg.astype(bf)
    acc_out(gg_ref, colsum(gn * n))
    acc_out(gb_ref, colsum(gn))
    acc_out(pb_ref, colsum(kg))


def ln2b_call(r0, c1, c3, h, c, keep, g):
    row = pl.BlockSpec((RB, D), lambda i: (i, 0))
    kp = pl.BlockSpec((RB, 1), lambda i: (i, 0))
    return pl.pallas_call(
        ln2b_body,
        grid=(TS // RB,),
        in_specs=[row, row, row, row, row, kp, full((1, D))],
        out_specs=[row, row] + [full((1, D))] * 3,
        out_shape=[sds((TS, D), f32), sds((TS, D), bf)] + [sds((1, D), f32)] * 3,
        compiler_params=params(),
        cost_estimate=cost(30 * TS * D, 20 * TS * D),
        name="ln2b",
    )(r0, c1, c3, h, c, keep, g)


def ln1b_body(r0, c1, c3, x, gh, keep, g, o_ref, gg_ref, gb_ref):
    gn = keep[...] * (r0[...] + c1[...].astype(f32) + c3[...].astype(f32))
    n, inv = stats(x[...].astype(f32))
    gt = (gh[...] + norm_back(gn * g[...], n, inv)).astype(bf)
    for k in range(NT):
        o_ref[k] = gt[:, k * TS : (k + 1) * TS]
    acc_out(gg_ref, colsum(gn * n))
    acc_out(gb_ref, colsum(gn))


def ln1b_call(r0, c1, c3, x, gh, keep, g):
    row = pl.BlockSpec((RB, D), lambda i: (i, 0))
    kp = pl.BlockSpec((RB, 1), lambda i: (i, 0))
    return pl.pallas_call(
        ln1b_body,
        grid=(TS // RB,),
        in_specs=[row, row, row, row, row, kp, full((1, D))],
        out_specs=[pl.BlockSpec((NT, RB, TS), lambda i: (0, i, 0))] + [full((1, D))] * 2,
        out_shape=[sds((NT, TS, TS), bf)] + [sds((1, D), f32)] * 2,
        compiler_params=params(),
        cost_estimate=cost(30 * TS * D, 18 * TS * D),
        name="ln1b",
    )(r0, c1, c3, x, gh, keep, g)


def pad_body(w_ref, q_ref, p_ref):
    rows = w_ref.shape[0]
    w = w_ref[...]
    zero = jnp.zeros((rows, HP - HDIM), bf)
    for h in range(3 * HL):
        q_ref[:, h * HP : (h + 1) * HP] = jnp.concatenate([w[:, h * HDIM : (h + 1) * HDIM], zero], axis=1)
    for h in range(HL):
        s = 3 * HL + h
        p_ref[:, h * HP : (h + 1) * HP] = jnp.concatenate([w[:, s * HDIM : (s + 1) * HDIM], zero], axis=1)


def pad_call(g1):
    rb = 160
    return pl.pallas_call(
        pad_body,
        grid=(D // rb,),
        in_specs=[pl.BlockSpec((rb, D), lambda i: (i, 0))],
        out_specs=[
            pl.BlockSpec((rb, 3 * HL * HP), lambda i: (i, 0)),
            pl.BlockSpec((rb, HL * HP), lambda i: (i, 0)),
        ],
        out_shape=[sds((D, 3 * HL * HP), bf), sds((D, HL * HP), bf)],
        compiler_params=params(),
        cost_estimate=cost(D * 2048, 2 * D * (1280 + 2048)),
        name="padw",
    )(g1)


def block_of(me, j):
    return lax.rem(me + j, NT)


def qkv_body(x_ref, w_ref, b_ref, o_ref):
    o_ref[...] = (dot(x_ref[...], w_ref[...]) + b_ref[...]).astype(bf)


def qkv_call(x, w, bias):
    n = w.shape[1]
    tn = 512
    rows = x.shape[0]
    return pl.pallas_call(
        qkv_body,
        grid=(n // tn,),
        in_specs=[
            full((rows, D)),
            pl.BlockSpec((D, tn), lambda i: (0, i)),
            pl.BlockSpec((1, tn), lambda i: (0, i)),
        ],
        out_specs=pl.BlockSpec((rows, tn), lambda i: (0, i)),
        out_shape=sds((rows, n), bf),
        compiler_params=params(24),
        cost_estimate=cost(2 * rows * D * n, 2 * (rows * D + D * n + rows * n)),
        name="qkv",
    )(x, w, bias)


def gatt_body(*refs):
    count = len(refs) - 4
    w_ref, o_ref = refs[1 + count], refs[-1]
    for t in range(count):

        @pl.when(pl.program_id(0) == t)
        def _(t=t):
            o_ref[0] = dot(refs[1 + t][...], w_ref[...]).astype(bf)


def gatt_call(me, which, xs, w, into):
    n = w.shape[1]
    k = len(which)
    first, step = which[0], which[-1] - which[0]
    return pl.pallas_call(
        gatt_body,
        grid_spec=pltpu.PrefetchScalarGridSpec(
            num_scalar_prefetch=1,
            grid=(k,),
            in_specs=[pl.BlockSpec((TS, D), lambda t, m: (0, 0))] * k
            + [pl.BlockSpec((D, n), lambda t, m: (0, 0)), ANY],
            out_specs=pl.BlockSpec((1, TS, n), lambda t, m: (block_of(m[0], first + step * t), 0, 0)),
        ),
        out_shape=sds((NT, TS, n), bf),
        input_output_aliases={2 + k: 0},
        compiler_params=params(),
        cost_estimate=cost(2 * k * TS * D * n, 2 * (k * TS * D + D * n + k * TS * n)),
        name="gatt",
    )(me, *xs, w, into)


def gatt2_body(me_ref, a_ref, b_ref, w_ref, z_ref, o_ref, p_ref):
    p_ref[:HALF] = a_ref[...]
    p_ref[HALF:] = b_ref[...]
    o_ref[0] = dot(p_ref[...], w_ref[...]).astype(bf)


def gatt2_call(me, halves, w, into):
    n = w.shape[1]
    half = pl.BlockSpec((HALF, D), lambda i, m: (0, 0))
    return pl.pallas_call(
        gatt2_body,
        grid_spec=pltpu.PrefetchScalarGridSpec(
            num_scalar_prefetch=1,
            grid=(1,),
            in_specs=[half, half, pl.BlockSpec((D, n), lambda i, m: (0, 0)), ANY],
            out_specs=[
                pl.BlockSpec((1, TS, n), lambda i, m: (block_of(m[0], 2), 0, 0)),
                pl.BlockSpec((TS, D), lambda i, m: (0, 0)),
            ],
        ),
        out_shape=[sds((NT, TS, n), bf), sds((TS, D), bf)],
        input_output_aliases={4: 0},
        compiler_params=params(),
        cost_estimate=cost(2 * TS * D * n, 2 * (2 * TS * D + D * n + TS * n)),
        name="gatt",
    )(me, *halves, w, into)


def attn_body(qkv_ref, tab_ref, sel_ref, mask_ref, sp_ref, km_ref, z_ref, o_ref, p_ref, t_ref):
    @pl.when(pl.program_id(0) == 0)
    def _():
        t_ref[...] = dot(sel_ref[...], tab_ref[...]).astype(bf)

    table = t_ref[...]
    for h in range(HL):
        q = qkv_ref[:, h * HP : (h + 1) * HP]
        k = qkv_ref[:, (HL + h) * HP : (HL + h + 1) * HP]
        v = qkv_ref[:, (2 * HL + h) * HP : (2 * HL + h + 1) * HP]
        along = (dot_nt(q, table) * mask_ref[...].astype(f32)).astype(bf)
        s = dot_nt(q, k) * SCALE + dot(along, sp_ref[...]) + km_ref[...]
        top = jnp.max(s, axis=1, keepdims=True)
        e = jnp.exp(s - top)
        p = (e * (1.0 / jnp.sum(e, axis=1, keepdims=True))).astype(bf)
        p_ref[0, h] = p
        o_ref[:, h * HP : (h + 1) * HP] = dot(p, v).astype(bf)


def attn_call(qkv, tab, sel, mask, spread, keys, into):
    n = 3 * HL * HP
    return pl.pallas_call(
        attn_body,
        grid=(NW,),
        in_specs=[
            pl.BlockSpec((WR, n), lambda i: (i, 0)),
            full((64, HP)),
            full((512, 64)),
            full((WR, 512)),
            full((512, WR)),
            full((1, WR)),
            ANY,
        ],
        out_specs=[
            pl.BlockSpec((WR, HL * HP), lambda i: (i, 0)),
            pl.BlockSpec((1, HL, WR, WR), lambda i: (i, 0, 0, 0)),
        ],
        out_shape=[sds((NT * TS, HL * HP), bf), sds((NW, HL, WR, WR), bf)],
        scratch_shapes=[pltpu.VMEM((512, HP), bf)],
        input_output_aliases={6: 0},
        compiler_params=params(),
        cost_estimate=cost(24 * 6 * 2 * WR * WR * 256, 8e6, 24 * WR * 256),
        name="attn",
    )(qkv, tab, sel, mask, spread, keys, into)


def attnb_body(qkv_ref, p_ref, ga_ref, tab_ref, sel_ref, mask_ref, sp_ref, z_ref, o_ref, rel_ref, bias_ref, t_ref):
    @pl.when(pl.program_id(0) == 0)
    def _():
        t_ref[...] = dot(sel_ref[...], tab_ref[...]).astype(bf)
        rel_ref[...] = jnp.zeros_like(rel_ref)
        bias_ref[...] = jnp.zeros_like(bias_ref)

    table = t_ref[...]
    rel = jnp.zeros((512, HP), f32)
    for h in range(HL):
        cq = slice(h * HP, (h + 1) * HP)
        ck = slice((HL + h) * HP, (HL + h + 1) * HP)
        cv = slice((2 * HL + h) * HP, (2 * HL + h + 1) * HP)
        q = qkv_ref[:, cq]
        k = qkv_ref[:, ck]
        v = qkv_ref[:, cv]
        ga = ga_ref[:, cq]
        p = p_ref[0, h]
        pf = p.astype(f32)
        gs = dot_nt(ga, v)
        delta = jnp.sum(pf * gs, axis=1, keepdims=True)
        ds = (pf * (gs - delta)).astype(bf)
        gv = dot_tn(p, ga).astype(bf)
        gk = (dot_tn(ds, q) * SCALE).astype(bf)
        sums = (dot_nt(ds, sp_ref[...]) * mask_ref[...].astype(f32)).astype(bf)
        gq = (dot(ds, k) * SCALE + dot(sums, table)).astype(bf)
        rel = rel + dot_tn(sums, q)
        o_ref[:, cq] = gq
        o_ref[:, ck] = gk
        o_ref[:, cv] = gv
        bias_ref[:, cq] += colsum(gq.astype(f32))
        bias_ref[:, cv] += colsum(gv.astype(f32))
    rel_ref[...] += rel


def attnb_call(qkv, p, ga, tab, sel, mask, spread, into):
    n = 3 * HL * HP
    return pl.pallas_call(
        attnb_body,
        grid=(NW,),
        in_specs=[
            pl.BlockSpec((WR, n), lambda i: (i, 0)),
            pl.BlockSpec((1, HL, WR, WR), lambda i: (i, 0, 0, 0)),
            pl.BlockSpec((WR, HL * HP), lambda i: (i, 0)),
            full((64, HP)),
            full((512, 64)),
            full((WR, 512)),
            full((512, WR)),
            ANY,
        ],
        out_specs=[pl.BlockSpec((WR, n), lambda i: (i, 0)), full((512, HP)), full((1, n))],
        out_shape=[sds((NT * TS, n), bf), sds((512, HP), f32), sds((1, n), f32)],
        scratch_shapes=[pltpu.VMEM((512, HP), bf)],
        input_output_aliases={7: 0},
        compiler_params=params(),
        cost_estimate=cost(24 * 10 * 2 * WR * WR * 256, 14e6),
        name="attnb",
    )(qkv, p, ga, tab, sel, mask, spread, into)


def partial_body(me_ref, a_ref, w_ref, r0, r1, r2a, r2b, r3):
    w = w_ref[...]
    for j, ref in ((2, None), (1, r1), (3, r3), (0, r0)):
        r = dot_nt(a_ref[block_of(me_ref[0], j)], w)
        if ref is None:
            r2a[...] = r[:HALF].astype(bf)
            r2b[...] = r[HALF:].astype(bf)
        else:
            ref[...] = r.astype(ref.dtype)


def partial_call(me, a, w, name):
    k = a.shape[2]
    tn = 256
    whole = pl.BlockSpec((TS, tn), lambda i, m: (0, i))
    half = pl.BlockSpec((HALF, tn), lambda i, m: (0, i))
    return pl.pallas_call(
        partial_body,
        grid_spec=pltpu.PrefetchScalarGridSpec(
            num_scalar_prefetch=1,
            grid=(D // tn,),
            in_specs=[
                pl.BlockSpec((NT, TS, k), lambda i, m: (0, 0, 0)),
                pl.BlockSpec((tn, k), lambda i, m: (i, 0)),
            ],
            out_specs=[whole, whole, half, half, whole],
        ),
        out_shape=[sds((TS, D), f32), sds((TS, D), bf), sds((HALF, D), bf), sds((HALF, D), bf), sds((TS, D), bf)],
        compiler_params=params(),
        cost_estimate=cost(2 * NT * TS * D * k, 2 * (NT * TS * k + D * k + 5 * TS * D)),
        name=name,
    )(me, a, w)


def merge_body(r1, a, r3, b, s1, s3):
    s1[...] = (r1[...].astype(f32) + a[...].astype(f32)).astype(bf)
    s3[...] = (r3[...].astype(f32) + b[...].astype(f32)).astype(bf)


def merge_call(r1, a, r3, b):
    one = pl.BlockSpec((HALF, D), lambda i: (0, 0))
    two = pl.BlockSpec((HALF, D), lambda i: (1, 0))
    return pl.pallas_call(
        merge_body,
        grid=(1,),
        in_specs=[one, one, two, one],
        out_specs=[one, two],
        out_shape=[sds((TS, D), bf)] * 2,
        input_output_aliases={0: 0, 2: 1},
        compiler_params=params(),
        cost_estimate=cost(4 * HALF * D, 12 * HALF * D),
        name="merge",
    )(r1, a, r3, b)


def mlp_body(halved, *refs):
    if halved:
        k = 1
        za, zb, gb_ref, w1_ref, w2_ref, b1_ref = refs[:6]
        z_refs, gb_refs = [refs[13]], [gb_ref]
        outs = refs[6:13]
        scratch = refs[14:]
    else:
        k = (len(refs) - 3) // 9
        z_refs, gb_refs = refs[:k], refs[k : 2 * k]
        w1_ref, w2_ref, b1_ref = refs[2 * k : 2 * k + 3]
        outs = refs[2 * k + 3 : 7 * k + 3]
        scratch = refs[7 * k + 3 :]
    step = pl.program_id(0)
    last = pl.num_programs(0) - 1
    if halved:

        @pl.when(step == 0)
        def _():
            z_refs[0][:HALF] = za[...]
            z_refs[0][HALF:] = zb[...]

    w1 = w1_ref[...]
    w2 = w2_ref[...]
    for t in range(k):
        if halved:
            act_ref, gp_ref, fb_ref = outs[0], outs[1], outs[6]
            finals = ((outs[2], outs[3]), (outs[4], outs[5]))
        else:
            act_ref, gp_ref, br_ref, gn_ref, fb_ref = outs[5 * t : 5 * t + 5]
            finals = ((br_ref,), (gn_ref,))
        br_s, gn_s = scratch[2 * t : 2 * t + 2]
        pre = dot(z_refs[t][...], w1) + b1_ref[...]
        ga = dot(gb_refs[t][0], w2)
        cdf = 0.5 + 0.5 * lax.erf(pre * 0.7071067811865476)
        act = (pre * cdf).astype(bf)
        slope = cdf + pre * (0.3989422804014327 * jnp.exp(-0.5 * pre * pre))
        gp = (ga * slope).astype(bf)
        act_ref[...] = act
        gp_ref[...] = gp
        fb_ref[...] = colsum(gp.astype(f32))
        br = dot_nt(act, w2)
        gn = dot_nt(gp, w1)

        @pl.when(step == 0)
        def _():
            br_s[...] = br
            gn_s[...] = gn

        @pl.when((step > 0) & (step < last))
        def _():
            br_s[...] += br
            gn_s[...] += gn

        @pl.when(step == last)
        def _():
            for total, refs_out in ((br_s[...] + br, finals[0]), (gn_s[...] + gn, finals[1])):
                if halved:
                    refs_out[0][...] = total[:HALF].astype(bf)
                    refs_out[1][...] = total[HALF:].astype(bf)
                else:
                    refs_out[0][...] = total.astype(refs_out[0].dtype)


def mlp_call(which, zs, gb, w, b1, kind):
    halved = which == (2,)
    k = len(which)
    tf = 256
    nf = D // tf
    col = pl.BlockSpec((TS, tf), lambda i: (0, i))
    bias = pl.BlockSpec((1, tf), lambda i: (0, i))
    half = full((HALF, D))
    block = full((TS, D))
    if halved:
        ins = [half, half]
        outs = [col, col, half, half, half, half, bias, block]
        shapes = [sds((TS, D), bf)] * 2 + [sds((HALF, D), bf)] * 4 + [sds((1, D), f32), sds((TS, D), bf)]
    else:
        ins = [block] * k
        outs = [col, col, block, block, bias] * k
        shapes = [sds((TS, D), bf), sds((TS, D), bf), sds((TS, D), kind), sds((TS, D), kind), sds((1, D), f32)] * k
    flat = pl.pallas_call(
        partial(mlp_body, halved),
        grid=(nf,),
        in_specs=ins
        + [pl.BlockSpec((1, TS, D), lambda i, j=j: (j, 0, 0)) for j in which]
        + [
            pl.BlockSpec((D, tf), lambda i: (0, i)),
            pl.BlockSpec((D, tf), lambda i: (0, i + nf)),
            bias,
        ],
        out_specs=outs,
        out_shape=shapes,
        scratch_shapes=[pltpu.VMEM((TS, D), f32)] * (2 * k),
        compiler_params=params(32),
        cost_estimate=cost(k * 8 * TS * D * D, 4 * D * D + k * 12 * TS * D, k * 2 * TS * D),
        name="mlp",
    )(*zs, *[gb] * k, w, w, b1)
    if halved:
        return flat
    return [flat[5 * t : 5 * t + 5] for t in range(k)]


NG = 2 * D + HL * HP


def tokgrad_body(*refs):
    o_ref = refs[-1]
    lhs, rhs = refs[:4], refs[4:8]
    total = None
    for j in range(NT):
        left = lhs[j][0] if len(lhs[j].shape) == 3 else lhs[j][...]
        part = dot_tn(left, rhs[j][...])
        total = part if total is None else total + part
    o_ref[...] = total.astype(bf)


def tokgrad_call(lhs, rhs, into, at):
    td = 256
    if len(lhs) == 1:
        left = [pl.BlockSpec((1, TS, td), lambda i, j=j: (j, 0, i)) for j in range(NT)]
        lhs = list(lhs) * NT
    else:
        left = [pl.BlockSpec((TS, td), lambda i: (0, i))] * NT
    return pl.pallas_call(
        tokgrad_body,
        grid=(D // td,),
        in_specs=left + [full((TS, D))] * NT + [ANY] * (into is not None),
        out_specs=pl.BlockSpec((td, D), lambda i: (i, at)),
        out_shape=sds((D, NG), bf),
        input_output_aliases={} if into is None else {2 * NT: 0},
        compiler_params=params(24),
        cost_estimate=cost(8 * TS * D * D, 2 * (8 * TS * D + D * D)),
        name="fcgrad",
    )(*lhs, *rhs, *(() if into is None else (into,)))


def narrow(x, heads):
    return jnp.concatenate([x[:, h * HP : h * HP + HDIM] for h in range(heads)], axis=1)


def projgrad_body(me_ref, e0, e1, e2, e3, a_ref, z_ref, o_ref):
    total = None
    for j, e in enumerate((e0, e1, e2, e3)):
        part = dot_tn(e[...], a_ref[block_of(me_ref[0], j)])
        total = part if total is None else total + part
    o_ref[...] = total.astype(bf)


def projgrad_call(me, e, a, into, at):
    td = 256
    n = a.shape[2]
    return pl.pallas_call(
        projgrad_body,
        grid_spec=pltpu.PrefetchScalarGridSpec(
            num_scalar_prefetch=1,
            grid=(D // td,),
            in_specs=[pl.BlockSpec((TS, td), lambda i, m: (0, i))] * 4
            + [pl.BlockSpec((NT, TS, n), lambda i, m: (0, 0, 0)), ANY],
            out_specs=pl.BlockSpec((td, n), lambda i, m: (i, at)),
        ),
        out_shape=sds(into.shape, bf),
        input_output_aliases={6: 0},
        compiler_params=params(56),
        cost_estimate=cost(8 * TS * D * n, 2 * (4 * TS * D + 4 * TS * n + D * n)),
        name="projgrad",
    )(me, *e, a, into)


def qkvgrad_body(e_ref, a_ref, o_ref):
    o_ref[...] = narrow(dot_tn(e_ref[...], a_ref[...]), 3 * HL).astype(bf)


def qkvgrad_call(e, a):
    td = 256
    rows, n = a.shape
    m = 3 * HL * HDIM
    return pl.pallas_call(
        qkvgrad_body,
        grid=(D // td,),
        in_specs=[pl.BlockSpec((rows, td), lambda i: (0, i)), full((rows, n))],
        out_specs=pl.BlockSpec((td, m), lambda i: (i, 0)),
        out_shape=sds((D, m), bf),
        compiler_params=params(24),
        cost_estimate=cost(2 * rows * D * n, 2 * (rows * D + rows * n + D * m)),
        name="qkvgrad",
    )(e, a)


UP = [(i, (i + 1) % NT) for i in range(NT)]
DOWN = [(i, (i - 1) % NT) for i in range(NT)]


def up(v):
    return lax.ppermute(v, "tp", UP)


def down(v):
    return lax.ppermute(v, "tp", DOWN)


def after(v, *deps):
    return lax.optimization_barrier((v, deps))[0]


def ring_gather(own, first=None, between=None):
    b3 = up(own)
    b1 = down(own)
    if first is not None:
        b3, b1, first = lax.optimization_barrier((b3, b1, first))
    half = own.shape[0] // 2
    u, d = up(b3[:half]), down(b1[half:])
    if between is not None:
        first = between(b1, b3, first)
        u, d, first = lax.optimization_barrier((u, d, first))
    return (own, b1, u, d, b3), first


def ring_scatter(r1, r2a, r2b, r3, first=None):
    a = up(r2a)
    b = down(r2b)
    if first is not None:
        a, b, first = lax.optimization_barrier((a, b, first))
    s1, s3 = merge_call(r1, a, r3, b)
    return (s3, s1), first


def ring_finish(sums):
    return down(sums[0]), up(sums[1])


def shard_place():
    s = lax.axis_index("shard")
    return s // 4, (s // 2) % 2, s % 2


def shard_move(v, f):
    return lax.ppermute(v, "shard", [(i, f(i)) for i in range(16)])


def pick(v, i, ax):
    return lax.dynamic_index_in_dim(v, i, ax, keepdims=False)


def add_low(p, q):
    return (p.astype(f32) + q.astype(f32)).astype(bf)


def over_shard_1(v):
    n = v.shape[1]
    y, zl, core = shard_place()
    v = v.reshape(4, 2, 2, 80, n)
    v = add_low(pick(v, core, 2), shard_move(pick(v, 1 - core, 2), lambda i: i ^ 1))
    w = [pick(v, (y + j) % 4, 0) for j in range(4)]
    a = shard_move(w[2][0], lambda i: (i + 4) % 16)
    b = shard_move(w[2][1], lambda i: (i + 12) % 16)
    return w[0], jnp.stack([add_low(w[1][0], a), w[1][1]]), jnp.stack([w[3][0], add_low(w[3][1], b)])


def over_shard_2(parts):
    w0, s1, s3 = parts
    return w0, shard_move(s3, lambda i: (i + 12) % 16), shard_move(s1, lambda i: (i + 4) % 16)


def over_shard_3(parts):
    w0, c1, c3 = parts
    y, zl, core = shard_place()
    v = (w0.astype(f32) + c1.astype(f32) + c3.astype(f32)).astype(bf)
    return add_low(pick(v, zl, 0), shard_move(pick(v, 1 - zl, 0), lambda i: i ^ 2))


def over_ctx(v):
    return v.astype(f32) + lax.ppermute(v, "ctx", [(0, 1), (1, 0)]).astype(f32)


def small_sums(world, group):
    w = jnp.concatenate([a.ravel() for a in world])
    w = jnp.pad(w, (0, -w.size % 1024)).reshape(-1, 128)
    w = w + lax.ppermute(w, "tp", [(i, i ^ 1) for i in range(NT)])
    w = w + lax.ppermute(w, "tp", [(i, i ^ 3) for i in range(NT)])
    g = jnp.concatenate([a.ravel() for a in group])
    g = jnp.pad(g, (0, -g.size % 1024)).reshape(-1, 128)
    return jnp.concatenate([w, g], axis=0).astype(bf)


def small_finish(everyone, world, group):
    both = jnp.sum(everyone.astype(f32), axis=0)
    out, at = [], 0
    for part in (world, group):
        flat = both[at:].ravel()
        start = 0
        for a in part:
            out.append(flat[start : start + a.size].reshape(a.shape))
            start += a.size
        at += -(-start // 1024) * 8
    return out


def from_everyone(array, axis):
    size = lax.axis_size(axis)
    return lax.all_to_all(jnp.broadcast_to(array[None], (size, *array.shape)), axis, 0, 0, tiled=True)


def windows(grid):
    n = grid.shape[-1]
    w = grid.reshape(2, WIN, 3, WIN, n).transpose(0, 2, 1, 3, 4).reshape(NW, CELLS, n)
    w = jnp.pad(w, ((0, 0), (0, WR - CELLS), (0, 0))).reshape(NW * WR, n)
    return jnp.pad(w, ((0, NT * TS - NW * WR), (0, 0))).reshape(NT, TS, n)


def unwindows(blocks):
    n = blocks.shape[-1]
    w = blocks.reshape(NT * TS, n)[: NW * WR].reshape(NW, WR, n)[:, :CELLS]
    return w.reshape(2, 3, WIN, WIN, n).transpose(0, 2, 1, 3, 4).reshape(2, WIN, 3 * WIN, n)


def local(
    tokens,
    valid_mask,
    ln1_gain,
    ln1_bias,
    qkv_weight,
    qkv_bias,
    rel_rows,
    rel_cols,
    proj_weight,
    proj_bias,
    ln2_gain,
    ln2_bias,
    fc1_weight,
    fc1_bias,
    fc2_weight,
    fc2_bias,
    cotangent,
):
    tp_index = lax.axis_index("tp")
    me = tp_index.astype(jnp.int32).reshape(1)
    sel, mask, spread, keys = rel_constants()
    sel = jnp.asarray(sel, bf)
    mask = jnp.asarray(mask, bf)
    spread = jnp.asarray(spread, bf)
    keys = jnp.asarray(keys, f32)
    row = lambda v: v.reshape(1, -1)

    own1 = jnp.concatenate([jnp.moveaxis(qkv_weight, 1, 0).reshape(80, 960), proj_weight.T], axis=1)
    own2 = jnp.concatenate([fc1_weight, fc2_weight.T], axis=1)
    all1 = lax.all_gather(own1, "shard", axis=0, tiled=True)
    all2 = lax.all_gather(own2, "shard", axis=0, tiled=True)
    bias_q = jnp.pad(qkv_bias.reshape(2, HL, HDIM), ((0, 0), (0, 0), (0, HP - HDIM))).reshape(2, HL * HP)
    bias_p = row(jnp.concatenate([bias_q[0], jnp.zeros((HL * HP,), f32), bias_q[1]]))
    tab = jnp.zeros((64, HP), bf).at[:RELS, :HDIM].set(rel_rows).at[32 : 32 + RELS, :HDIM].set(rel_cols)

    keep4 = windows(valid_mask.astype(f32)[..., None])
    keep = lax.dynamic_index_in_dim(keep4, tp_index, 0, keepdims=False)
    toks, (qkvp, projp) = ring_gather(windows(tokens), None, lambda b1, b3, _: pad_call(all1))
    x, e4 = ln1_call(me, toks, keep4, row(ln1_gain), row(ln1_bias))
    ents = e4.reshape(NT * TS, D)
    cots, flat = ring_gather(after(windows(cotangent), toks[2], toks[3]), qkv_call(ents, qkvp, bias_p))
    att, probs = attn_call(flat, tab, sel, mask, spread, keys, jnp.zeros((NT * TS, HL * HP), bf))
    att4 = att.reshape(NT, TS, HL * HP)
    r0, *rest = partial_call(me, att4, projp, "proj")
    sums, _ = ring_scatter(*rest)
    sums, *cots = lax.optimization_barrier((sums, *cots))
    c, gb, sum_fc2_bias = cot_call(me, cots, keep4)
    (c1, c3), gb = lax.optimization_barrier((ring_finish(sums), gb))
    h, z = ln2_call(r0, c1, c3, x, keep, row(proj_bias), row(ln2_gain), row(ln2_bias))

    b1row = row(fc1_bias)
    mlp = lambda which, zz, kind: mlp_call(which, zz, gb, all2, b1row, kind)
    zs, ((m0,), (m1, m3)) = ring_gather(
        z, mlp((0,), (z,), f32), lambda b1, b3, first: (first, mlp((1, 3), (b1, b3), bf))
    )
    act2, gpre2, br2a, br2b, gn2a, gn2b, fb2, z2 = mlp((2,), (zs[2], zs[3]), bf)
    acts = (m0[0], m1[0], act2, m3[0])
    gpres = (m0[1], m1[1], gpre2, m3[1])
    sum_fc1_bias = m0[4] + m1[4] + fb2 + m3[4]
    sums, grads = ring_scatter(m1[3], gn2a, gn2b, m3[3], tokgrad_call((gb,), acts, None, 1))
    grads = tokgrad_call((z, zs[1], z2, zs[4]), gpres, grads, 0)
    (c1, c3), grads = lax.optimization_barrier((ring_finish(sums), grads))
    gh, gproj, sum_ln2_gain, sum_ln2_bias, sum_proj_bias = ln2b_call(
        m0[3], c1, c3, h, c, keep, row(ln2_gain)
    )
    ga = gatt_call(me, (0,), (gproj,), projp, jnp.zeros((NT, TS, HL * HP), bf))
    gps, ga = ring_gather(gproj, ga, lambda b1, b3, ga: gatt_call(me, (1, 3), (b1, b3), projp, ga))
    ga, gp2 = gatt2_call(me, gps[2:4], projp, ga)
    grads = projgrad_call(me, (gproj, gps[1], gp2, gps[4]), att4, grads, 5)
    own_fp = lax.psum_scatter(grads, "shard", scatter_dimension=0, tiled=True)
    ga = after(ga, grads)

    branch = after((m1[2], br2a, br2b, m3[2]), gp2)
    dqkv, rel, sum_qkv_bias = attnb_call(
        flat,
        probs,
        ga.reshape(NT * TS, HL * HP),
        tab,
        sel,
        mask,
        spread,
        jnp.zeros((NT * TS, 3 * HL * HP), bf),
    )
    sums, dqkv = ring_scatter(*branch, dqkv)
    sums, dqkv = lax.optimization_barrier((sums, dqkv))
    f1, f3 = ring_finish(sums)
    r0, *rest = partial_call(me, dqkv.reshape(NT, TS, 3 * HL * HP), qkvp, "gnorm1")
    gradq = qkvgrad_call(ents, dqkv)
    gradq, f1, f3 = lax.optimization_barrier((gradq, f1, f3))
    sums, gradq = ring_scatter(*rest, gradq)
    c1, c3 = ring_finish(sums)
    parts = over_shard_1(gradq)
    res4 = result_call(m0[2], f1, f3, h, keep, row(fc2_bias))
    result = lax.all_to_all(res4, "tp", 0, 0, tiled=True)
    c1, c3, parts, result = lax.optimization_barrier((c1, c3, parts, result))
    parts = over_shard_2(parts)
    gt4, sum_ln1_gain, sum_ln1_bias = ln1b_call(r0, c1, c3, x, gh, keep, row(ln1_gain))
    token_grads = lax.all_to_all(gt4, "tp", 0, 0, tiled=True)
    rels = jnp.dot(sel.astype(f32).T, rel, precision=lax.Precision.HIGHEST)
    qb = sum_qkv_bias.reshape(3, HL, HP)[:, :, :HDIM]
    world = [
        sum_ln1_gain,
        sum_ln1_bias,
        sum_ln2_gain,
        sum_ln2_bias,
        sum_proj_bias,
        sum_fc2_bias,
        rels[:RELS, :HDIM],
        rels[32 : 32 + RELS, :HDIM],
    ]
    group = [qb[0], qb[2], sum_fc1_bias]
    both = small_sums(world, group)
    token_grads, both, parts = lax.optimization_barrier((token_grads, both, parts))
    everyone = from_everyone(both, ("shard", "ctx"))
    own_q = over_shard_3(parts)
    result, token_grads = unwindows(result), unwindows(token_grads).astype(f32)
    g_ln1g, g_ln1b, g_ln2g, g_ln2b, g_pb, g_f2b, g_rr, g_rc, g_q, g_v, g_f1b = small_finish(everyone, world, group)

    fc = over_ctx(own_fp)
    p = fc[:, 2 * D :].reshape(80, HL, HP)[:, :, :HDIM].reshape(80, HL * HDIM)
    q = over_ctx(own_q)
    return (
        result,
        token_grads,
        g_ln1g.ravel(),
        g_ln1b.ravel(),
        jnp.moveaxis(q.reshape(80, 3, 320), 0, 1),
        jnp.stack([g_q.ravel(), g_v.ravel()]),
        g_rr,
        g_rc,
        p.T,
        g_pb.ravel(),
        g_ln2g.ravel(),
        g_ln2b.ravel(),
        fc[:, :D],
        g_f1b.ravel(),
        fc[:, D : 2 * D].T,
        g_f2b.ravel(),
    )


def solution(mesh):
    cells = P("shard", "ctx", None, "tp")
    in_specs = (
        cells,
        P("shard", "ctx", None),
        P(),
        P(),
        P(None, "shard", "tp"),
        P(None, "tp"),
        P(),
        P(),
        P("tp", "shard"),
        P(),
        P(),
        P(),
        P("shard", "tp"),
        P("tp"),
        P("tp", "shard"),
        P(),
        cells,
    )
    out_specs = (
        cells,
        cells,
        P(),
        P(),
        P(None, "shard", "tp"),
        P(None, "tp"),
        P(),
        P(),
        P("tp", "shard"),
        P(),
        P(),
        P(),
        P("shard", "tp"),
        P("tp"),
        P("tp", "shard"),
        P(),
    )
    return jax.shard_map(local, mesh=mesh, in_specs=in_specs, out_specs=out_specs, check_vma=False)
```

```python
from functools import partial

import jax
import jax.numpy as jnp
import numpy as np
from jax import lax
from jax.experimental import pallas as pl
from jax.experimental.pallas import tpu as pltpu
from jax.sharding import PartitionSpec as P

HEADS = 16
HDIM = 80
WIN = 14
D = 1280
NT = 4
HL = HEADS // NT
CELLS = WIN * WIN
WR = 208
NW = 6
TS = 320
HALF = TS // 2
HP = 128
RELS = 2 * WIN - 1
EPS = 1e-06
SCALE = HDIM ** (-0.5)
bf = jnp.bfloat16
f32 = jnp.float32
MB = 1024 * 1024


def rel_constants():
    sel = np.zeros((512, 64), np.float32)
    mask = np.zeros((WR, 512), np.float32)
    spread = np.zeros((512, WR), np.float32)
    for a in range(WIN):
        for x in range(WIN):
            sel[a * WIN + x, a - x + WIN - 1] = 1
            sel[256 + a * WIN + x, 32 + a - x + WIN - 1] = 1
    for a in range(WIN):
        for b in range(WIN):
            row = a * WIN + b
            mask[row, a * WIN : a * WIN + WIN] = 1
            mask[row, 256 + b * WIN : 256 + b * WIN + WIN] = 1
    for a in range(WIN):
        for x in range(WIN):
            for y in range(WIN):
                spread[a * WIN + x, x * WIN + y] = 1
                spread[256 + a * WIN + y, x * WIN + y] = 1
    keys = np.where(np.arange(WR) < CELLS, 0.0, -1e30).astype(np.float32)[None]
    return sel, mask, spread, keys


def dot(a, b):
    return lax.dot_general(a, b, (((1,), (0,)), ((), ())), preferred_element_type=f32)


def dot_nt(a, b):
    return lax.dot_general(a, b, (((1,), (1,)), ((), ())), preferred_element_type=f32)


def dot_tn(a, b):
    return lax.dot_general(a, b, (((0,), (0,)), ((), ())), preferred_element_type=f32)


def params(mb=16):
    return pltpu.CompilerParams(vmem_limit_bytes=mb * MB)


def cost(flops, nbytes, trans=0):
    return pl.CostEstimate(flops=int(flops), bytes_accessed=int(nbytes), transcendentals=int(trans))


def sds(shape, dtype):
    return jax.ShapeDtypeStruct(shape, dtype)


def full(shape):
    return pl.BlockSpec(shape, lambda *g: (0,) * len(shape))


ANY = pl.BlockSpec(memory_space=pl.ANY)


def stats(x):
    mean = jnp.sum(x, axis=1, keepdims=True) * (1.0 / D)
    xc = x - mean
    var = jnp.sum(xc * xc, axis=1, keepdims=True) * (1.0 / D)
    inv = lax.rsqrt(var + EPS)
    return xc * inv, inv


def colsum(x):
    return jnp.sum(x, axis=0, keepdims=True)


def acc_out(ref, value):
    @pl.when(pl.program_id(0) == 0)
    def _():
        ref[...] = jnp.zeros_like(ref)

    ref[...] += value


RB = 160


def in_feature_order(me, t, refs, use):
    r0, r1, ra, rb, r3 = refs
    r2 = jnp.where(t < NT // 2, ra[0].astype(f32), rb[0].astype(f32))
    parts = (r0[0].astype(f32), r1[0].astype(f32), r2, r3[0].astype(f32))
    for k in range(NT):

        @pl.when(me == k)
        def _(k=k):
            use(jnp.concatenate([parts[(b - k) % NT] for b in range(NT)], axis=1))


def ln1_body(me_ref, r0, r1, ra, rb, r3, keep_ref, g_ref, b_ref, x_ref, e_ref, n_ref):
    me = me_ref[0]
    j = pl.program_id(0)

    def use(x):
        n, _ = stats(x)
        e_ref[0] = (keep_ref[0] * (n * g_ref[...] + b_ref[...])).astype(bf)
        n_ref[0] = (keep_ref[0] * n).astype(bf)

        @pl.when(j == 0)
        def _():
            x_ref[...] = x.astype(bf)

    in_feature_order(me, block_of(me, j), (r0, r1, ra, rb, r3), use)


def cot_body(me_ref, r0, r1, ra, rb, r3, keep_ref, c_ref, gb_ref, fb_ref):
    me = me_ref[0]
    j = pl.program_id(0)

    @pl.when((j == 0) & (pl.program_id(1) == 0))
    def _():
        fb_ref[...] = jnp.zeros_like(fb_ref)

    def use(c):
        gb = keep_ref[0] * c
        gb_ref[0] = gb.astype(bf)

        @pl.when(j == 0)
        def _():
            c_ref[...] = c.astype(bf)
            fb_ref[...] += colsum(gb)

    in_feature_order(me, block_of(me, j), (r0, r1, ra, rb, r3), use)


def raw_specs():
    steps = TS // RB
    blk = pl.BlockSpec((1, RB, TS), lambda j, i, m: (block_of(m[0], j), i, 0))
    lo = pl.BlockSpec((1, RB, TS), lambda j, i, m: (jnp.minimum(block_of(m[0], j), 1), i, 0))
    hi = pl.BlockSpec((1, RB, TS), lambda j, i, m: (jnp.maximum(block_of(m[0], j) - 2, 0), i, 0))
    keep = pl.BlockSpec((1, RB, 1), lambda j, i, m: (block_of(m[0], j), i, 0))
    mine = pl.BlockSpec((RB, D), lambda j, i, m: (jnp.minimum(j * steps + i, steps - 1), 0))
    vec = pl.BlockSpec((1, D), lambda j, i, m: (0, 0))
    return (NT, steps), [blk, blk, lo, hi, blk, keep], mine, vec


def ln1_call(me, parts, keep4, g, b):
    grid, ins, mine, vec = raw_specs()
    return pl.pallas_call(
        ln1_body,
        grid_spec=pltpu.PrefetchScalarGridSpec(
            num_scalar_prefetch=1,
            grid=grid,
            in_specs=ins + [vec, vec],
            out_specs=[mine] + [pl.BlockSpec((1, RB, D), lambda j, i, m: (block_of(m[0], j), i, 0))] * 2,
        ),
        out_shape=[sds((TS, D), bf), sds((NT, TS, D), bf), sds((NT, TS, D), bf)],
        compiler_params=params(),
        cost_estimate=cost(80 * TS * D, 20 * TS * D),
        name="ln1",
    )(me, *parts, keep4, g, b)


def cot_call(me, parts, keep4):
    grid, ins, mine, vec = raw_specs()
    return pl.pallas_call(
        cot_body,
        grid_spec=pltpu.PrefetchScalarGridSpec(
            num_scalar_prefetch=1,
            grid=grid,
            in_specs=ins,
            out_specs=[mine, pl.BlockSpec((1, RB, D), lambda j, i, m: (j, i, 0)), vec],
        ),
        out_shape=[sds((TS, D), bf), sds((NT, TS, D), bf), sds((1, D), f32)],
        compiler_params=params(),
        cost_estimate=cost(80 * TS * D, 20 * TS * D),
        name="cot",
    )(me, *parts, keep4)


def ln2_body(r0, c1, c3, x, keep, pb, g, b, h_ref, e_ref):
    s = r0[...] + c1[...].astype(f32) + c3[...].astype(f32)
    h = x[...].astype(f32) + keep[...] * (s + pb[...])
    h_ref[...] = h
    n, _ = stats(h)
    e_ref[...] = (n * g[...] + b[...]).astype(bf)


def ln2_call(r0, c1, c3, x, keep, pb, g, b):
    row = pl.BlockSpec((RB, D), lambda i: (i, 0))
    kp = pl.BlockSpec((RB, 1), lambda i: (i, 0))
    return pl.pallas_call(
        ln2_body,
        grid=(TS // RB,),
        in_specs=[row, row, row, row, kp] + [full((1, D))] * 3,
        out_specs=[row, row],
        out_shape=[sds((TS, D), f32), sds((TS, D), bf)],
        compiler_params=params(),
        cost_estimate=cost(20 * TS * D, 16 * TS * D),
        name="ln2",
    )(r0, c1, c3, x, keep, pb, g, b)


def norm_back(w, n, inv):
    m1 = jnp.sum(w, axis=1, keepdims=True) * (1.0 / D)
    m2 = jnp.sum(w * n, axis=1, keepdims=True) * (1.0 / D)
    return inv * (w - m1 - n * m2)


def ln2b_body(r0, c1, c3, h, c, keep, g, gh_ref, gp_ref, gg_ref, gb_ref, pb_ref):
    gn = r0[...] + c1[...].astype(f32) + c3[...].astype(f32)
    n, inv = stats(h[...])
    gh = c[...].astype(f32) + norm_back(gn * g[...], n, inv)
    gh_ref[...] = gh
    kg = keep[...] * gh
    gp_ref[...] = kg.astype(bf)
    acc_out(gg_ref, colsum(gn * n))
    acc_out(gb_ref, colsum(gn))
    acc_out(pb_ref, colsum(kg))


def ln2b_call(r0, c1, c3, h, c, keep, g):
    row = pl.BlockSpec((RB, D), lambda i: (i, 0))
    kp = pl.BlockSpec((RB, 1), lambda i: (i, 0))
    return pl.pallas_call(
        ln2b_body,
        grid=(TS // RB,),
        in_specs=[row, row, row, row, row, kp, full((1, D))],
        out_specs=[row, row] + [full((1, D))] * 3,
        out_shape=[sds((TS, D), f32), sds((TS, D), bf)] + [sds((1, D), f32)] * 3,
        compiler_params=params(),
        cost_estimate=cost(30 * TS * D, 20 * TS * D),
        name="ln2b",
    )(r0, c1, c3, h, c, keep, g)


def result_body(r0, c1, c3, h, keep, fb, o_ref):
    s = r0[...] + c1[...].astype(f32) + c3[...].astype(f32)
    o_ref[...] = (h[...] + keep[...] * (s + fb[...])).astype(bf)


def result_call(r0, c1, c3, h, keep, fb):
    row = pl.BlockSpec((RB, D), lambda i: (i, 0))
    kp = pl.BlockSpec((RB, 1), lambda i: (i, 0))
    return pl.pallas_call(
        result_body,
        grid=(TS // RB,),
        in_specs=[row, row, row, row, kp, full((1, D))],
        out_specs=row,
        out_shape=sds((TS, D), bf),
        compiler_params=params(60),
        cost_estimate=cost(8 * TS * D, 14 * TS * D),
        name="result",
    )(r0, c1, c3, h, keep, fb)


def ln1b_body(r0, c1, c3, x, gh, keep, g, res, o_ref):
    keep = keep[...]
    gn = keep * (r0[...] + c1[...].astype(f32) + c3[...].astype(f32))
    n, inv = stats(x[...].astype(f32))
    gt = (gh[...] + norm_back(gn * g[...], n, inv)).astype(bf)
    for b in range(NT):
        o_ref[b, 0] = gt[:, b * TS : (b + 1) * TS]
        o_ref[b, 1] = res[:, b * TS : (b + 1) * TS]


def ln1b_call(r0, c1, c3, x, gh, keep, g, res):
    rb = 80
    row = pl.BlockSpec((rb, D), lambda i: (i, 0))
    kp = pl.BlockSpec((rb, 1), lambda i: (i, 0))
    vec = full((1, D))
    return pl.pallas_call(
        ln1b_body,
        grid=(TS // rb,),
        in_specs=[row, row, row, row, row, kp, vec, row],
        out_specs=pl.BlockSpec((NT, 2, rb, TS), lambda i: (0, 0, i, 0)),
        out_shape=sds((NT, 2, TS, TS), bf),
        compiler_params=params(60),
        cost_estimate=cost(30 * TS * D, 24 * TS * D),
        name="ln1b",
    )(r0, c1, c3, x, gh, keep, g, res)


def place_body(x, gt_ref, res_ref, gt_s, res_s):
    for t in range(NT):
        gt_s[t * TS : (t + 1) * TS] = x[t, 0].astype(f32)
        res_s[t * TS : (t + 1) * TS] = x[t, 1].astype(f32)
    for n in range(NW * WIN):
        w, a = n // WIN, n % WIN
        rows = slice(w * WR + a * WIN, w * WR + a * WIN + WIN)
        gt_ref[n] = gt_s[rows]
        res_ref[n] = res_s[rows].astype(bf)


def place_call(x):
    n = NW * WIN
    return pl.pallas_call(
        place_body,
        grid=(1,),
        in_specs=[full((NT, 2, TS, TS))],
        out_specs=[full((n, WIN, TS))] * 2,
        scratch_shapes=[pltpu.VMEM((NT * TS, TS), f32)] * 2,
        out_shape=[sds((n, WIN, TS), f32), sds((n, WIN, TS), bf)],
        compiler_params=params(60),
        cost_estimate=cost(4 * TS * TS, 40 * TS * TS),
        name="place",
    )(x)


def turn(v):
    return v.reshape(2, 3, WIN, WIN, TS).transpose(0, 2, 1, 3, 4).reshape(2, WIN, 3 * WIN, TS)


def pad_body(w_ref, q_ref, p_ref):
    rows = w_ref.shape[0]
    w = w_ref[...]
    zero = jnp.zeros((rows, HP - HDIM), bf)
    for h in range(3 * HL):
        q_ref[:, h * HP : (h + 1) * HP] = jnp.concatenate([w[:, h * HDIM : (h + 1) * HDIM], zero], axis=1)
    for h in range(HL):
        s = 3 * HL + h
        p_ref[:, h * HP : (h + 1) * HP] = jnp.concatenate([w[:, s * HDIM : (s + 1) * HDIM], zero], axis=1)


def pad_call(g1):
    rb = 160
    return pl.pallas_call(
        pad_body,
        grid=(D // rb,),
        in_specs=[pl.BlockSpec((rb, D), lambda i: (i, 0))],
        out_specs=[
            pl.BlockSpec((rb, 3 * HL * HP), lambda i: (i, 0)),
            pl.BlockSpec((rb, HL * HP), lambda i: (i, 0)),
        ],
        out_shape=[sds((D, 3 * HL * HP), bf), sds((D, HL * HP), bf)],
        compiler_params=params(),
        cost_estimate=cost(D * 2048, 2 * D * (1280 + 2048)),
        name="padw",
    )(g1)


def block_of(me, j):
    return lax.rem(me + j, NT)


def qkv_body(x_ref, w_ref, b_ref, o_ref):
    o_ref[...] = (dot(x_ref[...], w_ref[...]) + b_ref[...]).astype(bf)


def qkv_call(x, w, bias):
    n = w.shape[1]
    tn = 512
    rows = x.shape[0]
    return pl.pallas_call(
        qkv_body,
        grid=(n // tn,),
        in_specs=[
            full((rows, D)),
            pl.BlockSpec((D, tn), lambda i: (0, i)),
            pl.BlockSpec((1, tn), lambda i: (0, i)),
        ],
        out_specs=pl.BlockSpec((rows, tn), lambda i: (0, i)),
        out_shape=sds((rows, n), bf),
        compiler_params=params(24),
        cost_estimate=cost(2 * rows * D * n, 2 * (rows * D + D * n + rows * n)),
        name="qkv",
    )(x, w, bias)


def gatt_body(*refs):
    count = len(refs) - 4
    w_ref, o_ref = refs[1 + count], refs[-1]
    for t in range(count):

        @pl.when(pl.program_id(0) == t)
        def _(t=t):
            o_ref[0] = dot(refs[1 + t][...], w_ref[...]).astype(bf)


def gatt_call(me, which, xs, w, into):
    n = w.shape[1]
    k = len(which)
    first, step = which[0], which[-1] - which[0]
    return pl.pallas_call(
        gatt_body,
        grid_spec=pltpu.PrefetchScalarGridSpec(
            num_scalar_prefetch=1,
            grid=(k,),
            in_specs=[pl.BlockSpec((TS, D), lambda t, m: (0, 0))] * k
            + [pl.BlockSpec((D, n), lambda t, m: (0, 0)), ANY],
            out_specs=pl.BlockSpec((1, TS, n), lambda t, m: (block_of(m[0], first + step * t), 0, 0)),
        ),
        out_shape=sds((NT, TS, n), bf),
        input_output_aliases={2 + k: 0},
        compiler_params=params(),
        cost_estimate=cost(2 * k * TS * D * n, 2 * (k * TS * D + D * n + k * TS * n)),
        name="gatt",
    )(me, *xs, w, into)


def gatt2_body(me_ref, a_ref, b_ref, w_ref, z_ref, o_ref, p_ref):
    p_ref[:HALF] = a_ref[...]
    p_ref[HALF:] = b_ref[...]
    o_ref[0] = dot(p_ref[...], w_ref[...]).astype(bf)


def gatt2_call(me, halves, w, into):
    n = w.shape[1]
    half = pl.BlockSpec((HALF, D), lambda i, m: (0, 0))
    return pl.pallas_call(
        gatt2_body,
        grid_spec=pltpu.PrefetchScalarGridSpec(
            num_scalar_prefetch=1,
            grid=(1,),
            in_specs=[half, half, pl.BlockSpec((D, n), lambda i, m: (0, 0)), ANY],
            out_specs=[
                pl.BlockSpec((1, TS, n), lambda i, m: (block_of(m[0], 2), 0, 0)),
                pl.BlockSpec((TS, D), lambda i, m: (0, 0)),
            ],
        ),
        out_shape=[sds((NT, TS, n), bf), sds((TS, D), bf)],
        input_output_aliases={4: 0},
        compiler_params=params(),
        cost_estimate=cost(2 * TS * D * n, 2 * (2 * TS * D + D * n + TS * n)),
        name="gatt",
    )(me, *halves, w, into)


def attn_body(qkv_ref, tab_ref, sel_ref, mask_ref, sp_ref, km_ref, z_ref, o_ref, p_ref, t_ref):
    @pl.when(pl.program_id(0) == 0)
    def _():
        t_ref[...] = dot(sel_ref[...], tab_ref[...]).astype(bf)

    qs = [qkv_ref[:, h * HP : (h + 1) * HP] for h in range(HL)]
    along = dot_nt(jnp.concatenate(qs, axis=0), t_ref[...])
    mask = mask_ref[...].astype(f32)
    along = jnp.concatenate([(along[h * WR : (h + 1) * WR] * mask).astype(bf) for h in range(HL)], axis=0)
    bias = dot(along, sp_ref[...])
    for h in range(HL):
        k = qkv_ref[:, (HL + h) * HP : (HL + h + 1) * HP]
        v = qkv_ref[:, (2 * HL + h) * HP : (2 * HL + h + 1) * HP]
        s = dot_nt(qs[h], k) * SCALE + bias[h * WR : (h + 1) * WR] + km_ref[...]
        top = jnp.max(s, axis=1, keepdims=True)
        e = jnp.exp(s - top)
        p = (e * (1.0 / jnp.sum(e, axis=1, keepdims=True))).astype(bf)
        p_ref[0, h] = p
        o_ref[:, h * HP : (h + 1) * HP] = dot(p, v).astype(bf)


def attn_call(qkv, tab, sel, mask, spread, keys, into):
    n = 3 * HL * HP
    return pl.pallas_call(
        attn_body,
        grid=(NW,),
        in_specs=[
            pl.BlockSpec((WR, n), lambda i: (i, 0)),
            full((64, HP)),
            full((512, 64)),
            full((WR, 512)),
            full((512, WR)),
            full((1, WR)),
            ANY,
        ],
        out_specs=[
            pl.BlockSpec((WR, HL * HP), lambda i: (i, 0)),
            pl.BlockSpec((1, HL, WR, WR), lambda i: (i, 0, 0, 0)),
        ],
        out_shape=[sds((NT * TS, HL * HP), bf), sds((NW, HL, WR, WR), bf)],
        scratch_shapes=[pltpu.VMEM((512, HP), bf)],
        input_output_aliases={6: 0},
        compiler_params=params(),
        cost_estimate=cost(24 * 6 * 2 * WR * WR * 256, 8e6, 24 * WR * 256),
        name="attn",
    )(qkv, tab, sel, mask, spread, keys, into)


def attnb_body(qkv_ref, p_ref, ga_ref, tab_ref, sel_ref, mask_ref, sp_ref, z_ref, o_ref, rel_ref, bias_ref, t_ref):
    @pl.when(pl.program_id(0) == 0)
    def _():
        t_ref[...] = dot(sel_ref[...], tab_ref[...]).astype(bf)
        rel_ref[...] = jnp.zeros_like(rel_ref)
        bias_ref[...] = jnp.zeros_like(bias_ref)

    table = t_ref[...]
    mask = mask_ref[...].astype(f32)
    qs, all_ds = [], []
    for h in range(HL):
        cq = slice(h * HP, (h + 1) * HP)
        cv = slice((2 * HL + h) * HP, (2 * HL + h + 1) * HP)
        ga = ga_ref[:, cq]
        p = p_ref[0, h]
        pf = p.astype(f32)
        gs = dot_nt(ga, qkv_ref[:, cv])
        delta = jnp.sum(pf * gs, axis=1, keepdims=True)
        all_ds.append((pf * (gs - delta)).astype(bf))
        qs.append(qkv_ref[:, cq])
        gv = dot_tn(p, ga).astype(bf)
        o_ref[:, cv] = gv
        bias_ref[:, cv] += colsum(gv.astype(f32))
    sums = dot_nt(jnp.concatenate(all_ds, axis=0), sp_ref[...])
    sums = jnp.concatenate([(sums[h * WR : (h + 1) * WR] * mask).astype(bf) for h in range(HL)], axis=0)
    gq_rel = dot(sums, table)
    rel_ref[...] += dot_tn(sums, jnp.concatenate(qs, axis=0))
    for h in range(HL):
        cq = slice(h * HP, (h + 1) * HP)
        ck = slice((HL + h) * HP, (HL + h + 1) * HP)
        ds = all_ds[h]
        o_ref[:, ck] = (dot_tn(ds, qs[h]) * SCALE).astype(bf)
        gq = (dot(ds, qkv_ref[:, ck]) * SCALE + gq_rel[h * WR : (h + 1) * WR]).astype(bf)
        o_ref[:, cq] = gq
        bias_ref[:, cq] += colsum(gq.astype(f32))


def attnb_call(qkv, p, ga, tab, sel, mask, spread, into):
    n = 3 * HL * HP
    return pl.pallas_call(
        attnb_body,
        grid=(NW,),
        in_specs=[
            pl.BlockSpec((WR, n), lambda i: (i, 0)),
            pl.BlockSpec((1, HL, WR, WR), lambda i: (i, 0, 0, 0)),
            pl.BlockSpec((WR, HL * HP), lambda i: (i, 0)),
            full((64, HP)),
            full((512, 64)),
            full((WR, 512)),
            full((512, WR)),
            ANY,
        ],
        out_specs=[pl.BlockSpec((WR, n), lambda i: (i, 0)), full((512, HP)), full((1, n))],
        out_shape=[sds((NT * TS, n), bf), sds((512, HP), f32), sds((1, n), f32)],
        scratch_shapes=[pltpu.VMEM((512, HP), bf)],
        input_output_aliases={7: 0},
        compiler_params=params(),
        cost_estimate=cost(24 * 10 * 2 * WR * WR * 256, 14e6),
        name="attnb",
    )(qkv, p, ga, tab, sel, mask, spread, into)


def partial_body(me_ref, a_ref, w_ref, *refs):
    w = w_ref[...]
    if len(refs) == 5:
        n_ref, (r0, r1, r2a, r2b, r3) = None, refs
    else:
        n_ref, keep_ref, r0, r1, r2a, r2b, r3, gg_ref, gb_ref = refs
    gain = bias = 0.0
    for j, ref in ((2, None), (1, r1), (3, r3), (0, r0)):
        t = block_of(me_ref[0], j)
        r = dot_nt(a_ref[t], w)
        if n_ref is not None:
            gain = gain + colsum(r * n_ref[t].astype(f32))
            bias = bias + colsum(r * keep_ref[t])
        if ref is None:
            r2a[...] = r[:HALF].astype(bf)
            r2b[...] = r[HALF:].astype(bf)
        else:
            ref[...] = r.astype(ref.dtype)
    if n_ref is not None:
        gg_ref[...] = gain
        gb_ref[...] = bias


def partial_call(me, a, w, name, norm=()):
    k = a.shape[2]
    tn = 256
    whole = pl.BlockSpec((TS, tn), lambda i, m: (0, i))
    half = pl.BlockSpec((HALF, tn), lambda i, m: (0, i))
    ins = [pl.BlockSpec((NT, TS, tn), lambda i, m: (0, 0, i)), pl.BlockSpec((NT, TS, 1), lambda i, m: (0, 0, 0))]
    outs = [whole, whole, half, half, whole]
    shapes = [sds((TS, D), f32), sds((TS, D), bf), sds((HALF, D), bf), sds((HALF, D), bf), sds((TS, D), bf)]
    if norm:
        outs += [pl.BlockSpec((1, tn), lambda i, m: (0, i))] * 2
        shapes += [sds((1, D), f32)] * 2
    return pl.pallas_call(
        partial_body,
        grid_spec=pltpu.PrefetchScalarGridSpec(
            num_scalar_prefetch=1,
            grid=(D // tn,),
            in_specs=[
                pl.BlockSpec((NT, TS, k), lambda i, m: (0, 0, 0)),
                pl.BlockSpec((tn, k), lambda i, m: (i, 0)),
            ]
            + ins[: len(norm)],
            out_specs=outs,
        ),
        out_shape=shapes,
        compiler_params=params(24),
        cost_estimate=cost(2 * NT * TS * D * k, 2 * (NT * TS * k + D * k + 9 * TS * D)),
        name=name,
    )(me, a, w, *norm)


def merge_body(r1, a, r3, b, s1, s3):
    s1[...] = (r1[...].astype(f32) + a[...].astype(f32)).astype(bf)
    s3[...] = (r3[...].astype(f32) + b[...].astype(f32)).astype(bf)


def merge_call(r1, a, r3, b, mb=16):
    one = pl.BlockSpec((HALF, D), lambda i: (0, 0))
    two = pl.BlockSpec((HALF, D), lambda i: (1, 0))
    return pl.pallas_call(
        merge_body,
        grid=(1,),
        in_specs=[one, one, two, one],
        out_specs=[one, two],
        out_shape=[sds((TS, D), bf)] * 2,
        input_output_aliases={0: 0, 2: 1},
        compiler_params=params(mb),
        cost_estimate=cost(4 * HALF * D, 12 * HALF * D),
        name="merge",
    )(r1, a, r3, b)


def mlp_body(halved, k, *refs):
    ins = refs[: 2 if halved else k]
    gb_refs = refs[len(ins) : len(ins) + k]
    w1_ref, w2_ref, b1_ref = refs[len(ins) + k : len(ins) + k + 3]
    outs = refs[len(ins) + k + 3 : -4]
    z_s, gb_s, br_s, gn_s = refs[-4:]
    step = pl.program_id(0)

    @pl.when(step == 0)
    def _():
        br_s[...] = jnp.zeros_like(br_s)
        gn_s[...] = jnp.zeros_like(gn_s)
        rows = k * TS // len(ins)
        for t, ref in enumerate(ins):
            z_s[t * rows : (t + 1) * rows] = ref[...]
        for t, ref in enumerate(gb_refs):
            gb_s[t * TS : (t + 1) * TS] = ref[0]

    w1 = w1_ref[...]
    w2 = w2_ref[...]
    pre = dot(z_s[...], w1) + b1_ref[...]
    ga = dot(gb_s[...], w2)
    cdf = 0.5 + 0.5 * lax.erf(pre * 0.7071067811865476)
    act = (pre * cdf).astype(bf)
    slope = cdf + pre * (0.3989422804014327 * jnp.exp(-0.5 * pre * pre))
    gp = (ga * slope).astype(bf)
    for t in range(k):
        rows = slice(t * TS, (t + 1) * TS)
        outs[3 * t][...] = act[rows]
        outs[3 * t + 1][...] = gp[rows]
        outs[3 * t + 2][...] = colsum(gp[rows].astype(f32))
    br_s[...] += dot_nt(act, w2)
    gn_s[...] += dot_nt(gp, w1)

    @pl.when(step == pl.num_programs(0) - 1)
    def _():
        rest = outs[3 * k :]
        for total, refs_out in ((br_s, rest[0::2]), (gn_s, rest[1::2])):
            at = 0
            for ref in refs_out:
                if at < total.shape[0]:
                    ref[...] = total[at : at + ref.shape[0]].astype(ref.dtype)
                    at += ref.shape[0]
        if halved:
            rest[4][...] = z_s[...]


def mlp_call(which, zs, gb, w, b1, kind):
    halved = which == (2,)
    k = len(which)
    tf = 256
    nf = D // tf
    col = pl.BlockSpec((TS, tf), lambda i: (0, i))
    bias = pl.BlockSpec((1, tf), lambda i: (0, i))
    half = full((HALF, D))
    block = full((TS, D))
    outs = [col, col, bias] * k
    shapes = [sds((TS, D), bf), sds((TS, D), bf), sds((1, D), f32)] * k
    if halved:
        outs += [half] * 4 + [block]
        shapes += [sds((HALF, D), bf)] * 4 + [sds((TS, D), bf)]
    else:
        outs += [block] * (2 * k)
        shapes += [sds((TS, D), kind)] * (2 * k)
    return pl.pallas_call(
        partial(mlp_body, halved, k),
        grid=(nf,),
        in_specs=[half if halved else block] * len(zs)
        + [pl.BlockSpec((1, TS, D), lambda i, j=j: (j, 0, 0)) for j in which]
        + [
            pl.BlockSpec((D, tf), lambda i: (0, i)),
            pl.BlockSpec((D, tf), lambda i: (0, i + nf)),
            bias,
        ],
        out_specs=outs,
        out_shape=shapes,
        scratch_shapes=[pltpu.VMEM((k * TS, D), bf)] * 2 + [pltpu.VMEM((k * TS, D), f32)] * 2,
        compiler_params=params(32),
        cost_estimate=cost(k * 8 * TS * D * D, 4 * D * D + k * 12 * TS * D, k * 2 * TS * D),
        name="mlp",
    )(*zs, *[gb] * k, w, w, b1)


NG = 2 * D


def tokgrad_body(*refs):
    o_ref = refs[-1]
    lhs, rhs = refs[:4], refs[4:8]
    total = None
    for j in range(NT):
        left = lhs[j][0] if len(lhs[j].shape) == 3 else lhs[j][...]
        part = dot_tn(left, rhs[j][...])
        total = part if total is None else total + part
    o_ref[...] = total.astype(bf)


def tokgrad_call(lhs, rhs, into, at):
    td = 256
    if len(lhs) == 1:
        left = [pl.BlockSpec((1, TS, td), lambda i, j=j: (j, 0, i)) for j in range(NT)]
        lhs = list(lhs) * NT
    else:
        left = [pl.BlockSpec((TS, td), lambda i: (0, i))] * NT
    return pl.pallas_call(
        tokgrad_body,
        grid=(D // td,),
        in_specs=left + [full((TS, D))] * NT + [ANY] * (into is not None),
        out_specs=pl.BlockSpec((td, D), lambda i: (i, at)),
        out_shape=sds((D, NG), bf),
        input_output_aliases={} if into is None else {2 * NT: 0},
        compiler_params=params(24),
        cost_estimate=cost(8 * TS * D * D, 2 * (8 * TS * D + D * D)),
        name="fcgrad",
    )(*lhs, *rhs, *(() if into is None else (into,)))


def narrow(x, heads):
    return jnp.concatenate([x[:, h * HP : h * HP + HDIM] for h in range(heads)], axis=1)


def qpgrad_body(me_ref, e_ref, dq_ref, p0, p1, p2, p3, a_ref, o_ref):
    o_ref[:, : 3 * HL * HDIM] = narrow(dot_tn(e_ref[...], dq_ref[...]), 3 * HL).astype(bf)
    total = None
    for j, p in enumerate((p0, p1, p2, p3)):
        part = dot_tn(p[...], a_ref[block_of(me_ref[0], j)])
        total = part if total is None else total + part
    o_ref[:, 3 * HL * HDIM :] = narrow(total, HL).astype(bf)


def qpgrad_call(me, e, dqkv, p, att4):
    td = 256
    rows, n = dqkv.shape
    k = att4.shape[2]
    return pl.pallas_call(
        qpgrad_body,
        grid_spec=pltpu.PrefetchScalarGridSpec(
            num_scalar_prefetch=1,
            grid=(D // td,),
            in_specs=[
                pl.BlockSpec((rows, td), lambda i, m: (0, i)),
                pl.BlockSpec((rows, n), lambda i, m: (0, 0)),
            ]
            + [pl.BlockSpec((TS, td), lambda i, m: (0, i))] * 4
            + [pl.BlockSpec((NT, TS, k), lambda i, m: (0, 0, 0))],
            out_specs=pl.BlockSpec((td, D), lambda i, m: (i, 0)),
        ),
        out_shape=sds((D, D), bf),
        compiler_params=params(24),
        cost_estimate=cost(2 * rows * D * (n + k), 2 * (2 * rows * D + rows * (n + k) + D * D)),
        name="qpgrad",
    )(me, e, dqkv, *p, att4)


UP = [(i, (i + 1) % NT) for i in range(NT)]
DOWN = [(i, (i - 1) % NT) for i in range(NT)]


def up(v):
    return lax.ppermute(v, "tp", UP)


def down(v):
    return lax.ppermute(v, "tp", DOWN)


def after(v, *deps):
    return lax.optimization_barrier((v, deps))[0]


def ring_gather(own, first=None, between=None):
    b3 = up(own)
    b1 = down(own)
    if first is not None:
        b3, b1, first = lax.optimization_barrier((b3, b1, first))
    half = own.shape[0] // 2
    u, d = up(b3[:half]), down(b1[half:])
    if between is not None:
        first = between(b1, b3, first)
        u, d, first = lax.optimization_barrier((u, d, first))
    return (own, b1, u, d, b3), first


def ring_scatter(r1, r2a, r2b, r3, first=None, mb=16):
    a = up(r2a)
    b = down(r2b)
    if first is not None:
        a, b, first = lax.optimization_barrier((a, b, first))
    s1, s3 = merge_call(r1, a, r3, b, mb)
    return (s3, s1), first


def ring_finish(sums):
    return down(sums[0]), up(sums[1])


def shard_place():
    s = lax.axis_index("shard")
    return s // 4, (s // 2) % 2, s % 2


def shard_move(v, f):
    return lax.ppermute(v, "shard", [(i, f(i)) for i in range(16)])


def pick(v, i, ax):
    return lax.dynamic_index_in_dim(v, i, ax, keepdims=False)


def add_low(p, q):
    return (p.astype(f32) + q.astype(f32)).astype(bf)


def over_shard_1(v):
    n = v.shape[1]
    y, zl, core = shard_place()
    v = v.reshape(4, 2, 2, 80, n)
    v = add_low(pick(v, core, 2), shard_move(pick(v, 1 - core, 2), lambda i: i ^ 1))
    w = [pick(v, (y + j) % 4, 0) for j in range(4)]
    a = shard_move(w[2][0], lambda i: (i + 4) % 16)
    b = shard_move(w[2][1], lambda i: (i + 12) % 16)
    return w[0], jnp.stack([add_low(w[1][0], a), w[1][1]]), jnp.stack([w[3][0], add_low(w[3][1], b)])


def over_shard_2(parts):
    w0, s1, s3 = parts
    return w0, shard_move(s3, lambda i: (i + 12) % 16), shard_move(s1, lambda i: (i + 4) % 16)


def over_shard_3(parts):
    w0, c1, c3 = parts
    y, zl, core = shard_place()
    v = (w0.astype(f32) + c1.astype(f32) + c3.astype(f32)).astype(bf)
    return pick(v, zl, 0), shard_move(pick(v, 1 - zl, 0), lambda i: i ^ 2)


def over_ctx(v):
    return v.astype(f32) + lax.ppermute(v, "ctx", [(0, 1), (1, 0)]).astype(f32)


def small_pack(parts):
    out = []
    for part in parts:
        v = jnp.concatenate([a.ravel() for a in part])
        out.append(jnp.pad(v, (0, -v.size % 1024)).reshape(-1, 128))
    return jnp.concatenate(out, axis=0).astype(bf)


def small_finish(everyone, world, group):
    both = jnp.sum(everyone.astype(f32), axis=0)
    rows = -(-sum(a.size for a in world) // 1024) * 8
    w, g = both[:rows], both[rows:]
    w = w + lax.ppermute(w, "tp", [(i, i ^ 1) for i in range(NT)])
    w = w + lax.ppermute(w, "tp", [(i, i ^ 3) for i in range(NT)])
    out = []
    for part, flat in ((world, w.ravel()), (group, g.ravel())):
        at = 0
        for a in part:
            out.append(flat[at : at + a.size].reshape(a.shape))
            at += a.size
    return out


def from_everyone(array, axis):
    size = lax.axis_size(axis)
    return lax.all_to_all(jnp.broadcast_to(array[None], (size, *array.shape)), axis, 0, 0, tiled=True)


def windows(grid):
    n = grid.shape[-1]
    w = grid.reshape(2, WIN, 3, WIN, n).transpose(0, 2, 1, 3, 4).reshape(NW, CELLS, n)
    w = jnp.pad(w, ((0, 0), (0, WR - CELLS), (0, 0))).reshape(NW * WR, n)
    return jnp.pad(w, ((0, NT * TS - NW * WR), (0, 0))).reshape(NT, TS, n)


def local(
    tokens,
    valid_mask,
    ln1_gain,
    ln1_bias,
    qkv_weight,
    qkv_bias,
    rel_rows,
    rel_cols,
    proj_weight,
    proj_bias,
    ln2_gain,
    ln2_bias,
    fc1_weight,
    fc1_bias,
    fc2_weight,
    fc2_bias,
    cotangent,
):
    tp_index = lax.axis_index("tp")
    me = tp_index.astype(jnp.int32).reshape(1)
    sel, mask, spread, keys = rel_constants()
    sel = jnp.asarray(sel, bf)
    mask = jnp.asarray(mask, bf)
    spread = jnp.asarray(spread, bf)
    keys = jnp.asarray(keys, f32)
    row = lambda v: v.reshape(1, -1)

    own1 = jnp.concatenate([jnp.moveaxis(qkv_weight, 1, 0).reshape(80, 960), proj_weight.T], axis=1)
    own2 = jnp.concatenate([fc1_weight, fc2_weight.T], axis=1)
    all1 = lax.all_gather(own1, "shard", axis=0, tiled=True)
    all2 = lax.all_gather(own2, "shard", axis=0, tiled=True)
    bias_q = jnp.pad(qkv_bias.reshape(2, HL, HDIM), ((0, 0), (0, 0), (0, HP - HDIM))).reshape(2, HL * HP)
    bias_p = row(jnp.concatenate([bias_q[0], jnp.zeros((HL * HP,), f32), bias_q[1]]))
    tab = jnp.zeros((64, HP), bf).at[:RELS, :HDIM].set(rel_rows).at[32 : 32 + RELS, :HDIM].set(rel_cols)

    keep4 = windows(valid_mask.astype(f32)[..., None])
    keep = lax.dynamic_index_in_dim(keep4, tp_index, 0, keepdims=False)
    toks, (qkvp, projp) = ring_gather(windows(tokens), None, lambda b1, b3, _: pad_call(all1))
    x, e4, n4 = ln1_call(me, toks, keep4, row(ln1_gain), row(ln1_bias))
    ents = e4.reshape(NT * TS, D)
    cots, flat = ring_gather(after(windows(cotangent), toks[2], toks[3]), qkv_call(ents, qkvp, bias_p))
    att, probs = attn_call(flat, tab, sel, mask, spread, keys, jnp.zeros((NT * TS, HL * HP), bf))
    att, *cots = lax.optimization_barrier((att, *cots))
    att4 = att.reshape(NT, TS, HL * HP)
    r0, *rest = partial_call(me, att4, projp, "proj")
    sums, _ = ring_scatter(*rest, None, 60)
    c, gb, sum_fc2_bias = cot_call(me, cots, keep4)
    (c1, c3), gb = lax.optimization_barrier((ring_finish(sums), gb))
    h, z = ln2_call(r0, c1, c3, x, keep, row(proj_bias), row(ln2_gain), row(ln2_bias))

    b1row = row(fc1_bias)
    mlp = lambda which, zz, kind: mlp_call(which, zz, gb, all2, b1row, kind)
    zs, (m0, m13) = ring_gather(
        z, mlp((0,), (z,), f32), lambda b1, b3, first: (first, mlp((1, 3), (b1, b3), bf))
    )
    act0, gpre0, fb0, br0, gn0 = m0
    act1, gpre1, fb1, act3, gpre3, fb3, br1, gn1, br3, gn3 = m13
    act2, gpre2, fb2, br2a, gn2a, br2b, gn2b, z2 = mlp((2,), (zs[2], zs[3]), bf)
    gpres = (gpre0, gpre1, gpre2, gpre3)
    sum_fc1_bias = fb0 + fb1 + fb2 + fb3
    sums, grads = ring_scatter(gn1, gn2a, gn2b, gn3, tokgrad_call((gb,), (act0, act1, act2, act3), None, 1))
    grads = tokgrad_call((z, zs[1], z2, zs[4]), gpres, grads, 0)
    (c1, c3), grads = lax.optimization_barrier((ring_finish(sums), grads))
    own_fc = lax.psum_scatter(grads, "shard", scatter_dimension=0, tiled=True)
    gh, gproj, sum_ln2_gain, sum_ln2_bias, sum_proj_bias = ln2b_call(
        gn0, c1, c3, h, c, keep, row(ln2_gain)
    )
    ga = gatt_call(me, (0,), (gproj,), projp, jnp.zeros((NT, TS, HL * HP), bf))
    gps, ga = ring_gather(gproj, ga, lambda b1, b3, ga: gatt_call(me, (1, 3), (b1, b3), projp, ga))
    ga, gp2 = gatt2_call(me, gps[2:4], projp, ga)

    branch = after((br1, br2a, br2b, br3), gp2)
    dqkv, rel, sum_qkv_bias = attnb_call(
        flat,
        probs,
        ga.reshape(NT * TS, HL * HP),
        tab,
        sel,
        mask,
        spread,
        jnp.zeros((NT * TS, 3 * HL * HP), bf),
    )
    sums, dqkv = ring_scatter(*branch, dqkv)
    sums, dqkv = lax.optimization_barrier((sums, dqkv))
    f1, f3 = ring_finish(sums)
    r0, r1, r2a, r2b, r3, sum_ln1_gain, sum_ln1_bias = partial_call(
        me, dqkv.reshape(NT, TS, 3 * HL * HP), qkvp, "gnorm1", (n4, keep4)
    )
    gradq = qpgrad_call(me, ents, dqkv, (gproj, gps[1], gp2, gps[4]), att4)
    gradq, f1, f3 = lax.optimization_barrier((gradq, f1, f3))
    sums, gradq = ring_scatter(r1, r2a, r2b, r3, gradq, 60)
    c1, c3 = ring_finish(sums)
    parts = over_shard_1(after(gradq, sums))
    res = result_call(br0, f1, f3, h, keep, row(fc2_bias))
    small = after(
        (
            rel,
            sum_qkv_bias,
            sum_fc1_bias,
            sum_ln1_gain,
            sum_ln1_bias,
            sum_ln2_gain,
            sum_ln2_bias,
            sum_proj_bias,
            sum_fc2_bias,
        ),
        sums,
    )
    rels = jnp.dot(sel.astype(f32).T, small[0], precision=lax.Precision.HIGHEST)
    qb = small[1].reshape(3, HL, HP)[:, :, :HDIM]
    world = [*small[3:], rels[:RELS, :HDIM], rels[32 : 32 + RELS, :HDIM]]
    group = [qb[0], qb[2], small[2]]
    everyone = from_everyone(small_pack((world, group)), ("shard", "ctx"))
    parts, res = lax.optimization_barrier((parts, res))
    c1, c3, parts, everyone = lax.optimization_barrier((c1, c3, parts, everyone))
    parts = over_shard_2(parts)
    out = ln1b_call(r0, c1, c3, x, gh, keep, row(ln1_gain), res)
    out, parts, fc = lax.optimization_barrier((out, parts, over_ctx(own_fc)))
    blocks = lax.all_to_all(out, "tp", 0, 0, tiled=True)
    half, other = over_shard_3(parts)
    q = over_ctx(add_low(half, other))
    blocks, q = lax.optimization_barrier((blocks, q))
    g_ln1g, g_ln1b, g_ln2g, g_ln2b, g_pb, g_f2b, g_rr, g_rc, g_q, g_v, g_f1b = small_finish(
        after(everyone, blocks), world, group
    )
    token_grads, result = place_call(blocks)
    token_grads, result = turn(token_grads), turn(result)
    return (
        result,
        token_grads,
        g_ln1g.ravel(),
        g_ln1b.ravel(),
        jnp.moveaxis(q[:, : 3 * HL * HDIM].reshape(80, 3, 320), 0, 1),
        jnp.stack([g_q.ravel(), g_v.ravel()]),
        g_rr,
        g_rc,
        q[:, 3 * HL * HDIM :].T,
        g_pb.ravel(),
        g_ln2g.ravel(),
        g_ln2b.ravel(),
        fc[:, :D],
        g_f1b.ravel(),
        fc[:, D:].T,
        g_f2b.ravel(),
    )


def solution(mesh):
    cells = P("shard", "ctx", None, "tp")
    in_specs = (
        cells,
        P("shard", "ctx", None),
        P(),
        P(),
        P(None, "shard", "tp"),
        P(None, "tp"),
        P(),
        P(),
        P("tp", "shard"),
        P(),
        P(),
        P(),
        P("shard", "tp"),
        P("tp"),
        P("tp", "shard"),
        P(),
        cells,
    )
    out_specs = (
        cells,
        cells,
        P(),
        P(),
        P(None, "shard", "tp"),
        P(None, "tp"),
        P(),
        P(),
        P("tp", "shard"),
        P(),
        P(),
        P(),
        P("shard", "tp"),
        P("tp"),
        P("tp", "shard"),
        P(),
    )
    return jax.shard_map(local, mesh=mesh, in_specs=in_specs, out_specs=out_specs, check_vma=False)
```

```python
from functools import partial

import jax
import jax.numpy as jnp
import numpy as np
from jax import lax
from jax.experimental import pallas as pl
from jax.experimental.pallas import tpu as pltpu
from jax.sharding import PartitionSpec as P

HEADS = 16
HDIM = 80
WIN = 14
D = 1280
NT = 4
HL = HEADS // NT
CELLS = WIN * WIN
WR = 208
NW = 6
TS = 320
HALF = TS // 2
HP = 128
RELS = 2 * WIN - 1
EPS = 1e-06
SCALE = HDIM ** (-0.5)
bf = jnp.bfloat16
f32 = jnp.float32
MB = 1024 * 1024


def rel_constants():
    sel = np.zeros((512, 64), np.float32)
    mask = np.zeros((WR, 512), np.float32)
    spread = np.zeros((512, WR), np.float32)
    for a in range(WIN):
        for x in range(WIN):
            sel[a * WIN + x, a - x + WIN - 1] = 1
            sel[256 + a * WIN + x, 32 + a - x + WIN - 1] = 1
    for a in range(WIN):
        for b in range(WIN):
            row = a * WIN + b
            mask[row, a * WIN : a * WIN + WIN] = 1
            mask[row, 256 + b * WIN : 256 + b * WIN + WIN] = 1
    for a in range(WIN):
        for x in range(WIN):
            for y in range(WIN):
                spread[a * WIN + x, x * WIN + y] = 1
                spread[256 + a * WIN + y, x * WIN + y] = 1
    keys = np.where(np.arange(WR) < CELLS, 0.0, -1e30).astype(np.float32)[None]
    return sel, mask, spread, keys


def dot(a, b):
    return lax.dot_general(a, b, (((1,), (0,)), ((), ())), preferred_element_type=f32)


def dot_nt(a, b):
    return lax.dot_general(a, b, (((1,), (1,)), ((), ())), preferred_element_type=f32)


def dot_tn(a, b):
    return lax.dot_general(a, b, (((0,), (0,)), ((), ())), preferred_element_type=f32)


def params(mb=16):
    return pltpu.CompilerParams(vmem_limit_bytes=mb * MB)


def cost(flops, nbytes, trans=0):
    return pl.CostEstimate(flops=int(flops), bytes_accessed=int(nbytes), transcendentals=int(trans))


def sds(shape, dtype):
    return jax.ShapeDtypeStruct(shape, dtype)


def full(shape):
    return pl.BlockSpec(shape, lambda *g: (0,) * len(shape))


ANY = pl.BlockSpec(memory_space=pl.ANY)


def stats(x):
    mean = jnp.sum(x, axis=1, keepdims=True) * (1.0 / D)
    xc = x - mean
    var = jnp.sum(xc * xc, axis=1, keepdims=True) * (1.0 / D)
    inv = lax.rsqrt(var + EPS)
    return xc * inv, inv


def colsum(x):
    return jnp.sum(x, axis=0, keepdims=True)


def acc_out(ref, value):
    @pl.when(pl.program_id(0) == 0)
    def _():
        ref[...] = jnp.zeros_like(ref)

    ref[...] += value


RB = 160


def in_feature_order(me, t, refs, use):
    if len(refs) == 5:
        r0, r1, ra, rb, r3 = refs
        r2 = jnp.where(t < NT // 2, ra[0].astype(f32), rb[0].astype(f32))
    else:
        r0, r1, r2, r3 = refs
        r2 = r2[0].astype(f32)
    parts = (r0[0].astype(f32), r1[0].astype(f32), r2, r3[0].astype(f32))
    for k in range(NT):

        @pl.when(me == k)
        def _(k=k):
            use(jnp.concatenate([parts[(b - k) % NT] for b in range(NT)], axis=1))


def ln1_body(me_ref, r0, r1, ra, rb, r3, keep_ref, g_ref, b_ref, x_ref, e_ref, n_ref):
    me = me_ref[0]
    j = pl.program_id(0)

    def use(x):
        n, _ = stats(x)
        e_ref[0] = (keep_ref[0] * (n * g_ref[...] + b_ref[...])).astype(bf)
        n_ref[0] = (keep_ref[0] * n).astype(bf)

        @pl.when(j == 0)
        def _():
            x_ref[...] = x.astype(bf)

    in_feature_order(me, block_of(me, j), (r0, r1, ra, rb, r3), use)


def cot_body(me_ref, r0, r1, r2, r3, keep_ref, c_ref, gb_ref, fb_ref):
    me = me_ref[0]
    j = pl.program_id(0)

    @pl.when((j == 0) & (pl.program_id(1) == 0))
    def _():
        fb_ref[...] = jnp.zeros_like(fb_ref)

    def use(c):
        gb = keep_ref[0] * c
        gb_ref[0] = gb.astype(bf)

        @pl.when(j == 0)
        def _():
            c_ref[...] = c.astype(bf)
            fb_ref[...] += colsum(gb)

    in_feature_order(me, block_of(me, j), (r0, r1, r2, r3), use)


def raw_specs():
    steps = TS // RB
    blk = pl.BlockSpec((1, RB, TS), lambda j, i, m: (block_of(m[0], j), i, 0))
    lo = pl.BlockSpec((1, RB, TS), lambda j, i, m: (jnp.minimum(block_of(m[0], j), 1), i, 0))
    hi = pl.BlockSpec((1, RB, TS), lambda j, i, m: (jnp.maximum(block_of(m[0], j) - 2, 0), i, 0))
    keep = pl.BlockSpec((1, RB, 1), lambda j, i, m: (block_of(m[0], j), i, 0))
    mine = pl.BlockSpec((RB, D), lambda j, i, m: (jnp.minimum(j * steps + i, steps - 1), 0))
    vec = pl.BlockSpec((1, D), lambda j, i, m: (0, 0))
    return (NT, steps), [blk, blk, lo, hi, blk, keep], mine, vec


def ln1_call(me, parts, keep4, g, b):
    grid, ins, mine, vec = raw_specs()
    return pl.pallas_call(
        ln1_body,
        grid_spec=pltpu.PrefetchScalarGridSpec(
            num_scalar_prefetch=1,
            grid=grid,
            in_specs=ins + [vec, vec],
            out_specs=[mine] + [pl.BlockSpec((1, RB, D), lambda j, i, m: (block_of(m[0], j), i, 0))] * 2,
        ),
        out_shape=[sds((TS, D), bf), sds((NT, TS, D), bf), sds((NT, TS, D), bf)],
        compiler_params=params(),
        cost_estimate=cost(80 * TS * D, 20 * TS * D),
        name="ln1",
    )(me, *parts, keep4, g, b)


def cot_call(me, parts, keep4):
    grid, ins, mine, vec = raw_specs()
    return pl.pallas_call(
        cot_body,
        grid_spec=pltpu.PrefetchScalarGridSpec(
            num_scalar_prefetch=1,
            grid=grid,
            in_specs=[ins[0]] * 4 + ins[-1:],
            out_specs=[mine, pl.BlockSpec((1, RB, D), lambda j, i, m: (j, i, 0)), vec],
        ),
        out_shape=[sds((TS, D), bf), sds((NT, TS, D), bf), sds((1, D), f32)],
        compiler_params=params(),
        cost_estimate=cost(80 * TS * D, 20 * TS * D),
        name="cot",
    )(me, *parts, keep4)


def ln2_body(r0, c1, c3, x, keep, pb, g, b, h_ref, e_ref):
    s = r0[...] + c1[...].astype(f32) + c3[...].astype(f32)
    h = x[...].astype(f32) + keep[...] * (s + pb[...])
    h_ref[...] = h
    n, _ = stats(h)
    e_ref[...] = (n * g[...] + b[...]).astype(bf)


def ln2_call(r0, c1, c3, x, keep, pb, g, b):
    row = pl.BlockSpec((RB, D), lambda i: (i, 0))
    kp = pl.BlockSpec((RB, 1), lambda i: (i, 0))
    return pl.pallas_call(
        ln2_body,
        grid=(TS // RB,),
        in_specs=[row, row, row, row, kp] + [full((1, D))] * 3,
        out_specs=[row, row],
        out_shape=[sds((TS, D), f32), sds((TS, D), bf)],
        compiler_params=params(),
        cost_estimate=cost(20 * TS * D, 16 * TS * D),
        name="ln2",
    )(r0, c1, c3, x, keep, pb, g, b)


def norm_back(w, n, inv):
    m1 = jnp.sum(w, axis=1, keepdims=True) * (1.0 / D)
    m2 = jnp.sum(w * n, axis=1, keepdims=True) * (1.0 / D)
    return inv * (w - m1 - n * m2)


def ln2b_body(r0, c1, c3, h, c, keep, g, gh_ref, gp_ref, gg_ref, gb_ref, pb_ref):
    gn = r0[...] + c1[...].astype(f32) + c3[...].astype(f32)
    n, inv = stats(h[...])
    gh = c[...].astype(f32) + norm_back(gn * g[...], n, inv)
    gh_ref[...] = gh
    kg = keep[...] * gh
    gp_ref[...] = kg.astype(bf)
    acc_out(gg_ref, colsum(gn * n))
    acc_out(gb_ref, colsum(gn))
    acc_out(pb_ref, colsum(kg))


def ln2b_call(r0, c1, c3, h, c, keep, g):
    row = pl.BlockSpec((RB, D), lambda i: (i, 0))
    kp = pl.BlockSpec((RB, 1), lambda i: (i, 0))
    return pl.pallas_call(
        ln2b_body,
        grid=(TS // RB,),
        in_specs=[row, row, row, row, row, kp, full((1, D))],
        out_specs=[row, row] + [full((1, D))] * 3,
        out_shape=[sds((TS, D), f32), sds((TS, D), bf)] + [sds((1, D), f32)] * 3,
        compiler_params=params(),
        cost_estimate=cost(30 * TS * D, 20 * TS * D),
        name="ln2b",
    )(r0, c1, c3, h, c, keep, g)


def result_body(r0, c1, c3, h, keep, fb, o_ref):
    s = r0[...] + c1[...].astype(f32) + c3[...].astype(f32)
    o_ref[...] = (h[...] + keep[...] * (s + fb[...])).astype(bf)


def result_call(r0, c1, c3, h, keep, fb):
    row = pl.BlockSpec((RB, D), lambda i: (i, 0))
    kp = pl.BlockSpec((RB, 1), lambda i: (i, 0))
    return pl.pallas_call(
        result_body,
        grid=(TS // RB,),
        in_specs=[row, row, row, row, kp, full((1, D))],
        out_specs=row,
        out_shape=sds((TS, D), bf),
        compiler_params=params(60),
        cost_estimate=cost(8 * TS * D, 14 * TS * D),
        name="result",
    )(r0, c1, c3, h, keep, fb)


def ln1b_body(r0, c1, c3, x, gh, keep, g, res, o_ref):
    keep = keep[...]
    gn = keep * (r0[...] + c1[...].astype(f32) + c3[...].astype(f32))
    n, inv = stats(x[...].astype(f32))
    gt = (gh[...] + norm_back(gn * g[...], n, inv)).astype(bf)
    for b in range(NT):
        o_ref[b, 0] = gt[:, b * TS : (b + 1) * TS]
        o_ref[b, 1] = res[:, b * TS : (b + 1) * TS]


def ln1b_call(r0, c1, c3, x, gh, keep, g, res):
    rb = 80
    row = pl.BlockSpec((rb, D), lambda i: (i, 0))
    kp = pl.BlockSpec((rb, 1), lambda i: (i, 0))
    vec = full((1, D))
    return pl.pallas_call(
        ln1b_body,
        grid=(TS // rb,),
        in_specs=[row, row, row, row, row, kp, vec, row],
        out_specs=pl.BlockSpec((NT, 2, rb, TS), lambda i: (0, 0, i, 0)),
        out_shape=sds((NT, 2, TS, TS), bf),
        compiler_params=params(60),
        cost_estimate=cost(30 * TS * D, 24 * TS * D),
        name="ln1b",
    )(r0, c1, c3, x, gh, keep, g, res)


def place_body(x, gt_ref, res_ref, gt_s, res_s):
    for t in range(NT):
        gt_s[t * TS : (t + 1) * TS] = x[t, 0].astype(f32)
        res_s[t * TS : (t + 1) * TS] = x[t, 1].astype(f32)
    for n in range(NW * WIN):
        w, a = n // WIN, n % WIN
        rows = slice(w * WR + a * WIN, w * WR + a * WIN + WIN)
        gt_ref[n] = gt_s[rows]
        res_ref[n] = res_s[rows].astype(bf)


def place_call(x):
    n = NW * WIN
    return pl.pallas_call(
        place_body,
        grid=(1,),
        in_specs=[full((NT, 2, TS, TS))],
        out_specs=[full((n, WIN, TS))] * 2,
        scratch_shapes=[pltpu.VMEM((NT * TS, TS), f32)] * 2,
        out_shape=[sds((n, WIN, TS), f32), sds((n, WIN, TS), bf)],
        compiler_params=params(60),
        cost_estimate=cost(4 * TS * TS, 40 * TS * TS),
        name="place",
    )(x)


def turn(v):
    return v.reshape(2, 3, WIN, WIN, TS).transpose(0, 2, 1, 3, 4).reshape(2, WIN, 3 * WIN, TS)


def pad_body(w_ref, q_ref, p_ref):
    rows = w_ref.shape[0]
    w = w_ref[...]
    zero = jnp.zeros((rows, HP - HDIM), bf)
    for h in range(3 * HL):
        q_ref[:, h * HP : (h + 1) * HP] = jnp.concatenate([w[:, h * HDIM : (h + 1) * HDIM], zero], axis=1)
    for h in range(HL):
        s = 3 * HL + h
        p_ref[:, h * HP : (h + 1) * HP] = jnp.concatenate([w[:, s * HDIM : (s + 1) * HDIM], zero], axis=1)


def pad_call(g1):
    rb = 160
    return pl.pallas_call(
        pad_body,
        grid=(D // rb,),
        in_specs=[pl.BlockSpec((rb, D), lambda i: (i, 0))],
        out_specs=[
            pl.BlockSpec((rb, 3 * HL * HP), lambda i: (i, 0)),
            pl.BlockSpec((rb, HL * HP), lambda i: (i, 0)),
        ],
        out_shape=[sds((D, 3 * HL * HP), bf), sds((D, HL * HP), bf)],
        compiler_params=params(),
        cost_estimate=cost(D * 2048, 2 * D * (1280 + 2048)),
        name="padw",
    )(g1)


def block_of(me, j):
    return lax.rem(me + j, NT)


def qkv_body(x_ref, w_ref, b_ref, o_ref):
    o_ref[...] = (dot(x_ref[...], w_ref[...]) + b_ref[...]).astype(bf)


def qkv_call(x, w, bias):
    n = w.shape[1]
    tn = 512
    rows = x.shape[0]
    return pl.pallas_call(
        qkv_body,
        grid=(n // tn,),
        in_specs=[
            full((rows, D)),
            pl.BlockSpec((D, tn), lambda i: (0, i)),
            pl.BlockSpec((1, tn), lambda i: (0, i)),
        ],
        out_specs=pl.BlockSpec((rows, tn), lambda i: (0, i)),
        out_shape=sds((rows, n), bf),
        compiler_params=params(24),
        cost_estimate=cost(2 * rows * D * n, 2 * (rows * D + D * n + rows * n)),
        name="qkv",
    )(x, w, bias)


def gatt_body(*refs):
    count = len(refs) - 4
    w_ref, o_ref = refs[1 + count], refs[-1]
    for t in range(count):

        @pl.when(pl.program_id(0) == t)
        def _(t=t):
            o_ref[0] = dot(refs[1 + t][...], w_ref[...]).astype(bf)


def gatt_call(me, which, xs, w, into):
    n = w.shape[1]
    k = len(which)
    first, step = which[0], which[-1] - which[0]
    return pl.pallas_call(
        gatt_body,
        grid_spec=pltpu.PrefetchScalarGridSpec(
            num_scalar_prefetch=1,
            grid=(k,),
            in_specs=[pl.BlockSpec((TS, D), lambda t, m: (0, 0))] * k
            + [pl.BlockSpec((D, n), lambda t, m: (0, 0)), ANY],
            out_specs=pl.BlockSpec((1, TS, n), lambda t, m: (block_of(m[0], first + step * t), 0, 0)),
        ),
        out_shape=sds((NT, TS, n), bf),
        input_output_aliases={2 + k: 0},
        compiler_params=params(),
        cost_estimate=cost(2 * k * TS * D * n, 2 * (k * TS * D + D * n + k * TS * n)),
        name="gatt",
    )(me, *xs, w, into)


def gatt2_body(me_ref, a_ref, b_ref, w_ref, z_ref, o_ref, p_ref):
    p_ref[:HALF] = a_ref[...]
    p_ref[HALF:] = b_ref[...]
    o_ref[0] = dot(p_ref[...], w_ref[...]).astype(bf)


def gatt2_call(me, halves, w, into):
    n = w.shape[1]
    half = pl.BlockSpec((HALF, D), lambda i, m: (0, 0))
    return pl.pallas_call(
        gatt2_body,
        grid_spec=pltpu.PrefetchScalarGridSpec(
            num_scalar_prefetch=1,
            grid=(1,),
            in_specs=[half, half, pl.BlockSpec((D, n), lambda i, m: (0, 0)), ANY],
            out_specs=[
                pl.BlockSpec((1, TS, n), lambda i, m: (block_of(m[0], 2), 0, 0)),
                pl.BlockSpec((TS, D), lambda i, m: (0, 0)),
            ],
        ),
        out_shape=[sds((NT, TS, n), bf), sds((TS, D), bf)],
        input_output_aliases={4: 0},
        compiler_params=params(),
        cost_estimate=cost(2 * TS * D * n, 2 * (2 * TS * D + D * n + TS * n)),
        name="gatt",
    )(me, *halves, w, into)


def attn_body(qkv_ref, tab_ref, sel_ref, mask_ref, sp_ref, km_ref, z_ref, o_ref, p_ref, t_ref):
    @pl.when(pl.program_id(0) == 0)
    def _():
        t_ref[...] = dot(sel_ref[...], tab_ref[...]).astype(bf)

    qs = [qkv_ref[:, h * HP : (h + 1) * HP] for h in range(HL)]
    along = dot_nt(jnp.concatenate(qs, axis=0), t_ref[...])
    mask = mask_ref[...].astype(f32)
    along = jnp.concatenate([(along[h * WR : (h + 1) * WR] * mask).astype(bf) for h in range(HL)], axis=0)
    bias = dot(along, sp_ref[...])
    for h in range(HL):
        k = qkv_ref[:, (HL + h) * HP : (HL + h + 1) * HP]
        v = qkv_ref[:, (2 * HL + h) * HP : (2 * HL + h + 1) * HP]
        s = dot_nt(qs[h], k) * SCALE + bias[h * WR : (h + 1) * WR] + km_ref[...]
        top = jnp.max(s, axis=1, keepdims=True)
        e = jnp.exp(s - top)
        p = (e * (1.0 / jnp.sum(e, axis=1, keepdims=True))).astype(bf)
        p_ref[0, h] = p
        o_ref[:, h * HP : (h + 1) * HP] = dot(p, v).astype(bf)


def attn_call(qkv, tab, sel, mask, spread, keys, into):
    n = 3 * HL * HP
    return pl.pallas_call(
        attn_body,
        grid=(NW,),
        in_specs=[
            pl.BlockSpec((WR, n), lambda i: (i, 0)),
            full((64, HP)),
            full((512, 64)),
            full((WR, 512)),
            full((512, WR)),
            full((1, WR)),
            ANY,
        ],
        out_specs=[
            pl.BlockSpec((WR, HL * HP), lambda i: (i, 0)),
            pl.BlockSpec((1, HL, WR, WR), lambda i: (i, 0, 0, 0)),
        ],
        out_shape=[sds((NT * TS, HL * HP), bf), sds((NW, HL, WR, WR), bf)],
        scratch_shapes=[pltpu.VMEM((512, HP), bf)],
        input_output_aliases={6: 0},
        compiler_params=params(),
        cost_estimate=cost(24 * 6 * 2 * WR * WR * 256, 8e6, 24 * WR * 256),
        name="attn",
    )(qkv, tab, sel, mask, spread, keys, into)


def attnb_body(qkv_ref, p_ref, ga_ref, tab_ref, sel_ref, mask_ref, sp_ref, z_ref, o_ref, rel_ref, bias_ref, t_ref):
    @pl.when(pl.program_id(0) == 0)
    def _():
        t_ref[...] = dot(sel_ref[...], tab_ref[...]).astype(bf)
        rel_ref[...] = jnp.zeros_like(rel_ref)
        bias_ref[...] = jnp.zeros_like(bias_ref)

    table = t_ref[...]
    mask = mask_ref[...].astype(f32)
    qs, all_ds = [], []
    for h in range(HL):
        cq = slice(h * HP, (h + 1) * HP)
        cv = slice((2 * HL + h) * HP, (2 * HL + h + 1) * HP)
        ga = ga_ref[:, cq]
        p = p_ref[0, h]
        pf = p.astype(f32)
        gs = dot_nt(ga, qkv_ref[:, cv])
        delta = jnp.sum(pf * gs, axis=1, keepdims=True)
        all_ds.append((pf * (gs - delta)).astype(bf))
        qs.append(qkv_ref[:, cq])
        gv = dot_tn(p, ga).astype(bf)
        o_ref[:, cv] = gv
        bias_ref[:, cv] += colsum(gv.astype(f32))
    sums = dot_nt(jnp.concatenate(all_ds, axis=0), sp_ref[...])
    sums = jnp.concatenate([(sums[h * WR : (h + 1) * WR] * mask).astype(bf) for h in range(HL)], axis=0)
    gq_rel = dot(sums, table)
    rel_ref[...] += dot_tn(sums, jnp.concatenate(qs, axis=0))
    for h in range(HL):
        cq = slice(h * HP, (h + 1) * HP)
        ck = slice((HL + h) * HP, (HL + h + 1) * HP)
        ds = all_ds[h]
        o_ref[:, ck] = (dot_tn(ds, qs[h]) * SCALE).astype(bf)
        gq = (dot(ds, qkv_ref[:, ck]) * SCALE + gq_rel[h * WR : (h + 1) * WR]).astype(bf)
        o_ref[:, cq] = gq
        bias_ref[:, cq] += colsum(gq.astype(f32))


def attnb_call(qkv, p, ga, tab, sel, mask, spread, into):
    n = 3 * HL * HP
    return pl.pallas_call(
        attnb_body,
        grid=(NW,),
        in_specs=[
            pl.BlockSpec((WR, n), lambda i: (i, 0)),
            pl.BlockSpec((1, HL, WR, WR), lambda i: (i, 0, 0, 0)),
            pl.BlockSpec((WR, HL * HP), lambda i: (i, 0)),
            full((64, HP)),
            full((512, 64)),
            full((WR, 512)),
            full((512, WR)),
            ANY,
        ],
        out_specs=[pl.BlockSpec((WR, n), lambda i: (i, 0)), full((512, HP)), full((1, n))],
        out_shape=[sds((NT * TS, n), bf), sds((512, HP), f32), sds((1, n), f32)],
        scratch_shapes=[pltpu.VMEM((512, HP), bf)],
        input_output_aliases={7: 0},
        compiler_params=params(),
        cost_estimate=cost(24 * 10 * 2 * WR * WR * 256, 14e6),
        name="attnb",
    )(qkv, p, ga, tab, sel, mask, spread, into)


def partial_body(me_ref, a_ref, w_ref, *refs):
    w = w_ref[...]
    if len(refs) == 5:
        n_ref, (r0, r1, r2a, r2b, r3) = None, refs
    else:
        n_ref, keep_ref, r0, r1, r2a, r2b, r3, gg_ref, gb_ref = refs
    gain = bias = 0.0
    for j, ref in ((2, None), (1, r1), (3, r3), (0, r0)):
        t = block_of(me_ref[0], j)
        r = dot_nt(a_ref[t], w)
        if n_ref is not None:
            gain = gain + colsum(r * n_ref[t].astype(f32))
            bias = bias + colsum(r * keep_ref[t])
        if ref is None:
            r2a[...] = r[:HALF].astype(bf)
            r2b[...] = r[HALF:].astype(bf)
        else:
            ref[...] = r.astype(ref.dtype)
    if n_ref is not None:
        gg_ref[...] = gain
        gb_ref[...] = bias


def partial_call(me, a, w, name, norm=()):
    k = a.shape[2]
    tn = 256
    whole = pl.BlockSpec((TS, tn), lambda i, m: (0, i))
    half = pl.BlockSpec((HALF, tn), lambda i, m: (0, i))
    ins = [pl.BlockSpec((NT, TS, tn), lambda i, m: (0, 0, i)), pl.BlockSpec((NT, TS, 1), lambda i, m: (0, 0, 0))]
    outs = [whole, whole, half, half, whole]
    shapes = [sds((TS, D), f32), sds((TS, D), bf), sds((HALF, D), bf), sds((HALF, D), bf), sds((TS, D), bf)]
    if norm:
        outs += [pl.BlockSpec((1, tn), lambda i, m: (0, i))] * 2
        shapes += [sds((1, D), f32)] * 2
    return pl.pallas_call(
        partial_body,
        grid_spec=pltpu.PrefetchScalarGridSpec(
            num_scalar_prefetch=1,
            grid=(D // tn,),
            in_specs=[
                pl.BlockSpec((NT, TS, k), lambda i, m: (0, 0, 0)),
                pl.BlockSpec((tn, k), lambda i, m: (i, 0)),
            ]
            + ins[: len(norm)],
            out_specs=outs,
        ),
        out_shape=shapes,
        compiler_params=params(24),
        cost_estimate=cost(2 * NT * TS * D * k, 2 * (NT * TS * k + D * k + 9 * TS * D)),
        name=name,
    )(me, a, w, *norm)


def merge_body(r1, a, r3, b, s1, s3):
    s1[...] = (r1[...].astype(f32) + a[...].astype(f32)).astype(bf)
    s3[...] = (r3[...].astype(f32) + b[...].astype(f32)).astype(bf)


def merge_call(r1, a, r3, b, mb=16):
    one = pl.BlockSpec((HALF, D), lambda i: (0, 0))
    two = pl.BlockSpec((HALF, D), lambda i: (1, 0))
    return pl.pallas_call(
        merge_body,
        grid=(1,),
        in_specs=[one, one, two, one],
        out_specs=[one, two],
        out_shape=[sds((TS, D), bf)] * 2,
        input_output_aliases={0: 0, 2: 1},
        compiler_params=params(mb),
        cost_estimate=cost(4 * HALF * D, 12 * HALF * D),
        name="merge",
    )(r1, a, r3, b)


def mlp_body(halved, k, *refs):
    ins = refs[: 2 if halved else k]
    gb_refs = refs[len(ins) : len(ins) + k]
    w1_ref, w2_ref, b1_ref = refs[len(ins) + k : len(ins) + k + 3]
    outs = refs[len(ins) + k + 3 : -4]
    z_s, gb_s, br_s, gn_s = refs[-4:]
    step = pl.program_id(0)

    @pl.when(step == 0)
    def _():
        br_s[...] = jnp.zeros_like(br_s)
        gn_s[...] = jnp.zeros_like(gn_s)
        rows = k * TS // len(ins)
        for t, ref in enumerate(ins):
            z_s[t * rows : (t + 1) * rows] = ref[...]
        for t, ref in enumerate(gb_refs):
            gb_s[t * TS : (t + 1) * TS] = ref[0]

    w1 = w1_ref[...]
    w2 = w2_ref[...]
    pre = dot(z_s[...], w1) + b1_ref[...]
    ga = dot(gb_s[...], w2)
    cdf = 0.5 + 0.5 * lax.erf(pre * 0.7071067811865476)
    act = (pre * cdf).astype(bf)
    slope = cdf + pre * (0.3989422804014327 * jnp.exp(-0.5 * pre * pre))
    gp = (ga * slope).astype(bf)
    for t in range(k):
        rows = slice(t * TS, (t + 1) * TS)
        outs[3 * t][...] = act[rows]
        outs[3 * t + 1][...] = gp[rows]
        outs[3 * t + 2][...] = colsum(gp[rows].astype(f32))
    br_s[...] += dot_nt(act, w2)
    gn_s[...] += dot_nt(gp, w1)

    @pl.when(step == pl.num_programs(0) - 1)
    def _():
        rest = outs[3 * k :]
        for total, refs_out in ((br_s, rest[0::2]), (gn_s, rest[1::2])):
            at = 0
            for ref in refs_out:
                if at < total.shape[0]:
                    ref[...] = total[at : at + ref.shape[0]].astype(ref.dtype)
                    at += ref.shape[0]
        if halved:
            rest[4][...] = z_s[...]


def mlp_call(which, zs, gb, w, b1, kind):
    halved = which == (2,)
    k = len(which)
    tf = 256
    nf = D // tf
    col = pl.BlockSpec((TS, tf), lambda i: (0, i))
    bias = pl.BlockSpec((1, tf), lambda i: (0, i))
    half = full((HALF, D))
    block = full((TS, D))
    outs = [col, col, bias] * k
    shapes = [sds((TS, D), bf), sds((TS, D), bf), sds((1, D), f32)] * k
    if halved:
        outs += [half] * 4 + [block]
        shapes += [sds((HALF, D), bf)] * 4 + [sds((TS, D), bf)]
    else:
        outs += [block] * (2 * k)
        shapes += [sds((TS, D), kind)] * (2 * k)
    return pl.pallas_call(
        partial(mlp_body, halved, k),
        grid=(nf,),
        in_specs=[half if halved else block] * len(zs)
        + [pl.BlockSpec((1, TS, D), lambda i, j=j: (j, 0, 0)) for j in which]
        + [
            pl.BlockSpec((D, tf), lambda i: (0, i)),
            pl.BlockSpec((D, tf), lambda i: (0, i + nf)),
            bias,
        ],
        out_specs=outs,
        out_shape=shapes,
        scratch_shapes=[pltpu.VMEM((k * TS, D), bf)] * 2 + [pltpu.VMEM((k * TS, D), f32)] * 2,
        compiler_params=params(32),
        cost_estimate=cost(k * 8 * TS * D * D, 4 * D * D + k * 12 * TS * D, k * 2 * TS * D),
        name="mlp",
    )(*zs, *[gb] * k, w, w, b1)


NG = 2 * D


def tokgrad_body(*refs):
    o_ref = refs[-1]
    lhs, rhs = refs[:4], refs[4:8]
    total = None
    for j in range(NT):
        left = lhs[j][0] if len(lhs[j].shape) == 3 else lhs[j][...]
        part = dot_tn(left, rhs[j][...])
        total = part if total is None else total + part
    o_ref[...] = total.astype(bf)


def tokgrad_call(lhs, rhs, into, at):
    td = 256
    if len(lhs) == 1:
        left = [pl.BlockSpec((1, TS, td), lambda i, j=j: (j, 0, i)) for j in range(NT)]
        lhs = list(lhs) * NT
    else:
        left = [pl.BlockSpec((TS, td), lambda i: (0, i))] * NT
    return pl.pallas_call(
        tokgrad_body,
        grid=(D // td,),
        in_specs=left + [full((TS, D))] * NT + [ANY] * (into is not None),
        out_specs=pl.BlockSpec((td, D), lambda i: (i, at)),
        out_shape=sds((D, NG), bf),
        input_output_aliases={} if into is None else {2 * NT: 0},
        compiler_params=params(24),
        cost_estimate=cost(8 * TS * D * D, 2 * (8 * TS * D + D * D)),
        name="fcgrad",
    )(*lhs, *rhs, *(() if into is None else (into,)))


def narrow(x, heads):
    return jnp.concatenate([x[:, h * HP : h * HP + HDIM] for h in range(heads)], axis=1)


def qpgrad_body(me_ref, e_ref, dq_ref, p0, p1, p2, p3, a_ref, o_ref):
    o_ref[:, : 3 * HL * HDIM] = narrow(dot_tn(e_ref[...], dq_ref[...]), 3 * HL).astype(bf)
    total = None
    for j, p in enumerate((p0, p1, p2, p3)):
        part = dot_tn(p[...], a_ref[block_of(me_ref[0], j)])
        total = part if total is None else total + part
    o_ref[:, 3 * HL * HDIM :] = narrow(total, HL).astype(bf)


def qpgrad_call(me, e, dqkv, p, att4):
    td = 256
    rows, n = dqkv.shape
    k = att4.shape[2]
    return pl.pallas_call(
        qpgrad_body,
        grid_spec=pltpu.PrefetchScalarGridSpec(
            num_scalar_prefetch=1,
            grid=(D // td,),
            in_specs=[
                pl.BlockSpec((rows, td), lambda i, m: (0, i)),
                pl.BlockSpec((rows, n), lambda i, m: (0, 0)),
            ]
            + [pl.BlockSpec((TS, td), lambda i, m: (0, i))] * 4
            + [pl.BlockSpec((NT, TS, k), lambda i, m: (0, 0, 0))],
            out_specs=pl.BlockSpec((td, D), lambda i, m: (i, 0)),
        ),
        out_shape=sds((D, D), bf),
        compiler_params=params(24),
        cost_estimate=cost(2 * rows * D * (n + k), 2 * (2 * rows * D + rows * (n + k) + D * D)),
        name="qpgrad",
    )(me, e, dqkv, *p, att4)


UP = [(i, (i + 1) % NT) for i in range(NT)]
DOWN = [(i, (i - 1) % NT) for i in range(NT)]


def up(v):
    return lax.ppermute(v, "tp", UP)


def down(v):
    return lax.ppermute(v, "tp", DOWN)


def after(v, *deps):
    return lax.optimization_barrier((v, deps))[0]


def ring_gather(own, first=None, between=None):
    b3 = up(own)
    b1 = down(own)
    if first is not None:
        b3, b1, first = lax.optimization_barrier((b3, b1, first))
    half = own.shape[0] // 2
    u, d = up(b3[:half]), down(b1[half:])
    if between is not None:
        first = between(b1, b3, first)
        u, d, first = lax.optimization_barrier((u, d, first))
    return (own, b1, u, d, b3), first


def ring_scatter(r1, r2a, r2b, r3, first=None, mb=16):
    a = up(r2a)
    b = down(r2b)
    if first is not None:
        a, b, first = lax.optimization_barrier((a, b, first))
    s1, s3 = merge_call(r1, a, r3, b, mb)
    return (s3, s1), first


def ring_finish(sums):
    return down(sums[0]), up(sums[1])


def shard_place():
    s = lax.axis_index("shard")
    return s // 4, (s // 2) % 2, s % 2


def shard_move(v, f):
    return lax.ppermute(v, "shard", [(i, f(i)) for i in range(16)])


def pick(v, i, ax):
    return lax.dynamic_index_in_dim(v, i, ax, keepdims=False)


def add_low(p, q):
    return (p.astype(f32) + q.astype(f32)).astype(bf)


def over_shard_1(v):
    n = v.shape[1]
    y, zl, core = shard_place()
    v = v.reshape(4, 2, 2, 80, n)
    v = add_low(pick(v, core, 2), shard_move(pick(v, 1 - core, 2), lambda i: i ^ 1))
    w = [pick(v, (y + j) % 4, 0) for j in range(4)]
    a = shard_move(w[2][0], lambda i: (i + 4) % 16)
    b = shard_move(w[2][1], lambda i: (i + 12) % 16)
    return w[0], jnp.stack([add_low(w[1][0], a), w[1][1]]), jnp.stack([w[3][0], add_low(w[3][1], b)])


def over_shard_2(parts):
    w0, s1, s3 = parts
    return w0, shard_move(s3, lambda i: (i + 12) % 16), shard_move(s1, lambda i: (i + 4) % 16)


def over_shard_3(parts):
    w0, c1, c3 = parts
    y, zl, core = shard_place()
    v = (w0.astype(f32) + c1.astype(f32) + c3.astype(f32)).astype(bf)
    return pick(v, zl, 0), shard_move(pick(v, 1 - zl, 0), lambda i: i ^ 2)


def over_ctx(v):
    return v.astype(f32) + lax.ppermute(v, "ctx", [(0, 1), (1, 0)]).astype(f32)


def small_pack(parts):
    out = []
    for part in parts:
        v = jnp.concatenate([a.ravel() for a in part])
        out.append(jnp.pad(v, (0, -v.size % 1024)).reshape(-1, 128))
    return jnp.concatenate(out, axis=0).astype(bf)


def small_sum(everyone):
    return jnp.sum(everyone.astype(f32), axis=0)


def small_split(both, world):
    rows = -(-sum(a.size for a in world) // 1024) * 8
    return both[:rows], both[rows:]


def pair_sum(w, step):
    return w + lax.ppermute(w, "tp", [(i, i ^ step) for i in range(NT)])


def small_finish(w, g, world, group):
    out = []
    for part, flat in ((world, w.ravel()), (group, g.ravel())):
        at = 0
        for a in part:
            out.append(flat[at : at + a.size].reshape(a.shape))
            at += a.size
    return out


def from_everyone(array, axis):
    size = lax.axis_size(axis)
    return lax.all_to_all(jnp.broadcast_to(array[None], (size, *array.shape)), axis, 0, 0, tiled=True)


def windows(grid):
    n = grid.shape[-1]
    w = grid.reshape(2, WIN, 3, WIN, n).transpose(0, 2, 1, 3, 4).reshape(NW, CELLS, n)
    w = jnp.pad(w, ((0, 0), (0, WR - CELLS), (0, 0))).reshape(NW * WR, n)
    return jnp.pad(w, ((0, NT * TS - NW * WR), (0, 0))).reshape(NT, TS, n)


def local(
    tokens,
    valid_mask,
    ln1_gain,
    ln1_bias,
    qkv_weight,
    qkv_bias,
    rel_rows,
    rel_cols,
    proj_weight,
    proj_bias,
    ln2_gain,
    ln2_bias,
    fc1_weight,
    fc1_bias,
    fc2_weight,
    fc2_bias,
    cotangent,
):
    tp_index = lax.axis_index("tp")
    me = tp_index.astype(jnp.int32).reshape(1)
    sel, mask, spread, keys = rel_constants()
    sel = jnp.asarray(sel, bf)
    mask = jnp.asarray(mask, bf)
    spread = jnp.asarray(spread, bf)
    keys = jnp.asarray(keys, f32)
    row = lambda v: v.reshape(1, -1)

    own1 = jnp.concatenate([jnp.moveaxis(qkv_weight, 1, 0).reshape(80, 960), proj_weight.T], axis=1)
    own2 = jnp.concatenate([fc1_weight, fc2_weight.T], axis=1)
    all1 = lax.all_gather(own1, "shard", axis=0, tiled=True)
    all2 = lax.all_gather(own2, "shard", axis=0, tiled=True)
    bias_q = jnp.pad(qkv_bias.reshape(2, HL, HDIM), ((0, 0), (0, 0), (0, HP - HDIM))).reshape(2, HL * HP)
    bias_p = row(jnp.concatenate([bias_q[0], jnp.zeros((HL * HP,), f32), bias_q[1]]))
    tab = jnp.zeros((64, HP), bf).at[:RELS, :HDIM].set(rel_rows).at[32 : 32 + RELS, :HDIM].set(rel_cols)

    keep4 = windows(valid_mask.astype(f32)[..., None])
    keep = lax.dynamic_index_in_dim(keep4, tp_index, 0, keepdims=False)
    toks, (qkvp, projp) = ring_gather(windows(tokens), None, lambda b1, b3, _: pad_call(all1))
    x, e4, n4 = ln1_call(me, toks, keep4, row(ln1_gain), row(ln1_bias))
    ents = e4.reshape(NT * TS, D)
    cot = after(windows(cotangent), toks[2], toks[3])
    cot3, cot1 = up(cot), down(cot)
    cot3, cot1, flat = lax.optimization_barrier((cot3, cot1, qkv_call(ents, qkvp, bias_p)))
    cots = (cot, cot1, up(cot3), cot3)
    att, probs = attn_call(flat, tab, sel, mask, spread, keys, jnp.zeros((NT * TS, HL * HP), bf))
    att, *cots = lax.optimization_barrier((att, *cots))
    att4 = att.reshape(NT, TS, HL * HP)
    r0, *rest = partial_call(me, att4, projp, "proj")
    sums, _ = ring_scatter(*rest, None, 60)
    c, gb, sum_fc2_bias = cot_call(me, cots, keep4)
    (c1, c3), gb = lax.optimization_barrier((ring_finish(sums), gb))
    h, z = ln2_call(r0, c1, c3, x, keep, row(proj_bias), row(ln2_gain), row(ln2_bias))

    b1row = row(fc1_bias)
    mlp = lambda which, zz, kind: mlp_call(which, zz, gb, all2, b1row, kind)
    zs, (m0, m13) = ring_gather(
        z, mlp((0,), (z,), f32), lambda b1, b3, first: (first, mlp((1, 3), (b1, b3), bf))
    )
    act0, gpre0, fb0, br0, gn0 = m0
    act1, gpre1, fb1, act3, gpre3, fb3, br1, gn1, br3, gn3 = m13
    act2, gpre2, fb2, br2a, gn2a, br2b, gn2b, z2 = mlp((2,), (zs[2], zs[3]), bf)
    gpres = (gpre0, gpre1, gpre2, gpre3)
    sum_fc1_bias = fb0 + fb1 + fb2 + fb3
    sums, grads = ring_scatter(gn1, gn2a, gn2b, gn3, tokgrad_call((gb,), (act0, act1, act2, act3), None, 1))
    grads = tokgrad_call((z, zs[1], z2, zs[4]), gpres, grads, 0)
    (c1, c3), grads = lax.optimization_barrier((ring_finish(sums), grads))
    own_fc = lax.psum_scatter(grads, "shard", scatter_dimension=0, tiled=True)
    gh, gproj, sum_ln2_gain, sum_ln2_bias, sum_proj_bias = ln2b_call(
        gn0, c1, c3, h, c, keep, row(ln2_gain)
    )
    ga = gatt_call(me, (0,), (gproj,), projp, jnp.zeros((NT, TS, HL * HP), bf))
    gps, ga = ring_gather(gproj, ga, lambda b1, b3, ga: gatt_call(me, (1, 3), (b1, b3), projp, ga))
    ga, gp2 = gatt2_call(me, gps[2:4], projp, ga)

    branch = after((br1, br2a, br2b, br3), gp2)
    dqkv, rel, sum_qkv_bias = attnb_call(
        flat,
        probs,
        ga.reshape(NT * TS, HL * HP),
        tab,
        sel,
        mask,
        spread,
        jnp.zeros((NT * TS, 3 * HL * HP), bf),
    )
    sums, dqkv = ring_scatter(*branch, dqkv)
    sums, dqkv = lax.optimization_barrier((sums, dqkv))
    f1, f3 = ring_finish(sums)
    r0, r1, r2a, r2b, r3, sum_ln1_gain, sum_ln1_bias = partial_call(
        me, dqkv.reshape(NT, TS, 3 * HL * HP), qkvp, "gnorm1", (n4, keep4)
    )
    gradq = qpgrad_call(me, ents, dqkv, (gproj, gps[1], gp2, gps[4]), att4)
    gradq, f1, f3 = lax.optimization_barrier((gradq, f1, f3))
    sums, gradq = ring_scatter(r1, r2a, r2b, r3, gradq, 60)
    c1, c3 = ring_finish(sums)
    parts = over_shard_1(after(gradq, sums))
    res = result_call(br0, f1, f3, h, keep, row(fc2_bias))
    small = after(
        (
            rel,
            sum_qkv_bias,
            sum_fc1_bias,
            sum_ln1_gain,
            sum_ln1_bias,
            sum_ln2_gain,
            sum_ln2_bias,
            sum_proj_bias,
            sum_fc2_bias,
        ),
        sums,
    )
    rels = jnp.dot(sel.astype(f32).T, small[0], precision=lax.Precision.HIGHEST)
    qb = small[1].reshape(3, HL, HP)[:, :, :HDIM]
    world = [*small[3:], rels[:RELS, :HDIM], rels[32 : 32 + RELS, :HDIM]]
    group = [qb[0], qb[2], small[2]]
    everyone = from_everyone(small_pack((world, group)), ("shard", "ctx"))
    c1, c3, res, everyone, parts = lax.optimization_barrier((c1, c3, res, everyone, parts))
    parts = over_shard_2(parts)
    out = ln1b_call(r0, c1, c3, x, gh, keep, row(ln1_gain), res)
    out, parts, fc = lax.optimization_barrier((out, parts, over_ctx(own_fc)))
    w, g = small_split(small_sum(after(everyone, out)), world)
    blocks = lax.all_to_all(out, "tp", 0, 0, tiled=True)
    half, other = over_shard_3(parts)
    q = over_ctx(add_low(half, other))
    blocks, q, w = lax.optimization_barrier((blocks, q, pair_sum(w, 1)))
    w = pair_sum(w, 3)
    g_ln1g, g_ln1b, g_ln2g, g_ln2b, g_pb, g_f2b, g_rr, g_rc, g_q, g_v, g_f1b = small_finish(w, g, world, group)
    token_grads, result = place_call(blocks)
    token_grads, result = turn(token_grads), turn(result)
    return (
        result,
        token_grads,
        g_ln1g.ravel(),
        g_ln1b.ravel(),
        jnp.moveaxis(q[:, : 3 * HL * HDIM].reshape(80, 3, 320), 0, 1),
        jnp.stack([g_q.ravel(), g_v.ravel()]),
        g_rr,
        g_rc,
        q[:, 3 * HL * HDIM :].T,
        g_pb.ravel(),
        g_ln2g.ravel(),
        g_ln2b.ravel(),
        fc[:, :D],
        g_f1b.ravel(),
        fc[:, D:].T,
        g_f2b.ravel(),
    )


def solution(mesh):
    cells = P("shard", "ctx", None, "tp")
    in_specs = (
        cells,
        P("shard", "ctx", None),
        P(),
        P(),
        P(None, "shard", "tp"),
        P(None, "tp"),
        P(),
        P(),
        P("tp", "shard"),
        P(),
        P(),
        P(),
        P("shard", "tp"),
        P("tp"),
        P("tp", "shard"),
        P(),
        cells,
    )
    out_specs = (
        cells,
        cells,
        P(),
        P(),
        P(None, "shard", "tp"),
        P(None, "tp"),
        P(),
        P(),
        P("tp", "shard"),
        P(),
        P(),
        P(),
        P("shard", "tp"),
        P("tp"),
        P("tp", "shard"),
        P(),
    )
    return jax.shard_map(local, mesh=mesh, in_specs=in_specs, out_specs=out_specs, check_vma=False)
```

```python
from functools import partial

import jax
import jax.numpy as jnp
import numpy as np
from jax import lax
from jax.experimental import pallas as pl
from jax.experimental.pallas import tpu as pltpu
from jax.sharding import PartitionSpec as P

HEADS = 16
HDIM = 80
WIN = 14
D = 1280
NT = 4
HL = HEADS // NT
CELLS = WIN * WIN
WR = 208
NW = 6
TS = 320
HALF = TS // 2
HP = 128
RELS = 2 * WIN - 1
EPS = 1e-06
SCALE = HDIM ** (-0.5)
bf = jnp.bfloat16
f32 = jnp.float32
MB = 1024 * 1024


def rel_constants():
    sel = np.zeros((512, 64), np.float32)
    mask = np.zeros((WR, 512), np.float32)
    spread = np.zeros((512, WR), np.float32)
    for a in range(WIN):
        for x in range(WIN):
            sel[a * WIN + x, a - x + WIN - 1] = 1
            sel[256 + a * WIN + x, 32 + a - x + WIN - 1] = 1
    for a in range(WIN):
        for b in range(WIN):
            row = a * WIN + b
            mask[row, a * WIN : a * WIN + WIN] = 1
            mask[row, 256 + b * WIN : 256 + b * WIN + WIN] = 1
    for a in range(WIN):
        for x in range(WIN):
            for y in range(WIN):
                spread[a * WIN + x, x * WIN + y] = 1
                spread[256 + a * WIN + y, x * WIN + y] = 1
    keys = np.where(np.arange(WR) < CELLS, 0.0, -1e30).astype(np.float32)[None]
    return sel, mask, spread, keys


def dot(a, b):
    return lax.dot_general(a, b, (((1,), (0,)), ((), ())), preferred_element_type=f32)


def dot_nt(a, b):
    return lax.dot_general(a, b, (((1,), (1,)), ((), ())), preferred_element_type=f32)


def dot_tn(a, b):
    return lax.dot_general(a, b, (((0,), (0,)), ((), ())), preferred_element_type=f32)


def params(mb=16):
    return pltpu.CompilerParams(vmem_limit_bytes=mb * MB)


def cost(flops, nbytes, trans=0):
    return pl.CostEstimate(flops=int(flops), bytes_accessed=int(nbytes), transcendentals=int(trans))


def sds(shape, dtype):
    return jax.ShapeDtypeStruct(shape, dtype)


def full(shape):
    return pl.BlockSpec(shape, lambda *g: (0,) * len(shape))


ANY = pl.BlockSpec(memory_space=pl.ANY)


def stats(x):
    mean = jnp.sum(x, axis=1, keepdims=True) * (1.0 / D)
    xc = x - mean
    var = jnp.sum(xc * xc, axis=1, keepdims=True) * (1.0 / D)
    inv = lax.rsqrt(var + EPS)
    return xc * inv, inv


def colsum(x):
    return jnp.sum(x, axis=0, keepdims=True)


def acc_out(ref, value):
    @pl.when(pl.program_id(0) == 0)
    def _():
        ref[...] = jnp.zeros_like(ref)

    ref[...] += value


RB = 160


def in_feature_order(me, t, refs, use):
    if len(refs) == 5:
        r0, r1, ra, rb, r3 = refs
        r2 = jnp.where(t < NT // 2, ra[0].astype(f32), rb[0].astype(f32))
    else:
        r0, r1, r2, r3 = refs
        r2 = r2[0].astype(f32)
    parts = (r0[0].astype(f32), r1[0].astype(f32), r2, r3[0].astype(f32))
    for k in range(NT):

        @pl.when(me == k)
        def _(k=k):
            use(jnp.concatenate([parts[(b - k) % NT] for b in range(NT)], axis=1))


def ln1_body(me_ref, r0, r1, ra, rb, r3, keep_ref, g_ref, b_ref, x_ref, e_ref, n_ref):
    me = me_ref[0]
    j = pl.program_id(0)

    def use(x):
        n, _ = stats(x)
        e_ref[0] = (keep_ref[0] * (n * g_ref[...] + b_ref[...])).astype(bf)
        n_ref[0] = (keep_ref[0] * n).astype(bf)

        @pl.when(j == 0)
        def _():
            x_ref[...] = x.astype(bf)

    in_feature_order(me, block_of(me, j), (r0, r1, ra, rb, r3), use)


def cot_body(me_ref, r0, r1, r2, r3, keep_ref, c_ref, gb_ref, fb_ref):
    me = me_ref[0]
    j = pl.program_id(0)

    @pl.when((j == 0) & (pl.program_id(1) == 0))
    def _():
        fb_ref[...] = jnp.zeros_like(fb_ref)

    def use(c):
        gb = keep_ref[0] * c
        gb_ref[0] = gb.astype(bf)

        @pl.when(j == 0)
        def _():
            c_ref[...] = c.astype(bf)
            fb_ref[...] += colsum(gb)

    in_feature_order(me, block_of(me, j), (r0, r1, r2, r3), use)


def raw_specs():
    steps = TS // RB
    blk = pl.BlockSpec((1, RB, TS), lambda j, i, m: (block_of(m[0], j), i, 0))
    lo = pl.BlockSpec((1, RB, TS), lambda j, i, m: (jnp.minimum(block_of(m[0], j), 1), i, 0))
    hi = pl.BlockSpec((1, RB, TS), lambda j, i, m: (jnp.maximum(block_of(m[0], j) - 2, 0), i, 0))
    keep = pl.BlockSpec((1, RB, 1), lambda j, i, m: (block_of(m[0], j), i, 0))
    mine = pl.BlockSpec((RB, D), lambda j, i, m: (jnp.minimum(j * steps + i, steps - 1), 0))
    vec = pl.BlockSpec((1, D), lambda j, i, m: (0, 0))
    return (NT, steps), [blk, blk, lo, hi, blk, keep], mine, vec


def ln1_call(me, parts, keep4, g, b):
    grid, ins, mine, vec = raw_specs()
    return pl.pallas_call(
        ln1_body,
        grid_spec=pltpu.PrefetchScalarGridSpec(
            num_scalar_prefetch=1,
            grid=grid,
            in_specs=ins + [vec, vec],
            out_specs=[mine] + [pl.BlockSpec((1, RB, D), lambda j, i, m: (block_of(m[0], j), i, 0))] * 2,
        ),
        out_shape=[sds((TS, D), bf), sds((NT, TS, D), bf), sds((NT, TS, D), bf)],
        compiler_params=params(),
        cost_estimate=cost(80 * TS * D, 20 * TS * D),
        name="ln1",
    )(me, *parts, keep4, g, b)


def cot_call(me, parts, keep4):
    grid, ins, mine, vec = raw_specs()
    return pl.pallas_call(
        cot_body,
        grid_spec=pltpu.PrefetchScalarGridSpec(
            num_scalar_prefetch=1,
            grid=grid,
            in_specs=[ins[0]] * 4 + ins[-1:],
            out_specs=[mine, pl.BlockSpec((1, RB, D), lambda j, i, m: (j, i, 0)), vec],
        ),
        out_shape=[sds((TS, D), bf), sds((NT, TS, D), bf), sds((1, D), f32)],
        compiler_params=params(),
        cost_estimate=cost(80 * TS * D, 20 * TS * D),
        name="cot",
    )(me, *parts, keep4)


def ln2_body(r0, c1, c3, x, keep, pb, g, b, h_ref, e_ref):
    s = r0[...] + c1[...].astype(f32) + c3[...].astype(f32)
    h = x[...].astype(f32) + keep[...] * (s + pb[...])
    h_ref[...] = h
    n, _ = stats(h)
    e_ref[...] = (n * g[...] + b[...]).astype(bf)


def ln2_call(r0, c1, c3, x, keep, pb, g, b):
    row = pl.BlockSpec((RB, D), lambda i: (i, 0))
    kp = pl.BlockSpec((RB, 1), lambda i: (i, 0))
    return pl.pallas_call(
        ln2_body,
        grid=(TS // RB,),
        in_specs=[row, row, row, row, kp] + [full((1, D))] * 3,
        out_specs=[row, row],
        out_shape=[sds((TS, D), f32), sds((TS, D), bf)],
        compiler_params=params(),
        cost_estimate=cost(20 * TS * D, 16 * TS * D),
        name="ln2",
    )(r0, c1, c3, x, keep, pb, g, b)


def norm_back(w, n, inv):
    m1 = jnp.sum(w, axis=1, keepdims=True) * (1.0 / D)
    m2 = jnp.sum(w * n, axis=1, keepdims=True) * (1.0 / D)
    return inv * (w - m1 - n * m2)


def ln2b_body(r0, c1, c3, h, c, keep, g, gh_ref, gp_ref, gg_ref, gb_ref, pb_ref):
    gn = r0[...] + c1[...].astype(f32) + c3[...].astype(f32)
    n, inv = stats(h[...])
    gh = c[...].astype(f32) + norm_back(gn * g[...], n, inv)
    gh_ref[...] = gh
    kg = keep[...] * gh
    gp_ref[...] = kg.astype(bf)
    acc_out(gg_ref, colsum(gn * n))
    acc_out(gb_ref, colsum(gn))
    acc_out(pb_ref, colsum(kg))


def ln2b_call(r0, c1, c3, h, c, keep, g):
    row = pl.BlockSpec((RB, D), lambda i: (i, 0))
    kp = pl.BlockSpec((RB, 1), lambda i: (i, 0))
    return pl.pallas_call(
        ln2b_body,
        grid=(TS // RB,),
        in_specs=[row, row, row, row, row, kp, full((1, D))],
        out_specs=[row, row] + [full((1, D))] * 3,
        out_shape=[sds((TS, D), f32), sds((TS, D), bf)] + [sds((1, D), f32)] * 3,
        compiler_params=params(),
        cost_estimate=cost(30 * TS * D, 20 * TS * D),
        name="ln2b",
    )(r0, c1, c3, h, c, keep, g)


def result_body(r0, c1, c3, h, keep, fb, o_ref):
    s = r0[...] + c1[...].astype(f32) + c3[...].astype(f32)
    o_ref[...] = (h[...] + keep[...] * (s + fb[...])).astype(bf)


def result_call(r0, c1, c3, h, keep, fb):
    row = pl.BlockSpec((RB, D), lambda i: (i, 0))
    kp = pl.BlockSpec((RB, 1), lambda i: (i, 0))
    return pl.pallas_call(
        result_body,
        grid=(TS // RB,),
        in_specs=[row, row, row, row, kp, full((1, D))],
        out_specs=row,
        out_shape=sds((TS, D), bf),
        compiler_params=params(60),
        cost_estimate=cost(8 * TS * D, 14 * TS * D),
        name="result",
    )(r0, c1, c3, h, keep, fb)


def ln1b_body(r0, c1, c3, x, gh, keep, g, res, o_ref):
    keep = keep[...]
    gn = keep * (r0[...] + c1[...].astype(f32) + c3[...].astype(f32))
    n, inv = stats(x[...].astype(f32))
    gt = (gh[...] + norm_back(gn * g[...], n, inv)).astype(bf)
    for b in range(NT):
        o_ref[b, 0] = gt[:, b * TS : (b + 1) * TS]
        o_ref[b, 1] = res[:, b * TS : (b + 1) * TS]


def ln1b_call(r0, c1, c3, x, gh, keep, g, res):
    rb = 80
    row = pl.BlockSpec((rb, D), lambda i: (i, 0))
    kp = pl.BlockSpec((rb, 1), lambda i: (i, 0))
    vec = full((1, D))
    return pl.pallas_call(
        ln1b_body,
        grid=(TS // rb,),
        in_specs=[row, row, row, row, row, kp, vec, row],
        out_specs=pl.BlockSpec((NT, 2, rb, TS), lambda i: (0, 0, i, 0)),
        out_shape=sds((NT, 2, TS, TS), bf),
        compiler_params=params(60),
        cost_estimate=cost(30 * TS * D, 24 * TS * D),
        name="ln1b",
    )(r0, c1, c3, x, gh, keep, g, res)


def place_body(x, gt_ref, res_ref, gt_s, res_s):
    for t in range(NT):
        gt_s[t * TS : (t + 1) * TS] = x[t, 0].astype(f32)
        res_s[t * TS : (t + 1) * TS] = x[t, 1].astype(f32)
    for n in range(NW * WIN):
        w, a = n // WIN, n % WIN
        rows = slice(w * WR + a * WIN, w * WR + a * WIN + WIN)
        gt_ref[n] = gt_s[rows]
        res_ref[n] = res_s[rows].astype(bf)


def place_call(x):
    n = NW * WIN
    return pl.pallas_call(
        place_body,
        grid=(1,),
        in_specs=[full((NT, 2, TS, TS))],
        out_specs=[full((n, WIN, TS))] * 2,
        scratch_shapes=[pltpu.VMEM((NT * TS, TS), f32)] * 2,
        out_shape=[sds((n, WIN, TS), f32), sds((n, WIN, TS), bf)],
        compiler_params=params(60),
        cost_estimate=cost(4 * TS * TS, 40 * TS * TS),
        name="place",
    )(x)


def turn(v):
    return v.reshape(2, 3, WIN, WIN, TS).transpose(0, 2, 1, 3, 4).reshape(2, WIN, 3 * WIN, TS)


def pad_body(w_ref, q_ref, p_ref):
    rows = w_ref.shape[0]
    w = w_ref[...]
    zero = jnp.zeros((rows, HP - HDIM), bf)
    for h in range(3 * HL):
        q_ref[:, h * HP : (h + 1) * HP] = jnp.concatenate([w[:, h * HDIM : (h + 1) * HDIM], zero], axis=1)
    for h in range(HL):
        s = 3 * HL + h
        p_ref[:, h * HP : (h + 1) * HP] = jnp.concatenate([w[:, s * HDIM : (s + 1) * HDIM], zero], axis=1)


def pad_call(g1):
    rb = 160
    return pl.pallas_call(
        pad_body,
        grid=(D // rb,),
        in_specs=[pl.BlockSpec((rb, D), lambda i: (i, 0))],
        out_specs=[
            pl.BlockSpec((rb, 3 * HL * HP), lambda i: (i, 0)),
            pl.BlockSpec((rb, HL * HP), lambda i: (i, 0)),
        ],
        out_shape=[sds((D, 3 * HL * HP), bf), sds((D, HL * HP), bf)],
        compiler_params=params(),
        cost_estimate=cost(D * 2048, 2 * D * (1280 + 2048)),
        name="padw",
    )(g1)


def block_of(me, j):
    return lax.rem(me + j, NT)


def qkv_body(x_ref, w_ref, b_ref, o_ref):
    o_ref[...] = (dot(x_ref[...], w_ref[...]) + b_ref[...]).astype(bf)


def qkv_call(x, w, bias):
    n = w.shape[1]
    tn = 512
    rows = x.shape[0]
    return pl.pallas_call(
        qkv_body,
        grid=(n // tn,),
        in_specs=[
            full((rows, D)),
            pl.BlockSpec((D, tn), lambda i: (0, i)),
            pl.BlockSpec((1, tn), lambda i: (0, i)),
        ],
        out_specs=pl.BlockSpec((rows, tn), lambda i: (0, i)),
        out_shape=sds((rows, n), bf),
        compiler_params=params(24),
        cost_estimate=cost(2 * rows * D * n, 2 * (rows * D + D * n + rows * n)),
        name="qkv",
    )(x, w, bias)


def gatt_body(*refs):
    count = len(refs) - 4
    w_ref, o_ref = refs[1 + count], refs[-1]
    for t in range(count):

        @pl.when(pl.program_id(0) == t)
        def _(t=t):
            o_ref[0] = dot(refs[1 + t][...], w_ref[...]).astype(bf)


def gatt_call(me, which, xs, w, into):
    n = w.shape[1]
    k = len(which)
    first, step = which[0], which[-1] - which[0]
    return pl.pallas_call(
        gatt_body,
        grid_spec=pltpu.PrefetchScalarGridSpec(
            num_scalar_prefetch=1,
            grid=(k,),
            in_specs=[pl.BlockSpec((TS, D), lambda t, m: (0, 0))] * k
            + [pl.BlockSpec((D, n), lambda t, m: (0, 0)), ANY],
            out_specs=pl.BlockSpec((1, TS, n), lambda t, m: (block_of(m[0], first + step * t), 0, 0)),
        ),
        out_shape=sds((NT, TS, n), bf),
        input_output_aliases={2 + k: 0},
        compiler_params=params(),
        cost_estimate=cost(2 * k * TS * D * n, 2 * (k * TS * D + D * n + k * TS * n)),
        name="gatt",
    )(me, *xs, w, into)


def gatt2_body(me_ref, a_ref, b_ref, w_ref, z_ref, o_ref, p_ref):
    p_ref[:HALF] = a_ref[...]
    p_ref[HALF:] = b_ref[...]
    o_ref[0] = dot(p_ref[...], w_ref[...]).astype(bf)


def gatt2_call(me, halves, w, into):
    n = w.shape[1]
    half = pl.BlockSpec((HALF, D), lambda i, m: (0, 0))
    return pl.pallas_call(
        gatt2_body,
        grid_spec=pltpu.PrefetchScalarGridSpec(
            num_scalar_prefetch=1,
            grid=(1,),
            in_specs=[half, half, pl.BlockSpec((D, n), lambda i, m: (0, 0)), ANY],
            out_specs=[
                pl.BlockSpec((1, TS, n), lambda i, m: (block_of(m[0], 2), 0, 0)),
                pl.BlockSpec((TS, D), lambda i, m: (0, 0)),
            ],
        ),
        out_shape=[sds((NT, TS, n), bf), sds((TS, D), bf)],
        input_output_aliases={4: 0},
        compiler_params=params(),
        cost_estimate=cost(2 * TS * D * n, 2 * (2 * TS * D + D * n + TS * n)),
        name="gatt",
    )(me, *halves, w, into)


def attn_body(qkv_ref, tab_ref, sel_ref, mask_ref, sp_ref, km_ref, z_ref, o_ref, p_ref, t_ref):
    @pl.when(pl.program_id(0) == 0)
    def _():
        t_ref[...] = dot(sel_ref[...], tab_ref[...]).astype(bf)

    qs = [qkv_ref[:, h * HP : (h + 1) * HP] for h in range(HL)]
    along = dot_nt(jnp.concatenate(qs, axis=0), t_ref[...])
    mask = mask_ref[...].astype(f32)
    along = jnp.concatenate([(along[h * WR : (h + 1) * WR] * mask).astype(bf) for h in range(HL)], axis=0)
    bias = dot(along, sp_ref[...])
    for h in range(HL):
        k = qkv_ref[:, (HL + h) * HP : (HL + h + 1) * HP]
        v = qkv_ref[:, (2 * HL + h) * HP : (2 * HL + h + 1) * HP]
        s = dot_nt(qs[h], k) * SCALE + bias[h * WR : (h + 1) * WR] + km_ref[...]
        top = jnp.max(s, axis=1, keepdims=True)
        e = jnp.exp(s - top)
        p = (e * (1.0 / jnp.sum(e, axis=1, keepdims=True))).astype(bf)
        p_ref[0, h] = p
        o_ref[:, h * HP : (h + 1) * HP] = dot(p, v).astype(bf)


def attn_call(qkv, tab, sel, mask, spread, keys, into):
    n = 3 * HL * HP
    return pl.pallas_call(
        attn_body,
        grid=(NW,),
        in_specs=[
            pl.BlockSpec((WR, n), lambda i: (i, 0)),
            full((64, HP)),
            full((512, 64)),
            full((WR, 512)),
            full((512, WR)),
            full((1, WR)),
            ANY,
        ],
        out_specs=[
            pl.BlockSpec((WR, HL * HP), lambda i: (i, 0)),
            pl.BlockSpec((1, HL, WR, WR), lambda i: (i, 0, 0, 0)),
        ],
        out_shape=[sds((NT * TS, HL * HP), bf), sds((NW, HL, WR, WR), bf)],
        scratch_shapes=[pltpu.VMEM((512, HP), bf)],
        input_output_aliases={6: 0},
        compiler_params=params(),
        cost_estimate=cost(24 * 6 * 2 * WR * WR * 256, 8e6, 24 * WR * 256),
        name="attn",
    )(qkv, tab, sel, mask, spread, keys, into)


def attnb_body(qkv_ref, p_ref, ga_ref, tab_ref, sel_ref, mask_ref, sp_ref, z_ref, o_ref, rel_ref, bias_ref, t_ref):
    @pl.when(pl.program_id(0) == 0)
    def _():
        t_ref[...] = dot(sel_ref[...], tab_ref[...]).astype(bf)
        rel_ref[...] = jnp.zeros_like(rel_ref)
        bias_ref[...] = jnp.zeros_like(bias_ref)

    table = t_ref[...]
    mask = mask_ref[...].astype(f32)
    qs, all_ds = [], []
    for h in range(HL):
        cq = slice(h * HP, (h + 1) * HP)
        cv = slice((2 * HL + h) * HP, (2 * HL + h + 1) * HP)
        ga = ga_ref[:, cq]
        p = p_ref[0, h]
        pf = p.astype(f32)
        gs = dot_nt(ga, qkv_ref[:, cv])
        delta = jnp.sum(pf * gs, axis=1, keepdims=True)
        all_ds.append((pf * (gs - delta)).astype(bf))
        qs.append(qkv_ref[:, cq])
        gv = dot_tn(p, ga).astype(bf)
        o_ref[:, cv] = gv
        bias_ref[:, cv] += colsum(gv.astype(f32))
    sums = dot_nt(jnp.concatenate(all_ds, axis=0), sp_ref[...])
    sums = jnp.concatenate([(sums[h * WR : (h + 1) * WR] * mask).astype(bf) for h in range(HL)], axis=0)
    gq_rel = dot(sums, table)
    rel_ref[...] += dot_tn(sums, jnp.concatenate(qs, axis=0))
    for h in range(HL):
        cq = slice(h * HP, (h + 1) * HP)
        ck = slice((HL + h) * HP, (HL + h + 1) * HP)
        ds = all_ds[h]
        o_ref[:, ck] = (dot_tn(ds, qs[h]) * SCALE).astype(bf)
        gq = (dot(ds, qkv_ref[:, ck]) * SCALE + gq_rel[h * WR : (h + 1) * WR]).astype(bf)
        o_ref[:, cq] = gq
        bias_ref[:, cq] += colsum(gq.astype(f32))


def attnb_call(qkv, p, ga, tab, sel, mask, spread, into):
    n = 3 * HL * HP
    return pl.pallas_call(
        attnb_body,
        grid=(NW,),
        in_specs=[
            pl.BlockSpec((WR, n), lambda i: (i, 0)),
            pl.BlockSpec((1, HL, WR, WR), lambda i: (i, 0, 0, 0)),
            pl.BlockSpec((WR, HL * HP), lambda i: (i, 0)),
            full((64, HP)),
            full((512, 64)),
            full((WR, 512)),
            full((512, WR)),
            ANY,
        ],
        out_specs=[pl.BlockSpec((WR, n), lambda i: (i, 0)), full((512, HP)), full((1, n))],
        out_shape=[sds((NT * TS, n), bf), sds((512, HP), f32), sds((1, n), f32)],
        scratch_shapes=[pltpu.VMEM((512, HP), bf)],
        input_output_aliases={7: 0},
        compiler_params=params(),
        cost_estimate=cost(24 * 10 * 2 * WR * WR * 256, 14e6),
        name="attnb",
    )(qkv, p, ga, tab, sel, mask, spread, into)


def partial_body(me_ref, a_ref, w_ref, *refs):
    w = w_ref[...]
    if len(refs) == 5:
        n_ref, (r0, r1, r2a, r2b, r3) = None, refs
    else:
        n_ref, keep_ref, r0, r1, r2a, r2b, r3, gg_ref, gb_ref = refs
    gain = bias = 0.0
    for j, ref in ((2, None), (1, r1), (3, r3), (0, r0)):
        t = block_of(me_ref[0], j)
        r = dot_nt(a_ref[t], w)
        if n_ref is not None:
            gain = gain + colsum(r * n_ref[t].astype(f32))
            bias = bias + colsum(r * keep_ref[t])
        if ref is None:
            r2a[...] = r[:HALF].astype(bf)
            r2b[...] = r[HALF:].astype(bf)
        else:
            ref[...] = r.astype(ref.dtype)
    if n_ref is not None:
        gg_ref[...] = gain
        gb_ref[...] = bias


def partial_call(me, a, w, name, norm=()):
    k = a.shape[2]
    tn = 256
    whole = pl.BlockSpec((TS, tn), lambda i, m: (0, i))
    half = pl.BlockSpec((HALF, tn), lambda i, m: (0, i))
    ins = [pl.BlockSpec((NT, TS, tn), lambda i, m: (0, 0, i)), pl.BlockSpec((NT, TS, 1), lambda i, m: (0, 0, 0))]
    outs = [whole, whole, half, half, whole]
    shapes = [sds((TS, D), f32), sds((TS, D), bf), sds((HALF, D), bf), sds((HALF, D), bf), sds((TS, D), bf)]
    if norm:
        outs += [pl.BlockSpec((1, tn), lambda i, m: (0, i))] * 2
        shapes += [sds((1, D), f32)] * 2
    return pl.pallas_call(
        partial_body,
        grid_spec=pltpu.PrefetchScalarGridSpec(
            num_scalar_prefetch=1,
            grid=(D // tn,),
            in_specs=[
                pl.BlockSpec((NT, TS, k), lambda i, m: (0, 0, 0)),
                pl.BlockSpec((tn, k), lambda i, m: (i, 0)),
            ]
            + ins[: len(norm)],
            out_specs=outs,
        ),
        out_shape=shapes,
        compiler_params=params(24),
        cost_estimate=cost(2 * NT * TS * D * k, 2 * (NT * TS * k + D * k + 9 * TS * D)),
        name=name,
    )(me, a, w, *norm)


def merge_body(r1, a, r3, b, s1, s3):
    s1[...] = (r1[...].astype(f32) + a[...].astype(f32)).astype(bf)
    s3[...] = (r3[...].astype(f32) + b[...].astype(f32)).astype(bf)


def merge_call(r1, a, r3, b, mb=16):
    one = pl.BlockSpec((HALF, D), lambda i: (0, 0))
    two = pl.BlockSpec((HALF, D), lambda i: (1, 0))
    return pl.pallas_call(
        merge_body,
        grid=(1,),
        in_specs=[one, one, two, one],
        out_specs=[one, two],
        out_shape=[sds((TS, D), bf)] * 2,
        input_output_aliases={0: 0, 2: 1},
        compiler_params=params(mb),
        cost_estimate=cost(4 * HALF * D, 12 * HALF * D),
        name="merge",
    )(r1, a, r3, b)


def mlp_body(halved, k, *refs):
    ins = refs[: 2 if halved else k]
    gb_refs = refs[len(ins) : len(ins) + k]
    w1_ref, w2_ref, b1_ref = refs[len(ins) + k : len(ins) + k + 3]
    outs = refs[len(ins) + k + 3 : -4]
    z_s, gb_s, br_s, gn_s = refs[-4:]
    step = pl.program_id(0)

    @pl.when(step == 0)
    def _():
        br_s[...] = jnp.zeros_like(br_s)
        gn_s[...] = jnp.zeros_like(gn_s)
        rows = k * TS // len(ins)
        for t, ref in enumerate(ins):
            z_s[t * rows : (t + 1) * rows] = ref[...]
        for t, ref in enumerate(gb_refs):
            gb_s[t * TS : (t + 1) * TS] = ref[0]

    w1 = w1_ref[...]
    w2 = w2_ref[...]
    pre = dot(z_s[...], w1) + b1_ref[...]
    ga = dot(gb_s[...], w2)
    cdf = 0.5 + 0.5 * lax.erf(pre * 0.7071067811865476)
    act = (pre * cdf).astype(bf)
    slope = cdf + pre * (0.3989422804014327 * jnp.exp(-0.5 * pre * pre))
    gp = (ga * slope).astype(bf)
    for t in range(k):
        rows = slice(t * TS, (t + 1) * TS)
        outs[3 * t][...] = act[rows]
        outs[3 * t + 1][...] = gp[rows]
        outs[3 * t + 2][...] = colsum(gp[rows].astype(f32))
    br_s[...] += dot_nt(act, w2)
    gn_s[...] += dot_nt(gp, w1)

    @pl.when(step == pl.num_programs(0) - 1)
    def _():
        rest = outs[3 * k :]
        for total, refs_out in ((br_s, rest[0::2]), (gn_s, rest[1::2])):
            at = 0
            for ref in refs_out:
                if at < total.shape[0]:
                    ref[...] = total[at : at + ref.shape[0]].astype(ref.dtype)
                    at += ref.shape[0]
        if halved:
            rest[4][...] = z_s[...]


def mlp_call(which, zs, gb, w, b1, kind):
    halved = which == (2,)
    k = len(which)
    tf = 256
    nf = D // tf
    col = pl.BlockSpec((TS, tf), lambda i: (0, i))
    bias = pl.BlockSpec((1, tf), lambda i: (0, i))
    half = full((HALF, D))
    block = full((TS, D))
    outs = [col, col, bias] * k
    shapes = [sds((TS, D), bf), sds((TS, D), bf), sds((1, D), f32)] * k
    if halved:
        outs += [half] * 4 + [block]
        shapes += [sds((HALF, D), bf)] * 4 + [sds((TS, D), bf)]
    else:
        outs += [block] * (2 * k)
        shapes += [sds((TS, D), kind)] * (2 * k)
    return pl.pallas_call(
        partial(mlp_body, halved, k),
        grid=(nf,),
        in_specs=[half if halved else block] * len(zs)
        + [pl.BlockSpec((1, TS, D), lambda i, j=j: (j, 0, 0)) for j in which]
        + [
            pl.BlockSpec((D, tf), lambda i: (0, i)),
            pl.BlockSpec((D, tf), lambda i: (0, i + nf)),
            bias,
        ],
        out_specs=outs,
        out_shape=shapes,
        scratch_shapes=[pltpu.VMEM((k * TS, D), bf)] * 2 + [pltpu.VMEM((k * TS, D), f32)] * 2,
        compiler_params=params(32),
        cost_estimate=cost(k * 8 * TS * D * D, 4 * D * D + k * 12 * TS * D, k * 2 * TS * D),
        name="mlp",
    )(*zs, *[gb] * k, w, w, b1)


NG = 2 * D


def tokgrad_body(*refs):
    o_ref = refs[-1]
    lhs, rhs = refs[:4], refs[4:8]
    total = None
    for j in range(NT):
        left = lhs[j][0] if len(lhs[j].shape) == 3 else lhs[j][...]
        part = dot_tn(left, rhs[j][...])
        total = part if total is None else total + part
    o_ref[...] = total.astype(bf)


def tokgrad_call(lhs, rhs, into, at):
    td = 256
    if len(lhs) == 1:
        left = [pl.BlockSpec((1, TS, td), lambda i, j=j: (j, 0, i)) for j in range(NT)]
        lhs = list(lhs) * NT
    else:
        left = [pl.BlockSpec((TS, td), lambda i: (0, i))] * NT
    return pl.pallas_call(
        tokgrad_body,
        grid=(D // td,),
        in_specs=left + [full((TS, D))] * NT + [ANY] * (into is not None),
        out_specs=pl.BlockSpec((td, D), lambda i: (i, at)),
        out_shape=sds((D, NG), bf),
        input_output_aliases={} if into is None else {2 * NT: 0},
        compiler_params=params(24),
        cost_estimate=cost(8 * TS * D * D, 2 * (8 * TS * D + D * D)),
        name="fcgrad",
    )(*lhs, *rhs, *(() if into is None else (into,)))


def narrow(x, heads):
    return jnp.concatenate([x[:, h * HP : h * HP + HDIM] for h in range(heads)], axis=1)


def qpgrad_body(me_ref, e_ref, dq_ref, p0, p1, p2, p3, a_ref, o_ref):
    o_ref[:, : 3 * HL * HDIM] = narrow(dot_tn(e_ref[...], dq_ref[...]), 3 * HL).astype(bf)
    total = None
    for j, p in enumerate((p0, p1, p2, p3)):
        part = dot_tn(p[...], a_ref[block_of(me_ref[0], j)])
        total = part if total is None else total + part
    o_ref[:, 3 * HL * HDIM :] = narrow(total, HL).astype(bf)


def qpgrad_call(me, e, dqkv, p, att4):
    td = 256
    rows, n = dqkv.shape
    k = att4.shape[2]
    return pl.pallas_call(
        qpgrad_body,
        grid_spec=pltpu.PrefetchScalarGridSpec(
            num_scalar_prefetch=1,
            grid=(D // td,),
            in_specs=[
                pl.BlockSpec((rows, td), lambda i, m: (0, i)),
                pl.BlockSpec((rows, n), lambda i, m: (0, 0)),
            ]
            + [pl.BlockSpec((TS, td), lambda i, m: (0, i))] * 4
            + [pl.BlockSpec((NT, TS, k), lambda i, m: (0, 0, 0))],
            out_specs=pl.BlockSpec((td, D), lambda i, m: (i, 0)),
        ),
        out_shape=sds((D, D), bf),
        compiler_params=params(24),
        cost_estimate=cost(2 * rows * D * (n + k), 2 * (2 * rows * D + rows * (n + k) + D * D)),
        name="qpgrad",
    )(me, e, dqkv, *p, att4)


UP = [(i, (i + 1) % NT) for i in range(NT)]
DOWN = [(i, (i - 1) % NT) for i in range(NT)]


def up(v):
    return lax.ppermute(v, "tp", UP)


def down(v):
    return lax.ppermute(v, "tp", DOWN)


def after(v, *deps):
    return lax.optimization_barrier((v, deps))[0]


def ring_gather(own, first=None, between=None):
    b3 = up(own)
    b1 = down(own)
    if first is not None:
        b3, b1, first = lax.optimization_barrier((b3, b1, first))
    half = own.shape[0] // 2
    u, d = up(b3[:half]), down(b1[half:])
    if between is not None:
        first = between(b1, b3, first)
        u, d, first = lax.optimization_barrier((u, d, first))
    return (own, b1, u, d, b3), first


def ring_scatter(r1, r2a, r2b, r3, first=None, mb=16):
    a = up(r2a)
    b = down(r2b)
    if first is not None:
        a, b, first = lax.optimization_barrier((a, b, first))
    s1, s3 = merge_call(r1, a, r3, b, mb)
    return (s3, s1), first


def ring_finish(sums):
    return down(sums[0]), up(sums[1])


def shard_place():
    s = lax.axis_index("shard")
    return s // 4, (s // 2) % 2, s % 2


def shard_move(v, f):
    return lax.ppermute(v, "shard", [(i, f(i)) for i in range(16)])


def pick(v, i, ax):
    return lax.dynamic_index_in_dim(v, i, ax, keepdims=False)


def add_low(p, q):
    return (p.astype(f32) + q.astype(f32)).astype(bf)


def over_shard_1(v):
    n = v.shape[1]
    y, zl, core = shard_place()
    v = v.reshape(4, 2, 2, 80, n)
    v = add_low(pick(v, core, 2), shard_move(pick(v, 1 - core, 2), lambda i: i ^ 1))
    w = [pick(v, (y + j) % 4, 0) for j in range(4)]
    a = shard_move(w[2][0], lambda i: (i + 4) % 16)
    b = shard_move(w[2][1], lambda i: (i + 12) % 16)
    return w[0], jnp.stack([add_low(w[1][0], a), w[1][1]]), jnp.stack([w[3][0], add_low(w[3][1], b)])


def over_shard_2(parts):
    w0, s1, s3 = parts
    return w0, shard_move(s3, lambda i: (i + 12) % 16), shard_move(s1, lambda i: (i + 4) % 16)


def over_shard_3(parts):
    w0, c1, c3 = parts
    y, zl, core = shard_place()
    v = (w0.astype(f32) + c1.astype(f32) + c3.astype(f32)).astype(bf)
    return pick(v, zl, 0), shard_move(pick(v, 1 - zl, 0), lambda i: i ^ 2)


def over_ctx(v):
    return v.astype(f32) + lax.ppermute(v, "ctx", [(0, 1), (1, 0)]).astype(f32)


def small_pack(parts):
    out = []
    for part in parts:
        v = jnp.concatenate([a.ravel() for a in part])
        out.append(jnp.pad(v, (0, -v.size % 1024)).reshape(-1, 128))
    return jnp.concatenate(out, axis=0).astype(bf)


def small_sum(everyone):
    return jnp.sum(everyone.astype(f32), axis=0)


def small_split(both, world):
    rows = -(-sum(a.size for a in world) // 1024) * 8
    return both[:rows], both[rows:]


def pair_sum(w, step):
    return w + lax.ppermute(w, "tp", [(i, i ^ step) for i in range(NT)])


def small_finish(w, g, world, group):
    out = []
    for part, flat in ((world, w.ravel()), (group, g.ravel())):
        at = 0
        for a in part:
            out.append(flat[at : at + a.size].reshape(a.shape))
            at += a.size
    return out


def from_everyone(array, axis):
    size = lax.axis_size(axis)
    return lax.all_to_all(jnp.broadcast_to(array[None], (size, *array.shape)), axis, 0, 0, tiled=True)


def windows(grid):
    n = grid.shape[-1]
    w = grid.reshape(2, WIN, 3, WIN, n).transpose(0, 2, 1, 3, 4).reshape(NW, CELLS, n)
    w = jnp.pad(w, ((0, 0), (0, WR - CELLS), (0, 0))).reshape(NW * WR, n)
    return jnp.pad(w, ((0, NT * TS - NW * WR), (0, 0))).reshape(NT, TS, n)


def local(
    tokens,
    valid_mask,
    ln1_gain,
    ln1_bias,
    qkv_weight,
    qkv_bias,
    rel_rows,
    rel_cols,
    proj_weight,
    proj_bias,
    ln2_gain,
    ln2_bias,
    fc1_weight,
    fc1_bias,
    fc2_weight,
    fc2_bias,
    cotangent,
):
    tp_index = lax.axis_index("tp")
    me = tp_index.astype(jnp.int32).reshape(1)
    sel, mask, spread, keys = rel_constants()
    sel = jnp.asarray(sel, bf)
    mask = jnp.asarray(mask, bf)
    spread = jnp.asarray(spread, bf)
    keys = jnp.asarray(keys, f32)
    row = lambda v: v.reshape(1, -1)

    own1 = jnp.concatenate([jnp.moveaxis(qkv_weight, 1, 0).reshape(80, 960), proj_weight.T], axis=1)
    own2 = jnp.concatenate([fc1_weight, fc2_weight.T], axis=1)
    all1 = lax.all_gather(own1, "shard", axis=0, tiled=True)
    all2 = lax.all_gather(own2, "shard", axis=0, tiled=True)
    bias_q = jnp.pad(qkv_bias.reshape(2, HL, HDIM), ((0, 0), (0, 0), (0, HP - HDIM))).reshape(2, HL * HP)
    bias_p = row(jnp.concatenate([bias_q[0], jnp.zeros((HL * HP,), f32), bias_q[1]]))
    tab = jnp.zeros((64, HP), bf).at[:RELS, :HDIM].set(rel_rows).at[32 : 32 + RELS, :HDIM].set(rel_cols)

    keep4 = windows(valid_mask.astype(f32)[..., None])
    keep = lax.dynamic_index_in_dim(keep4, tp_index, 0, keepdims=False)
    toks, (qkvp, projp) = ring_gather(windows(tokens), None, lambda b1, b3, _: pad_call(all1))
    x, e4, n4 = ln1_call(me, toks, keep4, row(ln1_gain), row(ln1_bias))
    ents = e4.reshape(NT * TS, D)
    cot = after(windows(cotangent), toks[2], toks[3])
    cot3, cot1 = up(cot), down(cot)
    cot3, cot1, flat = lax.optimization_barrier((cot3, cot1, qkv_call(ents, qkvp, bias_p)))
    cots = (cot, cot1, up(cot3), cot3)
    att, probs = attn_call(flat, tab, sel, mask, spread, keys, jnp.zeros((NT * TS, HL * HP), bf))
    att4 = att.reshape(NT, TS, HL * HP)
    r0, *rest = partial_call(me, att4, projp, "proj")
    rest, cots = lax.optimization_barrier((rest, cots))
    sums, _ = ring_scatter(*rest, None, 60)
    c, gb, sum_fc2_bias = cot_call(me, cots, keep4)
    (c1, c3), gb = lax.optimization_barrier((ring_finish(sums), gb))
    h, z = ln2_call(r0, c1, c3, x, keep, row(proj_bias), row(ln2_gain), row(ln2_bias))

    b1row = row(fc1_bias)
    mlp = lambda which, zz, kind: mlp_call(which, zz, gb, all2, b1row, kind)
    zs, (m0, m13) = ring_gather(
        z, mlp((0,), (z,), f32), lambda b1, b3, first: (first, mlp((1, 3), (b1, b3), bf))
    )
    act0, gpre0, fb0, br0, gn0 = m0
    act1, gpre1, fb1, act3, gpre3, fb3, br1, gn1, br3, gn3 = m13
    act2, gpre2, fb2, br2a, gn2a, br2b, gn2b, z2 = mlp((2,), (zs[2], zs[3]), bf)
    gpres = (gpre0, gpre1, gpre2, gpre3)
    sum_fc1_bias = fb0 + fb1 + fb2 + fb3
    sums, grads = ring_scatter(gn1, gn2a, gn2b, gn3, tokgrad_call((gb,), (act0, act1, act2, act3), None, 1))
    grads = tokgrad_call((z, zs[1], z2, zs[4]), gpres, grads, 0)
    (c1, c3), grads = lax.optimization_barrier((ring_finish(sums), grads))
    own_fc = lax.psum_scatter(grads, "shard", scatter_dimension=0, tiled=True)
    gh, gproj, sum_ln2_gain, sum_ln2_bias, sum_proj_bias = ln2b_call(
        gn0, c1, c3, h, c, keep, row(ln2_gain)
    )
    ga = gatt_call(me, (0,), (gproj,), projp, jnp.zeros((NT, TS, HL * HP), bf))
    gps, ga = ring_gather(gproj, ga, lambda b1, b3, ga: gatt_call(me, (1, 3), (b1, b3), projp, ga))
    ga, gp2 = gatt2_call(me, gps[2:4], projp, ga)

    branch = after((br1, br2a, br2b, br3), gp2)
    dqkv, rel, sum_qkv_bias = attnb_call(
        flat,
        probs,
        ga.reshape(NT * TS, HL * HP),
        tab,
        sel,
        mask,
        spread,
        jnp.zeros((NT * TS, 3 * HL * HP), bf),
    )
    sums, dqkv = ring_scatter(*branch, dqkv)
    sums, dqkv = lax.optimization_barrier((sums, dqkv))
    f1, f3 = ring_finish(sums)
    r0, r1, r2a, r2b, r3, sum_ln1_gain, sum_ln1_bias = partial_call(
        me, dqkv.reshape(NT, TS, 3 * HL * HP), qkvp, "gnorm1", (n4, keep4)
    )
    gradq = qpgrad_call(me, ents, dqkv, (gproj, gps[1], gp2, gps[4]), att4)
    gradq, f1, f3 = lax.optimization_barrier((gradq, f1, f3))
    sums, gradq = ring_scatter(r1, r2a, r2b, r3, gradq, 60)
    c1, c3 = ring_finish(sums)
    parts = over_shard_1(after(gradq, sums))
    res = result_call(br0, f1, f3, h, keep, row(fc2_bias))
    small = after(
        (
            rel,
            sum_qkv_bias,
            sum_fc1_bias,
            sum_ln1_gain,
            sum_ln1_bias,
            sum_ln2_gain,
            sum_ln2_bias,
            sum_proj_bias,
            sum_fc2_bias,
        ),
        sums,
    )
    rels = jnp.dot(sel.astype(f32).T, small[0], precision=lax.Precision.HIGHEST)
    qb = small[1].reshape(3, HL, HP)[:, :, :HDIM]
    world = [*small[3:], rels[:RELS, :HDIM], rels[32 : 32 + RELS, :HDIM]]
    group = [qb[0], qb[2], small[2]]
    everyone = from_everyone(small_pack((world, group)), ("shard", "ctx"))
    c1, c3, res, everyone, parts = lax.optimization_barrier((c1, c3, res, everyone, parts))
    parts = over_shard_2(parts)
    out = ln1b_call(r0, c1, c3, x, gh, keep, row(ln1_gain), res)
    out, parts, fc = lax.optimization_barrier((out, parts, over_ctx(own_fc)))
    w, g = small_split(small_sum(after(everyone, out)), world)
    blocks = lax.all_to_all(out, "tp", 0, 0, tiled=True)
    half, other = over_shard_3(parts)
    q = over_ctx(add_low(half, other))
    blocks, q, w = lax.optimization_barrier((blocks, q, pair_sum(w, 1)))
    w = pair_sum(w, 3)
    g_ln1g, g_ln1b, g_ln2g, g_ln2b, g_pb, g_f2b, g_rr, g_rc, g_q, g_v, g_f1b = small_finish(w, g, world, group)
    token_grads, result = place_call(blocks)
    token_grads, result = turn(token_grads), turn(result)
    return (
        result,
        token_grads,
        g_ln1g.ravel(),
        g_ln1b.ravel(),
        jnp.moveaxis(q[:, : 3 * HL * HDIM].reshape(80, 3, 320), 0, 1),
        jnp.stack([g_q.ravel(), g_v.ravel()]),
        g_rr,
        g_rc,
        q[:, 3 * HL * HDIM :].T,
        g_pb.ravel(),
        g_ln2g.ravel(),
        g_ln2b.ravel(),
        fc[:, :D],
        g_f1b.ravel(),
        fc[:, D:].T,
        g_f2b.ravel(),
    )


def solution(mesh):
    cells = P("shard", "ctx", None, "tp")
    in_specs = (
        cells,
        P("shard", "ctx", None),
        P(),
        P(),
        P(None, "shard", "tp"),
        P(None, "tp"),
        P(),
        P(),
        P("tp", "shard"),
        P(),
        P(),
        P(),
        P("shard", "tp"),
        P("tp"),
        P("tp", "shard"),
        P(),
        cells,
    )
    out_specs = (
        cells,
        cells,
        P(),
        P(),
        P(None, "shard", "tp"),
        P(None, "tp"),
        P(),
        P(),
        P("tp", "shard"),
        P(),
        P(),
        P(),
        P("shard", "tp"),
        P("tp"),
        P("tp", "shard"),
        P(),
    )
    return jax.shard_map(local, mesh=mesh, in_specs=in_specs, out_specs=out_specs, check_vma=False)
```

```python
from functools import partial

import jax
import jax.numpy as jnp
import numpy as np
from jax import lax
from jax.experimental import pallas as pl
from jax.experimental.pallas import tpu as pltpu
from jax.sharding import PartitionSpec as P

HEADS = 16
HDIM = 80
WIN = 14
D = 1280
NT = 4
HL = HEADS // NT
CELLS = WIN * WIN
WR = 208
NW = 6
TS = 320
HALF = TS // 2
HP = 128
RELS = 2 * WIN - 1
EPS = 1e-06
SCALE = HDIM ** (-0.5)
bf = jnp.bfloat16
f32 = jnp.float32
MB = 1024 * 1024


def rel_constants():
    sel = np.zeros((512, 64), np.float32)
    mask = np.zeros((WR, 512), np.float32)
    spread = np.zeros((512, WR), np.float32)
    for a in range(WIN):
        for x in range(WIN):
            sel[a * WIN + x, a - x + WIN - 1] = 1
            sel[256 + a * WIN + x, 32 + a - x + WIN - 1] = 1
    for a in range(WIN):
        for b in range(WIN):
            row = a * WIN + b
            mask[row, a * WIN : a * WIN + WIN] = 1
            mask[row, 256 + b * WIN : 256 + b * WIN + WIN] = 1
    for a in range(WIN):
        for x in range(WIN):
            for y in range(WIN):
                spread[a * WIN + x, x * WIN + y] = 1
                spread[256 + a * WIN + y, x * WIN + y] = 1
    keys = np.where(np.arange(WR) < CELLS, 0.0, -1e30).astype(np.float32)[None]
    return sel, mask, spread, keys


def dot(a, b):
    return lax.dot_general(a, b, (((1,), (0,)), ((), ())), preferred_element_type=f32)


def dot_nt(a, b):
    return lax.dot_general(a, b, (((1,), (1,)), ((), ())), preferred_element_type=f32)


def dot_tn(a, b):
    return lax.dot_general(a, b, (((0,), (0,)), ((), ())), preferred_element_type=f32)


def params(mb=16):
    return pltpu.CompilerParams(vmem_limit_bytes=mb * MB)


def cost(flops, nbytes, trans=0):
    return pl.CostEstimate(flops=int(flops), bytes_accessed=int(nbytes), transcendentals=int(trans))


def sds(shape, dtype):
    return jax.ShapeDtypeStruct(shape, dtype)


def full(shape):
    return pl.BlockSpec(shape, lambda *g: (0,) * len(shape))


ANY = pl.BlockSpec(memory_space=pl.ANY)


def stats(x):
    mean = jnp.sum(x, axis=1, keepdims=True) * (1.0 / D)
    xc = x - mean
    var = jnp.sum(xc * xc, axis=1, keepdims=True) * (1.0 / D)
    inv = lax.rsqrt(var + EPS)
    return xc * inv, inv


def colsum(x):
    return jnp.sum(x, axis=0, keepdims=True)


def acc_out(ref, value):
    @pl.when(pl.program_id(0) == 0)
    def _():
        ref[...] = jnp.zeros_like(ref)

    ref[...] += value


RB = 160


def in_feature_order(me, t, refs, use):
    if len(refs) == 5:
        r0, r1, ra, rb, r3 = refs
        r2 = jnp.where(t < NT // 2, ra[0].astype(f32), rb[0].astype(f32))
    else:
        r0, r1, r2, r3 = refs
        r2 = r2[0].astype(f32)
    parts = (r0[0].astype(f32), r1[0].astype(f32), r2, r3[0].astype(f32))
    for k in range(NT):

        @pl.when(me == k)
        def _(k=k):
            use(jnp.concatenate([parts[(b - k) % NT] for b in range(NT)], axis=1))


def ln1_body(me_ref, r0, r1, ra, rb, r3, keep_ref, g_ref, b_ref, x_ref, e_ref, n_ref):
    me = me_ref[0]
    j = pl.program_id(0)

    def use(x):
        n, _ = stats(x)
        e_ref[0] = (keep_ref[0] * (n * g_ref[...] + b_ref[...])).astype(bf)
        n_ref[0] = (keep_ref[0] * n).astype(bf)

        @pl.when(j == 0)
        def _():
            x_ref[...] = x.astype(bf)

    in_feature_order(me, block_of(me, j), (r0, r1, ra, rb, r3), use)


def cot_body(me_ref, r0, r1, r2, r3, keep_ref, c_ref, gb_ref, fb_ref):
    me = me_ref[0]
    j = pl.program_id(0)

    @pl.when((j == 0) & (pl.program_id(1) == 0))
    def _():
        fb_ref[...] = jnp.zeros_like(fb_ref)

    def use(c):
        gb = keep_ref[0] * c
        gb_ref[0] = gb.astype(bf)

        @pl.when(j == 0)
        def _():
            c_ref[...] = c.astype(bf)
            fb_ref[...] += colsum(gb)

    in_feature_order(me, block_of(me, j), (r0, r1, r2, r3), use)


def raw_specs():
    steps = TS // RB
    blk = pl.BlockSpec((1, RB, TS), lambda j, i, m: (block_of(m[0], j), i, 0))
    lo = pl.BlockSpec((1, RB, TS), lambda j, i, m: (jnp.minimum(block_of(m[0], j), 1), i, 0))
    hi = pl.BlockSpec((1, RB, TS), lambda j, i, m: (jnp.maximum(block_of(m[0], j) - 2, 0), i, 0))
    keep = pl.BlockSpec((1, RB, 1), lambda j, i, m: (block_of(m[0], j), i, 0))
    mine = pl.BlockSpec((RB, D), lambda j, i, m: (jnp.minimum(j * steps + i, steps - 1), 0))
    vec = pl.BlockSpec((1, D), lambda j, i, m: (0, 0))
    return (NT, steps), [blk, blk, lo, hi, blk, keep], mine, vec


def ln1_call(me, parts, keep4, g, b):
    grid, ins, mine, vec = raw_specs()
    return pl.pallas_call(
        ln1_body,
        grid_spec=pltpu.PrefetchScalarGridSpec(
            num_scalar_prefetch=1,
            grid=grid,
            in_specs=ins + [vec, vec],
            out_specs=[mine] + [pl.BlockSpec((1, RB, D), lambda j, i, m: (block_of(m[0], j), i, 0))] * 2,
        ),
        out_shape=[sds((TS, D), bf), sds((NT, TS, D), bf), sds((NT, TS, D), bf)],
        compiler_params=params(),
        cost_estimate=cost(80 * TS * D, 20 * TS * D),
        name="ln1",
    )(me, *parts, keep4, g, b)


def cot_call(me, parts, keep4):
    grid, ins, mine, vec = raw_specs()
    return pl.pallas_call(
        cot_body,
        grid_spec=pltpu.PrefetchScalarGridSpec(
            num_scalar_prefetch=1,
            grid=grid,
            in_specs=[ins[0]] * 4 + ins[-1:],
            out_specs=[mine, pl.BlockSpec((1, RB, D), lambda j, i, m: (j, i, 0)), vec],
        ),
        out_shape=[sds((TS, D), bf), sds((NT, TS, D), bf), sds((1, D), f32)],
        compiler_params=params(),
        cost_estimate=cost(80 * TS * D, 20 * TS * D),
        name="cot",
    )(me, *parts, keep4)


def ln2_body(r0, c1, c3, x, keep, pb, g, b, h_ref, e_ref):
    s = r0[...] + c1[...].astype(f32) + c3[...].astype(f32)
    h = x[...].astype(f32) + keep[...] * (s + pb[...])
    h_ref[...] = h
    n, _ = stats(h)
    e_ref[...] = (n * g[...] + b[...]).astype(bf)


def ln2_call(r0, c1, c3, x, keep, pb, g, b):
    row = pl.BlockSpec((RB, D), lambda i: (i, 0))
    kp = pl.BlockSpec((RB, 1), lambda i: (i, 0))
    return pl.pallas_call(
        ln2_body,
        grid=(TS // RB,),
        in_specs=[row, row, row, row, kp] + [full((1, D))] * 3,
        out_specs=[row, row],
        out_shape=[sds((TS, D), f32), sds((TS, D), bf)],
        compiler_params=params(),
        cost_estimate=cost(20 * TS * D, 16 * TS * D),
        name="ln2",
    )(r0, c1, c3, x, keep, pb, g, b)


def norm_back(w, n, inv):
    m1 = jnp.sum(w, axis=1, keepdims=True) * (1.0 / D)
    m2 = jnp.sum(w * n, axis=1, keepdims=True) * (1.0 / D)
    return inv * (w - m1 - n * m2)


def ln2b_body(r0, c1, c3, h, c, keep, g, gh_ref, gp_ref, gg_ref, gb_ref, pb_ref):
    gn = r0[...] + c1[...].astype(f32) + c3[...].astype(f32)
    n, inv = stats(h[...])
    gh = c[...].astype(f32) + norm_back(gn * g[...], n, inv)
    gh_ref[...] = gh
    kg = keep[...] * gh
    gp_ref[...] = kg.astype(bf)
    acc_out(gg_ref, colsum(gn * n))
    acc_out(gb_ref, colsum(gn))
    acc_out(pb_ref, colsum(kg))


def ln2b_call(r0, c1, c3, h, c, keep, g):
    row = pl.BlockSpec((RB, D), lambda i: (i, 0))
    kp = pl.BlockSpec((RB, 1), lambda i: (i, 0))
    return pl.pallas_call(
        ln2b_body,
        grid=(TS // RB,),
        in_specs=[row, row, row, row, row, kp, full((1, D))],
        out_specs=[row, row] + [full((1, D))] * 3,
        out_shape=[sds((TS, D), f32), sds((TS, D), bf)] + [sds((1, D), f32)] * 3,
        compiler_params=params(),
        cost_estimate=cost(30 * TS * D, 20 * TS * D),
        name="ln2b",
    )(r0, c1, c3, h, c, keep, g)


def result_body(r0, c1, c3, h, keep, fb, o_ref):
    s = r0[...] + c1[...].astype(f32) + c3[...].astype(f32)
    o_ref[...] = (h[...] + keep[...] * (s + fb[...])).astype(bf)


def result_call(r0, c1, c3, h, keep, fb):
    row = pl.BlockSpec((RB, D), lambda i: (i, 0))
    kp = pl.BlockSpec((RB, 1), lambda i: (i, 0))
    return pl.pallas_call(
        result_body,
        grid=(TS // RB,),
        in_specs=[row, row, row, row, kp, full((1, D))],
        out_specs=row,
        out_shape=sds((TS, D), bf),
        compiler_params=params(60),
        cost_estimate=cost(8 * TS * D, 14 * TS * D),
        name="result",
    )(r0, c1, c3, h, keep, fb)


def ln1b_body(r0, c1, c3, x, gh, keep, g, res, o_ref):
    keep = keep[...]
    gn = keep * (r0[...] + c1[...].astype(f32) + c3[...].astype(f32))
    n, inv = stats(x[...].astype(f32))
    gt = (gh[...] + norm_back(gn * g[...], n, inv)).astype(bf)
    for b in range(NT):
        o_ref[b, 0] = gt[:, b * TS : (b + 1) * TS]
        o_ref[b, 1] = res[:, b * TS : (b + 1) * TS]


def ln1b_call(r0, c1, c3, x, gh, keep, g, res):
    rb = 80
    row = pl.BlockSpec((rb, D), lambda i: (i, 0))
    kp = pl.BlockSpec((rb, 1), lambda i: (i, 0))
    vec = full((1, D))
    return pl.pallas_call(
        ln1b_body,
        grid=(TS // rb,),
        in_specs=[row, row, row, row, row, kp, vec, row],
        out_specs=pl.BlockSpec((NT, 2, rb, TS), lambda i: (0, 0, i, 0)),
        out_shape=sds((NT, 2, TS, TS), bf),
        compiler_params=params(60),
        cost_estimate=cost(30 * TS * D, 24 * TS * D),
        name="ln1b",
    )(r0, c1, c3, x, gh, keep, g, res)


def place_body(x, gt_ref, res_ref, gt_s, res_s):
    for t in range(NT):
        gt_s[t * TS : (t + 1) * TS] = x[t, 0].astype(f32)
        res_s[t * TS : (t + 1) * TS] = x[t, 1].astype(f32)
    for n in range(NW * WIN):
        w, a = n // WIN, n % WIN
        rows = slice(w * WR + a * WIN, w * WR + a * WIN + WIN)
        gt_ref[n] = gt_s[rows]
        res_ref[n] = res_s[rows].astype(bf)


def place_call(x):
    n = NW * WIN
    return pl.pallas_call(
        place_body,
        grid=(1,),
        in_specs=[full((NT, 2, TS, TS))],
        out_specs=[full((n, WIN, TS))] * 2,
        scratch_shapes=[pltpu.VMEM((NT * TS, TS), f32)] * 2,
        out_shape=[sds((n, WIN, TS), f32), sds((n, WIN, TS), bf)],
        compiler_params=params(60),
        cost_estimate=cost(4 * TS * TS, 40 * TS * TS),
        name="place",
    )(x)


def turn(v):
    return v.reshape(2, 3, WIN, WIN, TS).transpose(0, 2, 1, 3, 4).reshape(2, WIN, 3 * WIN, TS)


def pad_body(w_ref, q_ref, p_ref):
    rows = w_ref.shape[0]
    w = w_ref[...]
    zero = jnp.zeros((rows, HP - HDIM), bf)
    for h in range(3 * HL):
        q_ref[:, h * HP : (h + 1) * HP] = jnp.concatenate([w[:, h * HDIM : (h + 1) * HDIM], zero], axis=1)
    for h in range(HL):
        s = 3 * HL + h
        p_ref[:, h * HP : (h + 1) * HP] = jnp.concatenate([w[:, s * HDIM : (s + 1) * HDIM], zero], axis=1)


def pad_call(g1):
    rb = 160
    return pl.pallas_call(
        pad_body,
        grid=(D // rb,),
        in_specs=[pl.BlockSpec((rb, D), lambda i: (i, 0))],
        out_specs=[
            pl.BlockSpec((rb, 3 * HL * HP), lambda i: (i, 0)),
            pl.BlockSpec((rb, HL * HP), lambda i: (i, 0)),
        ],
        out_shape=[sds((D, 3 * HL * HP), bf), sds((D, HL * HP), bf)],
        compiler_params=params(),
        cost_estimate=cost(D * 2048, 2 * D * (1280 + 2048)),
        name="padw",
    )(g1)


def block_of(me, j):
    return lax.rem(me + j, NT)


def qkv_body(x_ref, w_ref, b_ref, o_ref):
    o_ref[...] = (dot(x_ref[...], w_ref[...]) + b_ref[...]).astype(bf)


def qkv_call(x, w, bias):
    n = w.shape[1]
    tn = 512
    rows = x.shape[0]
    return pl.pallas_call(
        qkv_body,
        grid=(n // tn,),
        in_specs=[
            full((rows, D)),
            pl.BlockSpec((D, tn), lambda i: (0, i)),
            pl.BlockSpec((1, tn), lambda i: (0, i)),
        ],
        out_specs=pl.BlockSpec((rows, tn), lambda i: (0, i)),
        out_shape=sds((rows, n), bf),
        compiler_params=params(24),
        cost_estimate=cost(2 * rows * D * n, 2 * (rows * D + D * n + rows * n)),
        name="qkv",
    )(x, w, bias)


def gatt_body(*refs):
    count = len(refs) - 4
    w_ref, o_ref = refs[1 + count], refs[-1]
    for t in range(count):

        @pl.when(pl.program_id(0) == t)
        def _(t=t):
            o_ref[0] = dot(refs[1 + t][...], w_ref[...]).astype(bf)


def gatt_call(me, which, xs, w, into):
    n = w.shape[1]
    k = len(which)
    first, step = which[0], which[-1] - which[0]
    return pl.pallas_call(
        gatt_body,
        grid_spec=pltpu.PrefetchScalarGridSpec(
            num_scalar_prefetch=1,
            grid=(k,),
            in_specs=[pl.BlockSpec((TS, D), lambda t, m: (0, 0))] * k
            + [pl.BlockSpec((D, n), lambda t, m: (0, 0)), ANY],
            out_specs=pl.BlockSpec((1, TS, n), lambda t, m: (block_of(m[0], first + step * t), 0, 0)),
        ),
        out_shape=sds((NT, TS, n), bf),
        input_output_aliases={2 + k: 0},
        compiler_params=params(),
        cost_estimate=cost(2 * k * TS * D * n, 2 * (k * TS * D + D * n + k * TS * n)),
        name="gatt",
    )(me, *xs, w, into)


def gatt2_body(me_ref, a_ref, b_ref, w_ref, z_ref, o_ref, p_ref):
    p_ref[:HALF] = a_ref[...]
    p_ref[HALF:] = b_ref[...]
    o_ref[0] = dot(p_ref[...], w_ref[...]).astype(bf)


def gatt2_call(me, halves, w, into):
    n = w.shape[1]
    half = pl.BlockSpec((HALF, D), lambda i, m: (0, 0))
    return pl.pallas_call(
        gatt2_body,
        grid_spec=pltpu.PrefetchScalarGridSpec(
            num_scalar_prefetch=1,
            grid=(1,),
            in_specs=[half, half, pl.BlockSpec((D, n), lambda i, m: (0, 0)), ANY],
            out_specs=[
                pl.BlockSpec((1, TS, n), lambda i, m: (block_of(m[0], 2), 0, 0)),
                pl.BlockSpec((TS, D), lambda i, m: (0, 0)),
            ],
        ),
        out_shape=[sds((NT, TS, n), bf), sds((TS, D), bf)],
        input_output_aliases={4: 0},
        compiler_params=params(),
        cost_estimate=cost(2 * TS * D * n, 2 * (2 * TS * D + D * n + TS * n)),
        name="gatt",
    )(me, *halves, w, into)


def attn_body(qkv_ref, tab_ref, sel_ref, mask_ref, sp_ref, km_ref, z_ref, o_ref, p_ref, t_ref):
    @pl.when(pl.program_id(0) == 0)
    def _():
        t_ref[...] = dot(sel_ref[...], tab_ref[...]).astype(bf)

    qs = [qkv_ref[:, h * HP : (h + 1) * HP] for h in range(HL)]
    along = dot_nt(jnp.concatenate(qs, axis=0), t_ref[...])
    mask = mask_ref[...].astype(f32)
    along = jnp.concatenate([(along[h * WR : (h + 1) * WR] * mask).astype(bf) for h in range(HL)], axis=0)
    bias = dot(along, sp_ref[...])
    for h in range(HL):
        k = qkv_ref[:, (HL + h) * HP : (HL + h + 1) * HP]
        v = qkv_ref[:, (2 * HL + h) * HP : (2 * HL + h + 1) * HP]
        s = dot_nt(qs[h], k) * SCALE + bias[h * WR : (h + 1) * WR] + km_ref[...]
        top = jnp.max(s, axis=1, keepdims=True)
        e = jnp.exp(s - top)
        p = (e * (1.0 / jnp.sum(e, axis=1, keepdims=True))).astype(bf)
        p_ref[0, h] = p
        o_ref[:, h * HP : (h + 1) * HP] = dot(p, v).astype(bf)


def attn_call(qkv, tab, sel, mask, spread, keys, into):
    n = 3 * HL * HP
    return pl.pallas_call(
        attn_body,
        grid=(NW,),
        in_specs=[
            pl.BlockSpec((WR, n), lambda i: (i, 0)),
            full((64, HP)),
            full((512, 64)),
            full((WR, 512)),
            full((512, WR)),
            full((1, WR)),
            ANY,
        ],
        out_specs=[
            pl.BlockSpec((WR, HL * HP), lambda i: (i, 0)),
            pl.BlockSpec((1, HL, WR, WR), lambda i: (i, 0, 0, 0)),
        ],
        out_shape=[sds((NT * TS, HL * HP), bf), sds((NW, HL, WR, WR), bf)],
        scratch_shapes=[pltpu.VMEM((512, HP), bf)],
        input_output_aliases={6: 0},
        compiler_params=params(),
        cost_estimate=cost(24 * 6 * 2 * WR * WR * 256, 8e6, 24 * WR * 256),
        name="attn",
    )(qkv, tab, sel, mask, spread, keys, into)


def attnb_body(qkv_ref, p_ref, ga_ref, tab_ref, sel_ref, mask_ref, sp_ref, z_ref, o_ref, rel_ref, bias_ref, t_ref):
    @pl.when(pl.program_id(0) == 0)
    def _():
        t_ref[...] = dot(sel_ref[...], tab_ref[...]).astype(bf)
        rel_ref[...] = jnp.zeros_like(rel_ref)
        bias_ref[...] = jnp.zeros_like(bias_ref)

    table = t_ref[...]
    mask = mask_ref[...].astype(f32)
    qs, all_ds = [], []
    for h in range(HL):
        cq = slice(h * HP, (h + 1) * HP)
        cv = slice((2 * HL + h) * HP, (2 * HL + h + 1) * HP)
        ga = ga_ref[:, cq]
        p = p_ref[0, h]
        pf = p.astype(f32)
        gs = dot_nt(ga, qkv_ref[:, cv])
        delta = jnp.sum(pf * gs, axis=1, keepdims=True)
        all_ds.append((pf * (gs - delta)).astype(bf))
        qs.append(qkv_ref[:, cq])
        gv = dot_tn(p, ga).astype(bf)
        o_ref[:, cv] = gv
        bias_ref[:, cv] += colsum(gv.astype(f32))
    sums = dot_nt(jnp.concatenate(all_ds, axis=0), sp_ref[...])
    sums = jnp.concatenate([(sums[h * WR : (h + 1) * WR] * mask).astype(bf) for h in range(HL)], axis=0)
    gq_rel = dot(sums, table)
    rel_ref[...] += dot_tn(sums, jnp.concatenate(qs, axis=0))
    for h in range(HL):
        cq = slice(h * HP, (h + 1) * HP)
        ck = slice((HL + h) * HP, (HL + h + 1) * HP)
        ds = all_ds[h]
        o_ref[:, ck] = (dot_tn(ds, qs[h]) * SCALE).astype(bf)
        gq = (dot(ds, qkv_ref[:, ck]) * SCALE + gq_rel[h * WR : (h + 1) * WR]).astype(bf)
        o_ref[:, cq] = gq
        bias_ref[:, cq] += colsum(gq.astype(f32))


def attnb_call(qkv, p, ga, tab, sel, mask, spread, into):
    n = 3 * HL * HP
    return pl.pallas_call(
        attnb_body,
        grid=(NW,),
        in_specs=[
            pl.BlockSpec((WR, n), lambda i: (i, 0)),
            pl.BlockSpec((1, HL, WR, WR), lambda i: (i, 0, 0, 0)),
            pl.BlockSpec((WR, HL * HP), lambda i: (i, 0)),
            full((64, HP)),
            full((512, 64)),
            full((WR, 512)),
            full((512, WR)),
            ANY,
        ],
        out_specs=[pl.BlockSpec((WR, n), lambda i: (i, 0)), full((512, HP)), full((1, n))],
        out_shape=[sds((NT * TS, n), bf), sds((512, HP), f32), sds((1, n), f32)],
        scratch_shapes=[pltpu.VMEM((512, HP), bf)],
        input_output_aliases={7: 0},
        compiler_params=params(),
        cost_estimate=cost(24 * 10 * 2 * WR * WR * 256, 14e6),
        name="attnb",
    )(qkv, p, ga, tab, sel, mask, spread, into)


def partial_body(me_ref, a_ref, w_ref, *refs):
    w = w_ref[...]
    if len(refs) == 5:
        n_ref, (r0, r1, r2a, r2b, r3) = None, refs
    else:
        n_ref, keep_ref, r0, r1, r2a, r2b, r3, gg_ref, gb_ref = refs
    gain = bias = 0.0
    for j, ref in ((2, None), (1, r1), (3, r3), (0, r0)):
        t = block_of(me_ref[0], j)
        r = dot_nt(a_ref[t], w)
        if n_ref is not None:
            gain = gain + colsum(r * n_ref[t].astype(f32))
            bias = bias + colsum(r * keep_ref[t])
        if ref is None:
            r2a[...] = r[:HALF].astype(bf)
            r2b[...] = r[HALF:].astype(bf)
        else:
            ref[...] = r.astype(ref.dtype)
    if n_ref is not None:
        gg_ref[...] = gain
        gb_ref[...] = bias


def partial_call(me, a, w, name, norm=()):
    k = a.shape[2]
    tn = 256
    whole = pl.BlockSpec((TS, tn), lambda i, m: (0, i))
    half = pl.BlockSpec((HALF, tn), lambda i, m: (0, i))
    ins = [pl.BlockSpec((NT, TS, tn), lambda i, m: (0, 0, i)), pl.BlockSpec((NT, TS, 1), lambda i, m: (0, 0, 0))]
    outs = [whole, whole, half, half, whole]
    shapes = [sds((TS, D), f32), sds((TS, D), bf), sds((HALF, D), bf), sds((HALF, D), bf), sds((TS, D), bf)]
    if norm:
        outs += [pl.BlockSpec((1, tn), lambda i, m: (0, i))] * 2
        shapes += [sds((1, D), f32)] * 2
    return pl.pallas_call(
        partial_body,
        grid_spec=pltpu.PrefetchScalarGridSpec(
            num_scalar_prefetch=1,
            grid=(D // tn,),
            in_specs=[
                pl.BlockSpec((NT, TS, k), lambda i, m: (0, 0, 0)),
                pl.BlockSpec((tn, k), lambda i, m: (i, 0)),
            ]
            + ins[: len(norm)],
            out_specs=outs,
        ),
        out_shape=shapes,
        compiler_params=params(24),
        cost_estimate=cost(2 * NT * TS * D * k, 2 * (NT * TS * k + D * k + 9 * TS * D)),
        name=name,
    )(me, a, w, *norm)


def merge_body(r1, a, r3, b, s1, s3):
    s1[...] = (r1[...].astype(f32) + a[...].astype(f32)).astype(bf)
    s3[...] = (r3[...].astype(f32) + b[...].astype(f32)).astype(bf)


def merge_call(r1, a, r3, b, mb=16):
    one = pl.BlockSpec((HALF, D), lambda i: (0, 0))
    two = pl.BlockSpec((HALF, D), lambda i: (1, 0))
    return pl.pallas_call(
        merge_body,
        grid=(1,),
        in_specs=[one, one, two, one],
        out_specs=[one, two],
        out_shape=[sds((TS, D), bf)] * 2,
        input_output_aliases={0: 0, 2: 1},
        compiler_params=params(mb),
        cost_estimate=cost(4 * HALF * D, 12 * HALF * D),
        name="merge",
    )(r1, a, r3, b)


def mlp_body(halved, k, *refs):
    ins = refs[: 2 if halved else k]
    gb_refs = refs[len(ins) : len(ins) + k]
    w1_ref, w2_ref, b1_ref = refs[len(ins) + k : len(ins) + k + 3]
    outs = refs[len(ins) + k + 3 : -4]
    z_s, gb_s, br_s, gn_s = refs[-4:]
    step = pl.program_id(0)

    @pl.when(step == 0)
    def _():
        br_s[...] = jnp.zeros_like(br_s)
        gn_s[...] = jnp.zeros_like(gn_s)
        rows = k * TS // len(ins)
        for t, ref in enumerate(ins):
            z_s[t * rows : (t + 1) * rows] = ref[...]
        for t, ref in enumerate(gb_refs):
            gb_s[t * TS : (t + 1) * TS] = ref[0]

    w1 = w1_ref[...]
    w2 = w2_ref[...]
    pre = dot(z_s[...], w1) + b1_ref[...]
    ga = dot(gb_s[...], w2)
    cdf = 0.5 + 0.5 * lax.erf(pre * 0.7071067811865476)
    act = (pre * cdf).astype(bf)
    slope = cdf + pre * (0.3989422804014327 * jnp.exp(-0.5 * pre * pre))
    gp = (ga * slope).astype(bf)
    for t in range(k):
        rows = slice(t * TS, (t + 1) * TS)
        outs[3 * t][...] = act[rows]
        outs[3 * t + 1][...] = gp[rows]
        outs[3 * t + 2][...] = colsum(gp[rows].astype(f32))
    br_s[...] += dot_nt(act, w2)
    gn_s[...] += dot_nt(gp, w1)

    @pl.when(step == pl.num_programs(0) - 1)
    def _():
        rest = outs[3 * k :]
        for total, refs_out in ((br_s, rest[0::2]), (gn_s, rest[1::2])):
            at = 0
            for ref in refs_out:
                if at < total.shape[0]:
                    ref[...] = total[at : at + ref.shape[0]].astype(ref.dtype)
                    at += ref.shape[0]
        if halved:
            rest[4][...] = z_s[...]


def mlp_call(which, zs, gb, w, b1, kind):
    halved = which == (2,)
    k = len(which)
    tf = 640
    nf = D // tf
    col = pl.BlockSpec((TS, tf), lambda i: (0, i))
    bias = pl.BlockSpec((1, tf), lambda i: (0, i))
    half = full((HALF, D))
    block = full((TS, D))
    outs = [col, col, bias] * k
    shapes = [sds((TS, D), bf), sds((TS, D), bf), sds((1, D), f32)] * k
    if halved:
        outs += [half] * 4 + [block]
        shapes += [sds((HALF, D), bf)] * 4 + [sds((TS, D), bf)]
    else:
        outs += [block] * (2 * k)
        shapes += [sds((TS, D), kind)] * (2 * k)
    return pl.pallas_call(
        partial(mlp_body, halved, k),
        grid=(nf,),
        in_specs=[half if halved else block] * len(zs)
        + [pl.BlockSpec((1, TS, D), lambda i, j=j: (j, 0, 0)) for j in which]
        + [
            pl.BlockSpec((D, tf), lambda i: (0, i)),
            pl.BlockSpec((D, tf), lambda i: (0, i + nf)),
            bias,
        ],
        out_specs=outs,
        out_shape=shapes,
        scratch_shapes=[pltpu.VMEM((k * TS, D), bf)] * 2 + [pltpu.VMEM((k * TS, D), f32)] * 2,
        compiler_params=params(32),
        cost_estimate=cost(k * 8 * TS * D * D, 4 * D * D + k * 12 * TS * D, k * 2 * TS * D),
        name="mlp",
    )(*zs, *[gb] * k, w, w, b1)


NG = 2 * D


def tokgrad_body(*refs):
    o_ref = refs[-1]
    lhs, rhs = refs[:4], refs[4:8]
    total = None
    for j in range(NT):
        left = lhs[j][0] if len(lhs[j].shape) == 3 else lhs[j][...]
        part = dot_tn(left, rhs[j][...])
        total = part if total is None else total + part
    o_ref[...] = total.astype(bf)


def tokgrad_call(lhs, rhs, into, at):
    td = 256
    if len(lhs) == 1:
        left = [pl.BlockSpec((1, TS, td), lambda i, j=j: (j, 0, i)) for j in range(NT)]
        lhs = list(lhs) * NT
    else:
        left = [pl.BlockSpec((TS, td), lambda i: (0, i))] * NT
    return pl.pallas_call(
        tokgrad_body,
        grid=(D // td,),
        in_specs=left + [full((TS, D))] * NT + [ANY] * (into is not None),
        out_specs=pl.BlockSpec((td, D), lambda i: (i, at)),
        out_shape=sds((D, NG), bf),
        input_output_aliases={} if into is None else {2 * NT: 0},
        compiler_params=params(24),
        cost_estimate=cost(8 * TS * D * D, 2 * (8 * TS * D + D * D)),
        name="fcgrad",
    )(*lhs, *rhs, *(() if into is None else (into,)))


def narrow(x, heads):
    return jnp.concatenate([x[:, h * HP : h * HP + HDIM] for h in range(heads)], axis=1)


def qpgrad_body(me_ref, e_ref, dq_ref, p0, p1, p2, p3, a_ref, o_ref):
    o_ref[:, : 3 * HL * HDIM] = narrow(dot_tn(e_ref[...], dq_ref[...]), 3 * HL).astype(bf)
    total = None
    for j, p in enumerate((p0, p1, p2, p3)):
        part = dot_tn(p[...], a_ref[block_of(me_ref[0], j)])
        total = part if total is None else total + part
    o_ref[:, 3 * HL * HDIM :] = narrow(total, HL).astype(bf)


def qpgrad_call(me, e, dqkv, p, att4):
    td = 256
    rows, n = dqkv.shape
    k = att4.shape[2]
    return pl.pallas_call(
        qpgrad_body,
        grid_spec=pltpu.PrefetchScalarGridSpec(
            num_scalar_prefetch=1,
            grid=(D // td,),
            in_specs=[
                pl.BlockSpec((rows, td), lambda i, m: (0, i)),
                pl.BlockSpec((rows, n), lambda i, m: (0, 0)),
            ]
            + [pl.BlockSpec((TS, td), lambda i, m: (0, i))] * 4
            + [pl.BlockSpec((NT, TS, k), lambda i, m: (0, 0, 0))],
            out_specs=pl.BlockSpec((td, D), lambda i, m: (i, 0)),
        ),
        out_shape=sds((D, D), bf),
        compiler_params=params(24),
        cost_estimate=cost(2 * rows * D * (n + k), 2 * (2 * rows * D + rows * (n + k) + D * D)),
        name="qpgrad",
    )(me, e, dqkv, *p, att4)


UP = [(i, (i + 1) % NT) for i in range(NT)]
DOWN = [(i, (i - 1) % NT) for i in range(NT)]


def up(v):
    return lax.ppermute(v, "tp", UP)


def down(v):
    return lax.ppermute(v, "tp", DOWN)


def after(v, *deps):
    return lax.optimization_barrier((v, deps))[0]


def ring_gather(own, first=None, between=None):
    b3 = up(own)
    b1 = down(own)
    if first is not None:
        b3, b1, first = lax.optimization_barrier((b3, b1, first))
    half = own.shape[0] // 2
    u, d = up(b3[:half]), down(b1[half:])
    if between is not None:
        first = between(b1, b3, first)
        u, d, first = lax.optimization_barrier((u, d, first))
    return (own, b1, u, d, b3), first


def ring_scatter(r1, r2a, r2b, r3, first=None, mb=16):
    a = up(r2a)
    b = down(r2b)
    if first is not None:
        a, b, first = lax.optimization_barrier((a, b, first))
    s1, s3 = merge_call(r1, a, r3, b, mb)
    return (s3, s1), first


def ring_finish(sums):
    return down(sums[0]), up(sums[1])


def shard_place():
    s = lax.axis_index("shard")
    return s // 4, (s // 2) % 2, s % 2


def shard_move(v, f):
    return lax.ppermute(v, "shard", [(i, f(i)) for i in range(16)])


def pick(v, i, ax):
    return lax.dynamic_index_in_dim(v, i, ax, keepdims=False)


def add_low(p, q):
    return (p.astype(f32) + q.astype(f32)).astype(bf)


def over_shard_1(v):
    n = v.shape[1]
    y, zl, core = shard_place()
    v = v.reshape(4, 2, 2, 80, n)
    v = add_low(pick(v, core, 2), shard_move(pick(v, 1 - core, 2), lambda i: i ^ 1))
    w = [pick(v, (y + j) % 4, 0) for j in range(4)]
    a = shard_move(w[2][0], lambda i: (i + 4) % 16)
    b = shard_move(w[2][1], lambda i: (i + 12) % 16)
    return w[0], jnp.stack([add_low(w[1][0], a), w[1][1]]), jnp.stack([w[3][0], add_low(w[3][1], b)])


def over_shard_2(parts):
    w0, s1, s3 = parts
    return w0, shard_move(s3, lambda i: (i + 12) % 16), shard_move(s1, lambda i: (i + 4) % 16)


def over_shard_3(parts):
    w0, c1, c3 = parts
    y, zl, core = shard_place()
    v = (w0.astype(f32) + c1.astype(f32) + c3.astype(f32)).astype(bf)
    return pick(v, zl, 0), shard_move(pick(v, 1 - zl, 0), lambda i: i ^ 2)


def over_ctx(v):
    return v.astype(f32) + lax.ppermute(v, "ctx", [(0, 1), (1, 0)]).astype(f32)


def small_pack(parts):
    out = []
    for part in parts:
        v = jnp.concatenate([a.ravel() for a in part])
        out.append(jnp.pad(v, (0, -v.size % 1024)).reshape(-1, 128))
    return jnp.concatenate(out, axis=0).astype(bf)


def small_sum(everyone):
    return jnp.sum(everyone.astype(f32), axis=0)


def small_split(both, world):
    rows = -(-sum(a.size for a in world) // 1024) * 8
    return both[:rows], both[rows:]


def pair_sum(w, step):
    return w + lax.ppermute(w, "tp", [(i, i ^ step) for i in range(NT)])


def small_finish(w, g, world, group):
    out = []
    for part, flat in ((world, w.ravel()), (group, g.ravel())):
        at = 0
        for a in part:
            out.append(flat[at : at + a.size].reshape(a.shape))
            at += a.size
    return out


def from_everyone(array, axis):
    size = lax.axis_size(axis)
    return lax.all_to_all(jnp.broadcast_to(array[None], (size, *array.shape)), axis, 0, 0, tiled=True)


def windows(grid):
    n = grid.shape[-1]
    w = grid.reshape(2, WIN, 3, WIN, n).transpose(0, 2, 1, 3, 4).reshape(NW, CELLS, n)
    w = jnp.pad(w, ((0, 0), (0, WR - CELLS), (0, 0))).reshape(NW * WR, n)
    return jnp.pad(w, ((0, NT * TS - NW * WR), (0, 0))).reshape(NT, TS, n)


def local(
    tokens,
    valid_mask,
    ln1_gain,
    ln1_bias,
    qkv_weight,
    qkv_bias,
    rel_rows,
    rel_cols,
    proj_weight,
    proj_bias,
    ln2_gain,
    ln2_bias,
    fc1_weight,
    fc1_bias,
    fc2_weight,
    fc2_bias,
    cotangent,
):
    tp_index = lax.axis_index("tp")
    me = tp_index.astype(jnp.int32).reshape(1)
    sel, mask, spread, keys = rel_constants()
    sel = jnp.asarray(sel, bf)
    mask = jnp.asarray(mask, bf)
    spread = jnp.asarray(spread, bf)
    keys = jnp.asarray(keys, f32)
    row = lambda v: v.reshape(1, -1)

    own1 = jnp.concatenate([jnp.moveaxis(qkv_weight, 1, 0).reshape(80, 960), proj_weight.T], axis=1)
    own2 = jnp.concatenate([fc1_weight, fc2_weight.T], axis=1)
    all1 = lax.all_gather(own1, "shard", axis=0, tiled=True)
    all2 = lax.all_gather(own2, "shard", axis=0, tiled=True)
    bias_q = jnp.pad(qkv_bias.reshape(2, HL, HDIM), ((0, 0), (0, 0), (0, HP - HDIM))).reshape(2, HL * HP)
    bias_p = row(jnp.concatenate([bias_q[0], jnp.zeros((HL * HP,), f32), bias_q[1]]))
    tab = jnp.zeros((64, HP), bf).at[:RELS, :HDIM].set(rel_rows).at[32 : 32 + RELS, :HDIM].set(rel_cols)

    keep4 = windows(valid_mask.astype(f32)[..., None])
    keep = lax.dynamic_index_in_dim(keep4, tp_index, 0, keepdims=False)
    toks, (qkvp, projp) = ring_gather(windows(tokens), None, lambda b1, b3, _: pad_call(all1))
    x, e4, n4 = ln1_call(me, toks, keep4, row(ln1_gain), row(ln1_bias))
    ents = e4.reshape(NT * TS, D)
    cot = after(windows(cotangent), toks[2], toks[3])
    cot3, cot1 = up(cot), down(cot)
    cot3, cot1, flat = lax.optimization_barrier((cot3, cot1, qkv_call(ents, qkvp, bias_p)))
    cots = (cot, cot1, up(cot3), cot3)
    att, probs = attn_call(flat, tab, sel, mask, spread, keys, jnp.zeros((NT * TS, HL * HP), bf))
    att4 = att.reshape(NT, TS, HL * HP)
    r0, *rest = partial_call(me, att4, projp, "proj")
    rest, cots = lax.optimization_barrier((rest, cots))
    sums, _ = ring_scatter(*rest, None, 60)
    c, gb, sum_fc2_bias = cot_call(me, cots, keep4)
    (c1, c3), gb = lax.optimization_barrier((ring_finish(sums), gb))
    h, z = ln2_call(r0, c1, c3, x, keep, row(proj_bias), row(ln2_gain), row(ln2_bias))

    b1row = row(fc1_bias)
    mlp = lambda which, zz, kind: mlp_call(which, zz, gb, all2, b1row, kind)
    zs, (m0, m13) = ring_gather(
        z, mlp((0,), (z,), f32), lambda b1, b3, first: (first, mlp((1, 3), (b1, b3), bf))
    )
    act0, gpre0, fb0, br0, gn0 = m0
    act1, gpre1, fb1, act3, gpre3, fb3, br1, gn1, br3, gn3 = m13
    act2, gpre2, fb2, br2a, gn2a, br2b, gn2b, z2 = mlp((2,), (zs[2], zs[3]), bf)
    gpres = (gpre0, gpre1, gpre2, gpre3)
    sum_fc1_bias = fb0 + fb1 + fb2 + fb3
    sums, grads = ring_scatter(gn1, gn2a, gn2b, gn3, tokgrad_call((gb,), (act0, act1, act2, act3), None, 1))
    grads = tokgrad_call((z, zs[1], z2, zs[4]), gpres, grads, 0)
    (c1, c3), grads = lax.optimization_barrier((ring_finish(sums), grads))
    own_fc = lax.psum_scatter(grads, "shard", scatter_dimension=0, tiled=True)
    gh, gproj, sum_ln2_gain, sum_ln2_bias, sum_proj_bias = ln2b_call(
        gn0, c1, c3, h, c, keep, row(ln2_gain)
    )
    ga = gatt_call(me, (0,), (gproj,), projp, jnp.zeros((NT, TS, HL * HP), bf))
    gps, ga = ring_gather(gproj, ga, lambda b1, b3, ga: gatt_call(me, (1, 3), (b1, b3), projp, ga))
    ga, gp2 = gatt2_call(me, gps[2:4], projp, ga)

    branch = after((br1, br2a, br2b, br3), gp2)
    dqkv, rel, sum_qkv_bias = attnb_call(
        flat,
        probs,
        ga.reshape(NT * TS, HL * HP),
        tab,
        sel,
        mask,
        spread,
        jnp.zeros((NT * TS, 3 * HL * HP), bf),
    )
    sums, dqkv = ring_scatter(*branch, dqkv)
    sums, dqkv = lax.optimization_barrier((sums, dqkv))
    f1, f3 = ring_finish(sums)
    r0, r1, r2a, r2b, r3, sum_ln1_gain, sum_ln1_bias = partial_call(
        me, dqkv.reshape(NT, TS, 3 * HL * HP), qkvp, "gnorm1", (n4, keep4)
    )
    gradq = qpgrad_call(me, ents, dqkv, (gproj, gps[1], gp2, gps[4]), att4)
    gradq, f1, f3 = lax.optimization_barrier((gradq, f1, f3))
    sums, gradq = ring_scatter(r1, r2a, r2b, r3, gradq, 60)
    c1, c3 = ring_finish(sums)
    parts = over_shard_1(after(gradq, sums))
    res = result_call(br0, f1, f3, h, keep, row(fc2_bias))
    small = after(
        (
            rel,
            sum_qkv_bias,
            sum_fc1_bias,
            sum_ln1_gain,
            sum_ln1_bias,
            sum_ln2_gain,
            sum_ln2_bias,
            sum_proj_bias,
            sum_fc2_bias,
        ),
        sums,
    )
    rels = jnp.dot(sel.astype(f32).T, small[0], precision=lax.Precision.HIGHEST)
    qb = small[1].reshape(3, HL, HP)[:, :, :HDIM]
    world = [*small[3:], rels[:RELS, :HDIM], rels[32 : 32 + RELS, :HDIM]]
    group = [qb[0], qb[2], small[2]]
    everyone = from_everyone(small_pack((world, group)), ("shard", "ctx"))
    c1, c3, res, everyone, parts = lax.optimization_barrier((c1, c3, res, everyone, parts))
    parts = over_shard_2(parts)
    out = ln1b_call(r0, c1, c3, x, gh, keep, row(ln1_gain), res)
    out, parts, fc = lax.optimization_barrier((out, parts, over_ctx(own_fc)))
    w, g = small_split(small_sum(after(everyone, out)), world)
    blocks = lax.all_to_all(out, "tp", 0, 0, tiled=True)
    half, other = over_shard_3(parts)
    q = over_ctx(add_low(half, other))
    blocks, q, w = lax.optimization_barrier((blocks, q, pair_sum(w, 1)))
    w = pair_sum(w, 3)
    g_ln1g, g_ln1b, g_ln2g, g_ln2b, g_pb, g_f2b, g_rr, g_rc, g_q, g_v, g_f1b = small_finish(w, g, world, group)
    token_grads, result = place_call(blocks)
    token_grads, result = turn(token_grads), turn(result)
    return (
        result,
        token_grads,
        g_ln1g.ravel(),
        g_ln1b.ravel(),
        jnp.moveaxis(q[:, : 3 * HL * HDIM].reshape(80, 3, 320), 0, 1),
        jnp.stack([g_q.ravel(), g_v.ravel()]),
        g_rr,
        g_rc,
        q[:, 3 * HL * HDIM :].T,
        g_pb.ravel(),
        g_ln2g.ravel(),
        g_ln2b.ravel(),
        fc[:, :D],
        g_f1b.ravel(),
        fc[:, D:].T,
        g_f2b.ravel(),
    )


def solution(mesh):
    cells = P("shard", "ctx", None, "tp")
    in_specs = (
        cells,
        P("shard", "ctx", None),
        P(),
        P(),
        P(None, "shard", "tp"),
        P(None, "tp"),
        P(),
        P(),
        P("tp", "shard"),
        P(),
        P(),
        P(),
        P("shard", "tp"),
        P("tp"),
        P("tp", "shard"),
        P(),
        cells,
    )
    out_specs = (
        cells,
        cells,
        P(),
        P(),
        P(None, "shard", "tp"),
        P(None, "tp"),
        P(),
        P(),
        P("tp", "shard"),
        P(),
        P(),
        P(),
        P("shard", "tp"),
        P("tp"),
        P("tp", "shard"),
        P(),
    )
    return jax.shard_map(local, mesh=mesh, in_specs=in_specs, out_specs=out_specs, check_vma=False)
```
